32 devices in a mesh: dp: 4 (over y, core), seq: 8 (over z, x).
Axes of the slice: x: 2, y: 2, z: 4, core: 2. Of those that a mesh axis runs over, the one named last changes fastest.
Arguments:
- tokens: bfloat16 [32, 1024, 768], P('dp', 'seq'), may hold values from -6 to 6
- offsets: int32 [32], P('dp'), may hold values from 0 to 511, as said below
- norm_gain: float32 [768], replicated, may hold values from 0.5 to 1.5
- norm_bias: float32 [768], replicated, may hold values from -1.5 to 1.5
- proj_weight: bfloat16 [768, 2304], replicated, may hold values from -0.21875 to 0.21875
- proj_bias: float32 [2304], replicated, may hold values from -1.5 to 1.5
- short_filter: float32 [2304, 3], replicated, may hold values from -3 to 3
- short_bias: float32 [2304], replicated, may hold values from -1.5 to 1.5
- long_kernel: float32 [768, 1024], P(None, 'seq'), may hold values from -0.1875 to 0.1875
- skip_bias: float32 [768], replicated, may hold values from -4 to 4
- out_weight: bfloat16 [768, 768], replicated, may hold values from -0.21875 to 0.21875
- out_bias: float32 [768], replicated, may hold values from -1.5 to 1.5
- second_gain: float32 [768], replicated, may hold values from 0.5 to 1.5
- second_bias: float32 [768], replicated, may hold values from -1.5 to 1.5
- up_weight: bfloat16 [768, 3072], replicated, may hold values from -0.21875 to 0.21875
- up_bias: float32 [3072], replicated, may hold values from -1.5 to 1.5
- down_weight: bfloat16 [3072, 768], replicated, may hold values from -0.21875 to 0.21875
- down_bias: float32 [768], replicated, may hold values from -1.5 to 1.5
- cotangent: bfloat16 [32, 1024, 768], P('dp', 'seq'), may hold values from -6 to 6
Outputs:
- output: float32 [32, 1024, 768], P('dp', 'seq')
- input_grad: float32 [32, 1024, 768], P('dp', 'seq')
- norm_gain_grad: float32 [768], P('seq')
- norm_bias_grad: float32 [768], P('seq')
- proj_grad: float32 [768, 2304], P('seq')
- proj_bias_grad: float32 [2304], P('seq')
- filter_grad: float32 [2304, 3], P('seq')
- short_bias_grad: float32 [2304], P('seq')
- kernel_grad: float32 [768, 1024], P('seq')
- skip_bias_grad: float32 [768], P('seq')
- out_grad: float32 [768, 768], P('seq')
- out_bias_grad: float32 [768], P('seq')
- second_gain_grad: float32 [768], P('seq')
- second_bias_grad: float32 [768], P('seq')
- up_grad: float32 [768, 3072], P('seq')
- up_bias_grad: float32 [3072], P('seq')
- down_grad: float32 [3072, 768], P('seq')
- down_bias_grad: float32 [768], P('seq')
The draws below stay inside these ranges and needn't reach their ends.
Inputs may be any that keep to these rules, and one draw needn't show every extreme that they name: `offsets`: in each group of 8 consecutive sequences one starts within its first 128 tokens; the others start below 512.
All inputs are finite; a program needn't handle non-finite values.
Results may differ from the reference program's by a relative error of at most 0.0072.
Values sent between devices are 32-bit elements; how exact they have to be, the bound alone decides.
No kernel may reach another device: no remote copies, remote signals or barrier semaphores. Data moves between devices by JAX's collectives and lax.ppermute only.
A program may use at most 256 MiB of HBM per device.

```python
import jax
import jax.numpy as jnp
from jax import lax

D = 768
FF = 3072
PROJ = 2304
KSHORT = 3
TOK_SEQ = 128
SEQS = 8
L = 1024
BATCH = 32


def draw_offsets(key, part):
    key = jax.random.fold_in(key, 7)
    first_key, second_key, third_key = jax.random.split(key, 3)
    groups = BATCH // SEQS
    broad = jax.random.randint(first_key, (BATCH,), 0, L // 2, dtype=jnp.int32)
    picked = jax.random.randint(second_key, (groups,), 0, SEQS, dtype=jnp.int32)
    early = jax.random.randint(third_key, (BATCH,), 0, TOK_SEQ, dtype=jnp.int32)
    position = jnp.arange(BATCH, dtype=jnp.int32) % SEQS
    chosen = position == jnp.repeat(picked, SEQS)
    result = jnp.where(chosen, early, broad).astype(jnp.int32)
    step_over = min(SEQS - 1, 1)
    highest = max(TOK_SEQ, L // 2 * step_over) - 1
    target = (picked[0] + step_over) % SEQS
    result = jnp.where(jnp.arange(BATCH, dtype=jnp.int32) == target, jnp.int32(highest), result)
    return result.astype(jnp.int32)


def block_levels(rng, shape, cuts, least, top_value):
    factor_of, own = 1.0, jax.random.fold_in(rng, 6)
    for dim, shards_of in cuts:
        draws = jnp.exp(jax.random.uniform(jax.random.fold_in(own, dim), (shards_of,), jnp.float32, least / len(cuts), top_value / len(cuts)))
        factor_of = factor_of * jnp.repeat(draws, shape[dim] // shards_of).reshape([-1 if axis == dim else 1 for axis in range(len(shape))])
    return factor_of


def bell_draw(rng, dims, scale, most, cuts=(), kind=jnp.bfloat16):
    values = scale * jax.random.normal(rng, dims, jnp.float32)
    if cuts:
        values = values * block_levels(rng, dims, cuts, -0.22, 0.18)
    return jnp.clip(values, -most, most).astype(kind)


def setup_inputs(seed: int = 0) -> dict:
    arg_keys = jax.random.split(jax.random.key(seed), 20)
    tokens = bell_draw(arg_keys[0], (BATCH, L, D), 1.0, 6.0, ((0, 4), (1, 8)))
    offsets = draw_offsets(jax.random.fold_in(arg_keys[19], 71), 0)
    norm_gain = jnp.clip(1.0 + 0.1 * jax.random.normal(arg_keys[2], (D,), jnp.float32), 0.5, 1.5)
    norm_bias = bell_draw(arg_keys[3], (D,), 0.3, 1.5, (), jnp.float32)
    proj_weight = bell_draw(arg_keys[4], (D, PROJ), D ** -0.5, 0.21875)
    proj_bias = bell_draw(arg_keys[5], (PROJ,), 0.3, 1.5, (), jnp.float32)
    short_filter = bell_draw(arg_keys[6], (PROJ, KSHORT), 0.6, 3.0, (), jnp.float32)
    short_bias = bell_draw(arg_keys[7], (PROJ,), 0.3, 1.5, (), jnp.float32)
    long_kernel = bell_draw(arg_keys[8], (D, L), L ** -0.5, 0.1875, ((1, 8),), jnp.float32)
    skip_bias = bell_draw(arg_keys[9], (D,), 1.0, 4.0, (), jnp.float32)
    out_weight = bell_draw(arg_keys[10], (D, D), D ** -0.5, 0.21875)
    out_bias = bell_draw(arg_keys[11], (D,), 0.3, 1.5, (), jnp.float32)
    second_gain = jnp.clip(1.0 + 0.1 * jax.random.normal(arg_keys[12], (D,), jnp.float32), 0.5, 1.5)
    second_bias = bell_draw(arg_keys[13], (D,), 0.3, 1.5, (), jnp.float32)
    up_weight = bell_draw(arg_keys[14], (D, FF), D ** -0.5, 0.21875)
    up_bias = bell_draw(arg_keys[15], (FF,), 0.3, 1.5, (), jnp.float32)
    down_weight = bell_draw(arg_keys[16], (FF, D), (FF // 4) ** -0.5, 0.21875)
    down_bias = bell_draw(arg_keys[17], (D,), 0.3, 1.5, (), jnp.float32)
    cotangent = bell_draw(arg_keys[18], (BATCH, L, D), 1.0, 6.0, ((0, 4), (1, 8)))
    return dict(tokens=tokens, offsets=offsets, norm_gain=norm_gain, norm_bias=norm_bias, proj_weight=proj_weight, proj_bias=proj_bias, short_filter=short_filter, short_bias=short_bias, long_kernel=long_kernel, skip_bias=skip_bias, out_weight=out_weight, out_bias=out_bias, second_gain=second_gain, second_bias=second_bias, up_weight=up_weight, up_bias=up_bias, down_weight=down_weight, down_bias=down_bias, cotangent=cotangent)


EPSILON = 1e-05

@jax.custom_vjp
def low(v):
    return lax.optimization_barrier(v.astype(jnp.bfloat16)).astype(jnp.float32)

@jax.custom_vjp
def low_back(v):
    return v

def low_keep(v):
    return (low(v), None)

def low_pass(kept, grad):
    return (grad,)

def back_keep(v):
    return (v, None)

def back_low(kept, grad):
    return (low(grad),)
low.defvjp(low_keep, low_pass)
low_back.defvjp(back_keep, back_low)

def layer_norm(values, gain, offset):
    centered = values - lax.optimization_barrier(jnp.mean(values, axis=-1, keepdims=True))
    spread = lax.rsqrt(lax.optimization_barrier(jnp.mean(centered * centered, axis=-1, keepdims=True)) + EPSILON)
    return centered * spread * gain + offset

def matmul(left, right):
    return jnp.dot(left, right, precision=lax.Precision.HIGHEST)

def long_conv(signal, kernel):
    length = signal.shape[0]
    spectrum = jnp.fft.rfft(signal, n=2 * length, axis=0)
    response = jnp.fft.rfft(kernel, n=2 * length, axis=1).T
    return jnp.fft.irfft(spectrum * response, n=2 * length, axis=0)[:length]

def block(hidden, params, start):
    norm_gain, norm_bias, proj_weight, proj_bias, short_filter, short_bias, long_kernel, skip_bias, out_weight, out_bias, second_gain, second_bias, up_weight, up_bias, down_weight, down_bias = params
    length = hidden.shape[0]
    width = hidden.shape[1]
    live = (jnp.arange(length, dtype=jnp.int32) >= start).astype(hidden.dtype)[:, None]
    normed = layer_norm(hidden, norm_gain, norm_bias)
    mixed = low_back(matmul(low(normed), proj_weight) + proj_bias)
    padded = jnp.pad(mixed, ((2, 0), (0, 0)))
    filtered = short_filter[:, 0] * padded[:length] + short_filter[:, 1] * padded[1:length + 1] + short_filter[:, 2] * padded[2:] + short_bias
    outer_gate = filtered[:, :width]
    inner_gate = filtered[:, width:2 * width]
    values = filtered[:, 2 * width:]
    gated = values * inner_gate * live
    convolved = long_conv(gated, long_kernel) + gated * skip_bias
    branch = convolved * outer_gate
    residual = hidden + low_back(matmul(low(branch), out_weight) + out_bias)
    normed_two = layer_norm(residual, second_gain, second_bias)
    expanded = low_back(matmul(low(normed_two), up_weight) + up_bias)
    return residual + matmul(low(jax.nn.gelu(expanded)), down_weight) + down_bias

def reference(tokens, offsets, norm_gain, norm_bias, proj_weight, proj_bias, short_filter, short_bias, long_kernel, skip_bias, out_weight, out_bias, second_gain, second_bias, up_weight, up_bias, down_weight, down_bias, cotangent):
    params = tuple((weight.astype(jnp.float32) for weight in (norm_gain, norm_bias, proj_weight, proj_bias, short_filter, short_bias, long_kernel, skip_bias, out_weight, out_bias, second_gain, second_bias, up_weight, up_bias, down_weight, down_bias)))

    def one_sequence(totals, triple):
        sequence, upstream, start = triple
        result, pullback = jax.vjp(lambda inner, weights: block(inner, weights, start), sequence.astype(jnp.float32), params)
        seq_grad, param_grads = pullback(upstream.astype(jnp.float32))
        totals = jax.tree.map(lambda summed, fresh: summed + fresh, totals, param_grads)
        return (totals, (result, seq_grad))
    zeros = jax.tree.map(jnp.zeros_like, params)
    totals, (outputs, input_grads) = lax.scan(one_sequence, zeros, (tokens, cotangent, offsets.astype(jnp.int32)))
    g_norm_gain, g_norm_bias, g_proj, g_proj_bias, g_filter, g_short_bias, g_kernel, g_skip, g_out, g_out_bias, g_second_gain, g_second_bias, g_up, g_up_bias, g_down, g_down_bias = totals
    return (outputs, input_grads, g_norm_gain, g_norm_bias, g_proj, g_proj_bias, g_filter, g_short_bias, g_kernel, g_skip, g_out, g_out_bias, g_second_gain, g_second_bias, g_up, g_up_bias, g_down, g_down_bias)
```

```python
import functools
import math

import jax
import jax.numpy as jnp
import ml_dtypes
import numpy as np
from jax import lax
from jax.experimental import pallas as pl
from jax.experimental.pallas import tpu as pltpu
from jax.sharding import PartitionSpec as P

EPSILON = 1e-05
PRECISE = lax.Precision.HIGHEST
NO_COST = pl.CostEstimate(flops=0, bytes_accessed=0, transcendentals=0)


def passed_along(array, axis, by):
    count = lax.axis_size(axis)
    pairs = [(i, i + by) for i in range(count) if 0 <= i + by < count]
    return lax.ppermute(array, axis, pairs)


def layer_norm(values, gain, offset):
    centered = values - jnp.mean(values, axis=-1, keepdims=True)
    spread = lax.rsqrt(jnp.mean(centered * centered, axis=-1, keepdims=True) + EPSILON)
    return centered * spread * gain + offset


def angle_table(rows, cols, modulus):
    product = (
        jnp.arange(rows, dtype=jnp.int32)[:, None]
        * jnp.arange(cols, dtype=jnp.int32)[None, :]
        % modulus
    )
    angles = product.astype(jnp.float32) * (2.0 * math.pi / modulus)
    return (jnp.cos(angles), jnp.sin(angles))


def fourier_tables(blocks, width):
    coarse_cos, coarse_sin = angle_table(blocks, 2 * blocks, 2 * blocks)
    twist_cos, twist_sin = angle_table(2 * blocks, width, 2 * blocks * width)
    fine_cos, fine_sin = angle_table(width, width, width)
    return (coarse_cos, coarse_sin, twist_cos, twist_sin, fine_cos, fine_sin)


def forward_transform(signal, tables):
    coarse_cos, coarse_sin, twist_cos, twist_sin, fine_cos, fine_sin = tables
    first_real = jnp.einsum("rpc,pk->rkc", signal, coarse_cos, precision=PRECISE)
    first_imag = -jnp.einsum("rpc,pk->rkc", signal, coarse_sin, precision=PRECISE)
    turned_real = first_real * twist_cos + first_imag * twist_sin
    turned_imag = first_imag * twist_cos - first_real * twist_sin
    spectrum_real = jnp.einsum(
        "rkc,cm->rkm", turned_real, fine_cos, precision=PRECISE
    ) + jnp.einsum("rkc,cm->rkm", turned_imag, fine_sin, precision=PRECISE)
    spectrum_imag = jnp.einsum(
        "rkc,cm->rkm", turned_imag, fine_cos, precision=PRECISE
    ) - jnp.einsum("rkc,cm->rkm", turned_real, fine_sin, precision=PRECISE)
    return (spectrum_real, spectrum_imag)


def inverse_transform(spectrum_real, spectrum_imag, tables):
    coarse_cos, coarse_sin, twist_cos, twist_sin, fine_cos, fine_sin = tables
    back_real = jnp.einsum("rkm,cm->rkc", spectrum_real, fine_cos, precision=PRECISE) - jnp.einsum(
        "rkm,cm->rkc", spectrum_imag, fine_sin, precision=PRECISE
    )
    back_imag = jnp.einsum("rkm,cm->rkc", spectrum_real, fine_sin, precision=PRECISE) + jnp.einsum(
        "rkm,cm->rkc", spectrum_imag, fine_cos, precision=PRECISE
    )
    turned_real = back_real * twist_cos - back_imag * twist_sin
    turned_imag = back_real * twist_sin + back_imag * twist_cos
    total = 2 * coarse_cos.shape[0] * twist_cos.shape[1]
    signal = jnp.einsum("rkc,pk->rpc", turned_real, coarse_cos, precision=PRECISE) - jnp.einsum(
        "rkc,pk->rpc", turned_imag, coarse_sin, precision=PRECISE
    )
    return signal / total


def by_channels(
    tokens,
    offsets,
    norm_gain,
    norm_bias,
    proj_weight,
    proj_bias,
    short_filter,
    short_bias,
    long_kernel,
    skip_bias,
    out_weight,
    out_bias,
    second_gain,
    second_bias,
    up_weight,
    up_bias,
    down_weight,
    down_bias,
    cotangent,
):
    seq_count, tok_count, features = tokens.shape
    parts = lax.axis_size("seq")
    chans = features // parts
    length = parts * tok_count
    tables = fourier_tables(parts, tok_count)
    spectral = (seq_count, chans, 2 * parts, tok_count)
    positions = lax.axis_index("seq") * tok_count + jnp.arange(tok_count, dtype=jnp.int32)
    live = (positions[None, :] >= offsets[:, None]).astype(jnp.float32)[:, :, None]
    hidden = tokens.astype(jnp.float32)
    normed, norm_pull = jax.vjp(layer_norm, hidden, norm_gain, norm_bias)
    normed_low = normed.astype(jnp.bfloat16)
    mixed = (
        jnp.einsum("sti,ij->stj", normed_low, proj_weight, preferred_element_type=jnp.float32)
        + proj_bias
    )
    rim = passed_along(mixed[:, tok_count - 2 :, :], "seq", 1)
    extended = jnp.concatenate([rim, mixed], axis=1)
    filtered = (
        short_filter[:, 0] * extended[:, :tok_count]
        + short_filter[:, 1] * extended[:, 1 : tok_count + 1]
        + short_filter[:, 2] * extended[:, 2:]
        + short_bias
    )
    outer_gate = filtered[:, :, :features]
    inner_gate = filtered[:, :, features : 2 * features]
    values = filtered[:, :, 2 * features :]
    gated = values * inner_gate * live
    gated_chan, kernel_chan = (
        lax.all_to_all(jnp.swapaxes(gated, 1, 2), "seq", split_axis=1, concat_axis=2, tiled=True),
        lax.all_to_all(long_kernel[None], "seq", split_axis=1, concat_axis=2, tiled=True),
    )
    gated_real, gated_imag = forward_transform(
        gated_chan.reshape(seq_count * chans, parts, tok_count), tables
    )
    gated_real = gated_real.reshape(spectral)
    gated_imag = gated_imag.reshape(spectral)
    kernel_real, kernel_imag = forward_transform(
        kernel_chan.reshape(chans, parts, tok_count), tables
    )
    prod_real = gated_real * kernel_real - gated_imag * kernel_imag
    prod_imag = gated_real * kernel_imag + gated_imag * kernel_real
    conv_chan = inverse_transform(
        prod_real.reshape(-1, 2 * parts, tok_count),
        prod_imag.reshape(-1, 2 * parts, tok_count),
        tables,
    )
    conv_chan = conv_chan.reshape(seq_count, chans, length)
    conv_tokens = jnp.swapaxes(
        lax.all_to_all(conv_chan, "seq", split_axis=2, concat_axis=1, tiled=True), 1, 2
    )
    convolved = conv_tokens + gated * skip_bias
    branch = convolved * outer_gate
    branch_low = branch.astype(jnp.bfloat16)
    residual = (
        hidden
        + jnp.einsum("sti,ij->stj", branch_low, out_weight, preferred_element_type=jnp.float32)
        + out_bias
    )
    normed_two, second_pull = jax.vjp(layer_norm, residual, second_gain, second_bias)
    normed_two_low = normed_two.astype(jnp.bfloat16)
    expanded = (
        jnp.einsum("sti,ij->stj", normed_two_low, up_weight, preferred_element_type=jnp.float32)
        + up_bias
    )
    activated, gelu_pull = jax.vjp(jax.nn.gelu, expanded)
    activated_low = activated.astype(jnp.bfloat16)
    output = (
        residual
        + jnp.einsum("sti,ij->stj", activated_low, down_weight, preferred_element_type=jnp.float32)
        + down_bias
    )
    upstream = cotangent.astype(jnp.float32)
    down_grad = jnp.einsum(
        "sti,stj->ij", activated_low, cotangent, preferred_element_type=jnp.float32
    )
    down_bias_grad = jnp.sum(upstream, axis=(0, 1))
    act_grad = jnp.einsum("stj,ij->sti", cotangent, down_weight, preferred_element_type=jnp.float32)
    (expanded_grad,) = gelu_pull(act_grad)
    expanded_low = expanded_grad.astype(jnp.bfloat16)
    up_grad = jnp.einsum(
        "sti,stj->ij", normed_two_low, expanded_low, preferred_element_type=jnp.float32
    )
    up_bias_grad = jnp.sum(expanded_low.astype(jnp.float32), axis=(0, 1))
    normed_two_grad = jnp.einsum(
        "stj,ij->sti", expanded_low, up_weight, preferred_element_type=jnp.float32
    )
    residual_part, second_gain_grad, second_bias_grad = second_pull(normed_two_grad)
    residual_grad = upstream + residual_part
    residual_low = residual_grad.astype(jnp.bfloat16)
    out_grad = jnp.einsum(
        "sti,stj->ij", branch_low, residual_low, preferred_element_type=jnp.float32
    )
    out_bias_grad = jnp.sum(residual_low.astype(jnp.float32), axis=(0, 1))
    branch_grad = jnp.einsum(
        "stj,ij->sti", residual_low, out_weight, preferred_element_type=jnp.float32
    )
    conv_grad = branch_grad * outer_gate
    outer_grad = branch_grad * convolved
    skip_bias_grad = jnp.sum(conv_grad * gated, axis=(0, 1))
    conv_grad_chan = lax.all_to_all(
        jnp.swapaxes(conv_grad, 1, 2), "seq", split_axis=1, concat_axis=2, tiled=True
    )
    grad_real, grad_imag = forward_transform(
        conv_grad_chan.reshape(seq_count * chans, parts, tok_count), tables
    )
    grad_real = grad_real.reshape(spectral)
    grad_imag = grad_imag.reshape(spectral)
    back_real = kernel_real * grad_real + kernel_imag * grad_imag
    back_imag = kernel_real * grad_imag - kernel_imag * grad_real
    gated_back_chan = inverse_transform(
        back_real.reshape(-1, 2 * parts, tok_count),
        back_imag.reshape(-1, 2 * parts, tok_count),
        tables,
    )
    gated_back_chan = gated_back_chan.reshape(seq_count, chans, length)
    tap_real = jnp.sum(gated_real * grad_real + gated_imag * grad_imag, axis=0)
    tap_imag = jnp.sum(gated_real * grad_imag - gated_imag * grad_real, axis=0)
    kernel_grad = inverse_transform(tap_real, tap_imag, tables).reshape(chans, length)
    gated_back = jnp.swapaxes(
        lax.all_to_all(gated_back_chan, "seq", split_axis=2, concat_axis=1, tiled=True), 1, 2
    )
    gated_grad = (gated_back + conv_grad * skip_bias) * live
    value_grad = gated_grad * inner_gate
    inner_grad = gated_grad * values
    filtered_grad = jnp.concatenate([outer_grad, inner_grad, value_grad], axis=2)
    following = passed_along(filtered_grad[:, :2, :], "seq", -1)
    grad_extended = jnp.concatenate([filtered_grad, following], axis=1)
    mixed_grad = (
        short_filter[:, 2] * grad_extended[:, :tok_count]
        + short_filter[:, 1] * grad_extended[:, 1 : tok_count + 1]
        + short_filter[:, 0] * grad_extended[:, 2:]
    )
    filter_grad = jnp.stack(
        [
            jnp.sum(filtered_grad * extended[:, position : position + tok_count], axis=(0, 1))
            for position in range(3)
        ],
        axis=1,
    )
    short_bias_grad = jnp.sum(filtered_grad, axis=(0, 1))
    mixed_low = mixed_grad.astype(jnp.bfloat16)
    proj_grad = jnp.einsum("sti,stj->ij", normed_low, mixed_low, preferred_element_type=jnp.float32)
    proj_bias_grad = jnp.sum(mixed_low.astype(jnp.float32), axis=(0, 1))
    normed_grad = jnp.einsum(
        "stj,ij->sti", mixed_low, proj_weight, preferred_element_type=jnp.float32
    )
    hidden_part, norm_gain_grad, norm_bias_grad = norm_pull(normed_grad)
    input_grad = residual_grad + hidden_part
    (
        norm_gain_share,
        norm_bias_share,
        proj_share,
        proj_bias_share,
        filter_share,
        short_bias_share,
        skip_share,
        out_share,
        out_bias_share,
        second_gain_share,
        second_bias_share,
        up_share,
        up_bias_share,
        down_share,
        down_bias_share,
    ) = (
        lax.psum_scatter(norm_gain_grad, "seq", scatter_dimension=0, tiled=True),
        lax.psum_scatter(norm_bias_grad, "seq", scatter_dimension=0, tiled=True),
        lax.psum_scatter(proj_grad, "seq", scatter_dimension=0, tiled=True),
        lax.psum_scatter(proj_bias_grad, "seq", scatter_dimension=0, tiled=True),
        lax.psum_scatter(filter_grad, "seq", scatter_dimension=0, tiled=True),
        lax.psum_scatter(short_bias_grad, "seq", scatter_dimension=0, tiled=True),
        lax.psum_scatter(skip_bias_grad, "seq", scatter_dimension=0, tiled=True),
        lax.psum_scatter(out_grad, "seq", scatter_dimension=0, tiled=True),
        lax.psum_scatter(out_bias_grad, "seq", scatter_dimension=0, tiled=True),
        lax.psum_scatter(second_gain_grad, "seq", scatter_dimension=0, tiled=True),
        lax.psum_scatter(second_bias_grad, "seq", scatter_dimension=0, tiled=True),
        lax.psum_scatter(up_grad, "seq", scatter_dimension=0, tiled=True),
        lax.psum_scatter(up_bias_grad, "seq", scatter_dimension=0, tiled=True),
        lax.psum_scatter(down_grad, "seq", scatter_dimension=0, tiled=True),
        lax.psum_scatter(down_bias_grad, "seq", scatter_dimension=0, tiled=True),
    )
    (
        norm_gain_grad,
        norm_bias_grad,
        proj_grad,
        proj_bias_grad,
        filter_grad,
        short_bias_grad,
        skip_bias_grad,
        out_grad,
        out_bias_grad,
        second_gain_grad,
        second_bias_grad,
        up_grad,
        up_bias_grad,
        down_grad,
        down_bias_grad,
        kernel_grad,
    ) = lax.psum(
        (
            norm_gain_share,
            norm_bias_share,
            proj_share,
            proj_bias_share,
            filter_share,
            short_bias_share,
            skip_share,
            out_share,
            out_bias_share,
            second_gain_share,
            second_bias_share,
            up_share,
            up_bias_share,
            down_share,
            down_bias_share,
            kernel_grad,
        ),
        "dp",
    )
    return (
        output,
        input_grad,
        norm_gain_grad,
        norm_bias_grad,
        proj_grad,
        proj_bias_grad,
        filter_grad,
        short_bias_grad,
        kernel_grad,
        skip_bias_grad,
        out_grad,
        out_bias_grad,
        second_gain_grad,
        second_bias_grad,
        up_grad,
        up_bias_grad,
        down_grad,
        down_bias_grad,
    )


def block_tables(width):
    def stacked(matrix):
        high = matrix.astype(np.float32).astype(ml_dtypes.bfloat16)
        low = (matrix - high.astype(np.float64)).astype(ml_dtypes.bfloat16)
        return np.concatenate([high, high, low], axis=1)

    odd = 2 * np.arange(width) + 1
    angles = np.pi / (2 * width) * (odd[:, None] * np.arange(width)[None, :] % (4 * width))
    analysis = np.concatenate([np.cos(angles), -np.sin(angles)], axis=0)
    angles = np.pi / (2 * width) * (np.arange(2 * width)[:, None] * odd[None, :] % (4 * width))
    synthesis = np.concatenate([np.cos(angles), -np.sin(angles)], axis=1) / width
    return stacked(analysis), stacked(synthesis)


def in_parts(values):
    high = values.astype(jnp.bfloat16)
    low = (values - high.astype(jnp.float32)).astype(jnp.bfloat16)
    return high, low


def earlier(values, by):
    rows = lax.broadcasted_iota(jnp.int32, values.shape, 0)
    return jnp.where(rows >= by, pltpu.roll(values, by, 0), 0.0)


def later(values, by):
    count = values.shape[0]
    rows = lax.broadcasted_iota(jnp.int32, values.shape, 0)
    return jnp.where(rows < count - by, pltpu.roll(values, count - by, 0), 0.0)


def short_filtered(mixed, taps):
    return (
        taps[0:1] * earlier(mixed, 2) + taps[1:2] * earlier(mixed, 1) + taps[2:3] * mixed + taps[3:4]
    )


def analyse(signal, table_ref, spectra_ref):
    blocks, double, lanes = spectra_ref.shape
    width = double // 2
    high, low = in_parts(signal)
    for first in range(0, blocks, 2):
        columns = []
        for block in (first, first + 1):
            rows = slice(block * width, (block + 1) * width)
            columns.append(jnp.concatenate([high[rows], low[rows], high[rows]], axis=0))
        found = jnp.dot(
            table_ref[...], jnp.concatenate(columns, axis=1), preferred_element_type=jnp.float32
        )
        spectra_ref[first] = found[:, :lanes]
        spectra_ref[first + 1] = found[:, lanes:]


def analyse_kernel(kernel_ref, table_ref, spectra_ref):
    blocks, double, lanes = spectra_ref.shape
    for first in range(0, blocks, 2):
        rows = []
        for block in (first, first + 1):
            high, low = in_parts(kernel_ref[block])
            rows.append(jnp.concatenate([high, low, high], axis=1))
        found = lax.dot_general(
            table_ref[...],
            jnp.concatenate(rows, axis=0),
            (((1,), (1,)), ((), ())),
            preferred_element_type=jnp.float32,
        )
        spectra_ref[first] = found[:, :lanes]
        spectra_ref[first + 1] = found[:, lanes:]


def synthesise(spectra_ref, table_ref):
    blocks, double, lanes = spectra_ref.shape
    found = []
    for first in range(0, blocks, 2):
        columns = []
        for block in (first, first + 1):
            high, low = in_parts(spectra_ref[block])
            columns.append(jnp.concatenate([high, low, high], axis=0))
        pair = jnp.dot(
            table_ref[...], jnp.concatenate(columns, axis=1), preferred_element_type=jnp.float32
        )
        found.append(pair[:, :lanes])
        found.append(pair[:, lanes:])
    return found


def multiply(left_ref, right_ref, out_ref, reverse):
    blocks, double, lanes = out_ref.shape
    width = double // 2

    def step(index, carry):
        real_rows = pl.ds(pl.multiple_of(index * 8, 8), 8)
        imag_rows = pl.ds(pl.multiple_of(width + index * 8, 8), 8)
        left_real = [left_ref[block, real_rows] for block in range(blocks)]
        left_imag = [left_ref[block, imag_rows] for block in range(blocks)]
        right_real = [right_ref[block, real_rows] for block in range(blocks)]
        right_imag = [right_ref[block, imag_rows] for block in range(blocks)]
        for m in range(blocks):
            real = imag = None
            for l in range(blocks - m if reverse else m + 1):
                r = m + l if reverse else m - l
                if reverse:
                    new_real = left_real[l] * right_real[r] + left_imag[l] * right_imag[r]
                    new_imag = left_real[l] * right_imag[r] - left_imag[l] * right_real[r]
                else:
                    new_real = left_real[l] * right_real[r] - left_imag[l] * right_imag[r]
                    new_imag = left_real[l] * right_imag[r] + left_imag[l] * right_real[r]
                real = new_real if real is None else real + new_real
                imag = new_imag if imag is None else imag + new_imag
            out_ref[m, real_rows] = real
            out_ref[m, imag_rows] = imag
        return carry

    lax.fori_loop(0, width // 8, step, 0)


def gates(start_ref, mixed_refs, taps_ref):
    outer, inner, values = [
        short_filtered(ref[...], taps_ref[group]) for group, ref in enumerate(mixed_refs)
    ]
    rows = lax.broadcasted_iota(jnp.int32, outer.shape, 0)
    live = (rows >= start_ref[0]).astype(jnp.float32)
    return outer, inner, values, live


def forward_kernel(
    start_ref,
    outer_ref,
    inner_ref,
    value_ref,
    kernel_ref,
    taps_ref,
    skip_ref,
    analysis_ref,
    synthesis_ref,
    convolved_ref,
    branch_ref,
    signal_spectra,
    kernel_spectra,
    spectra,
):
    width = kernel_ref.shape[2]
    outer, inner, values, live = gates(start_ref, (outer_ref, inner_ref, value_ref), taps_ref)
    gated = values * inner * live
    analyse(gated, analysis_ref, signal_spectra)
    analyse_kernel(kernel_ref, analysis_ref, kernel_spectra)
    multiply(kernel_spectra, signal_spectra, spectra, False)
    found = synthesise(spectra, synthesis_ref)
    pieces = [found[0][:width]]
    for block in range(1, len(found)):
        pieces.append(found[block][:width] + found[block - 1][width:])
    convolved = jnp.concatenate(pieces, axis=0) + gated * skip_ref[...]
    convolved_ref[...] = convolved
    branch_ref[...] = (convolved * outer).astype(jnp.bfloat16)


def lag_blocks(found, width):
    pieces = []
    for block in range(len(found)):
        piece = found[block][:width]
        if block + 1 < len(found):
            piece = piece - found[block + 1][width:]
        pieces.append(piece)
    return pieces


def backward_kernel(
    start_ref,
    grad_ref,
    convolved_ref,
    outer_ref,
    inner_ref,
    value_ref,
    kernel_ref,
    taps_ref,
    skip_ref,
    analysis_ref,
    synthesis_ref,
    mixed_grad_ref,
    kernel_grad_ref,
    sums_ref,
    signal_spectra,
    kernel_spectra,
    grad_spectra,
    spectra,
):
    width = kernel_ref.shape[2]
    mixed_refs = (outer_ref, inner_ref, value_ref)
    outer, inner, values, live = gates(start_ref, mixed_refs, taps_ref)
    gated = values * inner * live
    branch_grad = grad_ref[...]
    conv_grad = branch_grad * outer
    outer_grad = branch_grad * convolved_ref[...]
    analyse(gated, analysis_ref, signal_spectra)
    analyse_kernel(kernel_ref, analysis_ref, kernel_spectra)
    analyse(conv_grad, analysis_ref, grad_spectra)
    multiply(signal_spectra, grad_spectra, spectra, True)
    lags = lag_blocks(synthesise(spectra, synthesis_ref), width)
    half = len(lags) // 2
    for block, piece in enumerate(lags):
        first = block % half * width
        kernel_grad_ref[block // half, :, first : first + width] = piece.T
    multiply(kernel_spectra, grad_spectra, spectra, True)
    back = jnp.concatenate(lag_blocks(synthesise(spectra, synthesis_ref), width), axis=0)
    gated_grad = (back + conv_grad * skip_ref[...]) * live

    def total(array):
        return jnp.sum(array, axis=0, keepdims=True)

    filter_rows, bias_rows, low_rows = [], [], []
    grads = (outer_grad, gated_grad * values, gated_grad * inner)
    for group in range(3):
        grad, mixed, taps = grads[group], mixed_refs[group][...], taps_ref[group]
        next_one, next_two = later(grad, 1), later(grad, 2)
        mixed_grad = taps[2:3] * grad + taps[1:2] * next_one + taps[0:1] * next_two
        low = mixed_grad.astype(jnp.bfloat16)
        mixed_grad_ref[group] = low
        filter_rows += [total(next_two * mixed), total(next_one * mixed), total(grad * mixed)]
        bias_rows.append(total(grad))
        low_rows.append(total(low.astype(jnp.float32)))
    rows = filter_rows + bias_rows + low_rows + [total(conv_grad * gated)]
    sums_ref[...] = jnp.concatenate(rows, axis=0)


def kernel_parameters():
    return pltpu.CompilerParams(
        vmem_limit_bytes=56 * 1024 * 1024
    )


def kernel_specs(tokens, parts, width, lanes, features):
    groups = features // lanes

    def mixed(group):
        return pl.BlockSpec((tokens, lanes), lambda tile, *_: (0, group * groups + tile))

    return (
        [pl.BlockSpec(memory_space=pltpu.SMEM)],
        [mixed(0), mixed(1), mixed(2)],
        [
            pl.BlockSpec((parts, lanes, width), lambda tile, *_: (0, tile, 0)),
            pl.BlockSpec((3, 4, lanes), lambda tile, *_: (0, 0, tile)),
            pl.BlockSpec((1, lanes), lambda tile, *_: (0, tile)),
            pl.BlockSpec((2 * width, 3 * width), lambda *_: (0, 0)),
            pl.BlockSpec((2 * width, 6 * width), lambda *_: (0, 0)),
        ],
        pl.BlockSpec((tokens, lanes), lambda tile, *_: (0, tile)),
        pltpu.VMEM((parts, 2 * width, lanes), jnp.float32),
    )


def forward_convolution(start, mixed, kernel, taps, skip, tables, lanes=128):
    parts, features, width = kernel.shape
    tokens = mixed.shape[0]
    start_spec, mixed_specs, rest, plain, spectra = kernel_specs(tokens, parts, width, lanes, features)
    return pl.pallas_call(
        forward_kernel,
        grid=(features // lanes,),
        in_specs=start_spec + mixed_specs + rest,
        out_specs=(plain, plain),
        out_shape=(
            jax.ShapeDtypeStruct((tokens, features), jnp.float32),
            jax.ShapeDtypeStruct((tokens, features), jnp.bfloat16),
        ),
        scratch_shapes=[spectra] * 3,
        compiler_params=kernel_parameters(),
        cost_estimate=NO_COST,
        name="forward_convolution",
    )(start, mixed, mixed, mixed, kernel, taps, skip, *tables)


def backward_convolution(start, grad, convolved, mixed, kernel, taps, skip, tables, lanes=128):
    parts, features, width = kernel.shape
    tokens = mixed.shape[0]
    start_spec, mixed_specs, rest, plain, spectra = kernel_specs(tokens, parts, width, lanes, features)
    return pl.pallas_call(
        backward_kernel,
        grid=(features // lanes,),
        in_specs=start_spec + [plain, plain] + mixed_specs + rest,
        out_specs=(
            pl.BlockSpec((3, tokens, lanes), lambda tile: (0, 0, tile)),
            pl.BlockSpec((2, lanes, tokens // 2), lambda tile: (0, tile, 0)),
            pl.BlockSpec((16, lanes), lambda tile: (0, tile)),
        ),
        out_shape=(
            jax.ShapeDtypeStruct((3, tokens, features), jnp.bfloat16),
            jax.ShapeDtypeStruct((2, features, tokens // 2), jnp.float32),
            jax.ShapeDtypeStruct((16, features), jnp.float32),
        ),
        scratch_shapes=[spectra] * 4,
        compiler_params=kernel_parameters(),
        cost_estimate=NO_COST,
        name="backward_convolution",
    )(start, grad, convolved, mixed, mixed, mixed, kernel, taps, skip, *tables)


def unit_rows(values):
    centered = values - jnp.mean(values, axis=-1, keepdims=True)
    spread = lax.rsqrt(jnp.mean(centered * centered, axis=-1, keepdims=True) + EPSILON)
    return centered * spread, spread


def unit_rows_back(grad, unit, spread, gain):
    scaled = grad * gain
    inner = scaled - jnp.mean(scaled, axis=-1, keepdims=True)
    return (inner - unit * jnp.mean(scaled * unit, axis=-1, keepdims=True)) * spread


def matmul(left, right):
    return jnp.dot(left, right, preferred_element_type=jnp.float32)


def matmul_back(left, right):
    return lax.dot_general(left, right, (((1,), (1,)), ((), ())), preferred_element_type=jnp.float32)


def column_pair(array):
    half = array.shape[1] // 2
    return array[:, :half], array[:, half:]


def column_sums(array):
    return jnp.sum(array, axis=0, keepdims=True)


def project_kernel(x_ref, gain_ref, bias_ref, weight_ref, offset_ref, normed_ref, mixed_ref):
    unit, _ = unit_rows(x_ref[...])
    normed = (unit * gain_ref[...] + bias_ref[...]).astype(jnp.bfloat16)
    normed_ref[...] = normed
    mixed_ref[...] = matmul(normed, weight_ref[...]) + offset_ref[...]


def feed_kernel(
    x_ref,
    branch_ref,
    out_weight_ref,
    out_bias_ref,
    gain_ref,
    bias_ref,
    up_weight_ref,
    up_bias_ref,
    down_weight_ref,
    down_bias_ref,
    residual_ref,
    normed_ref,
    activated_ref,
    slope_ref,
    *output_refs,
):
    residual = x_ref[...] + matmul(branch_ref[...], out_weight_ref[...]) + out_bias_ref[...]
    residual_ref[...] = residual
    unit, _ = unit_rows(residual)
    normed = (unit * gain_ref[...] + bias_ref[...]).astype(jnp.bfloat16)
    normed_ref[...] = normed
    total = residual + down_bias_ref[...]
    factor = math.sqrt(2.0 / math.pi)
    chunk = residual.shape[1]
    for first in range(0, up_weight_ref.shape[1], chunk):
        columns = slice(first, first + chunk)
        expanded = matmul(normed, up_weight_ref[:, columns]) + up_bias_ref[:, columns]
        square = expanded * expanded
        turned = jnp.tanh(factor * (expanded + 0.044715 * (square * expanded)))
        half = 0.5 + 0.5 * turned
        activated = (expanded * half).astype(jnp.bfloat16)
        activated_ref[:, columns] = activated
        slope_ref[:, columns] = half + (0.5 * factor) * expanded * (1.0 - turned * turned) * (
            1.0 + (3 * 0.044715) * square
        )
        total = total + matmul(activated, down_weight_ref[columns, :])
    for ref, half in zip(output_refs, column_pair(total)):
        ref[...] = half


def feed_back_kernel(
    grad_ref,
    residual_ref,
    slope_ref,
    gain_ref,
    out_weight_ref,
    up_weight_ref,
    down_weight_ref,
    expanded_ref,
    residual_grad_ref,
    residual_low_ref,
    branch_grad_ref,
    sums_ref,
    wide_sums_ref,
):
    grad = grad_ref[...]
    grad_low = grad.astype(jnp.bfloat16)
    chunk = grad.shape[1]
    normed_grad = None
    wide = []
    for first in range(0, up_weight_ref.shape[1], chunk):
        columns = slice(first, first + chunk)
        expanded = matmul_back(grad_low, down_weight_ref[columns, :]) * slope_ref[:, columns]
        low = expanded.astype(jnp.bfloat16)
        expanded_ref[:, columns] = low
        wide.append(column_sums(low.astype(jnp.float32)))
        part = matmul_back(low, up_weight_ref[:, columns])
        normed_grad = part if normed_grad is None else normed_grad + part
    unit, spread = unit_rows(residual_ref[...])
    residual_grad = grad + unit_rows_back(normed_grad, unit, spread, gain_ref[...])
    residual_grad_ref[...] = residual_grad
    low = residual_grad.astype(jnp.bfloat16)
    residual_low_ref[...] = low
    branch_grad_ref[...] = matmul_back(low, out_weight_ref[...])
    sums = [
        column_sums(normed_grad * unit),
        column_sums(normed_grad),
        column_sums(low.astype(jnp.float32)),
        column_sums(grad),
    ]

    @pl.when(pl.program_id(0) == 0)
    def _():
        sums_ref[...] = jnp.zeros_like(sums_ref)
        wide_sums_ref[...] = jnp.zeros_like(wide_sums_ref)

    sums_ref[...] += jnp.concatenate(sums, axis=0)
    wide_sums_ref[...] += jnp.concatenate(wide, axis=1)


def input_grad_kernel(
    mixed_ref, weight_ref, x_ref, gain_ref, residual_grad_ref, first_ref, second_ref, sums_ref
):
    features = x_ref.shape[1]
    normed_grad = None
    for group in range(3):
        columns = slice(group * features, (group + 1) * features)
        part = matmul_back(mixed_ref[group], weight_ref[:, columns])
        normed_grad = part if normed_grad is None else normed_grad + part
    unit, spread = unit_rows(x_ref[...])
    total = residual_grad_ref[...] + unit_rows_back(normed_grad, unit, spread, gain_ref[...])
    first_ref[...], second_ref[...] = column_pair(total)
    sums = jnp.concatenate([column_sums(normed_grad * unit), column_sums(normed_grad)], axis=0)

    @pl.when(pl.program_id(0) == 0)
    def _():
        sums_ref[...] = jnp.zeros_like(sums_ref)

    sums_ref[...] += sums


def by_rows(kernel, name, rows, inputs, outputs, height=256):
    def spec(shape, held):
        if len(shape) == 3:
            return pl.BlockSpec((shape[0], height, shape[2]), lambda step: (0, step, 0))
        if shape[0] == rows and not held:
            return pl.BlockSpec((height, shape[1]), lambda step: (step, 0))
        return pl.BlockSpec(shape, lambda step: (0, 0))

    return pl.pallas_call(
        kernel,
        grid=(rows // height,),
        in_specs=[spec(array.shape, held) for array, held in inputs],
        out_specs=tuple(spec(shape, False) for shape, _ in outputs),
        out_shape=tuple(jax.ShapeDtypeStruct(shape, kind) for shape, kind in outputs),
        compiler_params=kernel_parameters(),
        cost_estimate=NO_COST,
        name=name,
    )(*[array for array, _ in inputs])


def product_kernel(half_ref, left_ref, right_ref, out_ref):
    out_ref[...] = product_tile(left_ref, right_ref)


def product_tile(left_ref, right_ref):
    if len(right_ref.shape) == 2:
        return product(left_ref[...], right_ref[...])
    return jnp.concatenate(
        [product(left_ref[...], right_ref[group]) for group in range(right_ref.shape[0])], axis=1
    )


def product_specs(left, right, tile):
    tokens = left.shape[0]
    half = right.shape[-1] // 2
    left_spec = pl.BlockSpec((tokens, tile), lambda step, half_ref: (0, step))
    if right.ndim == 2:
        right_spec = pl.BlockSpec((tokens, half), lambda step, half_ref: (0, half_ref[0]))
        return half, left_spec, right_spec
    right_spec = pl.BlockSpec((right.shape[0], tokens, half), lambda step, half_ref: (0, 0, half_ref[0]))
    return half * right.shape[0], left_spec, right_spec


def half_product(left, right, half, tile=384):
    rows = left.shape[1]
    columns, left_spec, right_spec = product_specs(left, right, tile)
    return pl.pallas_call(
        product_kernel,
        grid_spec=pltpu.PrefetchScalarGridSpec(
            num_scalar_prefetch=1,
            grid=(rows // tile,),
            in_specs=[left_spec, right_spec],
            out_specs=pl.BlockSpec((tile, columns), lambda step, half_ref: (step, 0)),
        ),
        out_shape=jax.ShapeDtypeStruct((rows, columns), jnp.float32),
        compiler_params=kernel_parameters(),
        cost_estimate=NO_COST,
        name="half_product",
    )(half, left, right)


def parted_product_kernel(bits_ref, left_ref, right_ref, taken_ref, kept_ref, given_ref):
    total = product_tile(left_ref, right_ref) + taken_ref[...]
    pieces, rows, _ = kept_ref.shape
    first = bits_ref[1] == 0
    for piece in range(pieces):
        one = total[2 * piece * rows : (2 * piece + 1) * rows]
        two = total[(2 * piece + 1) * rows : (2 * piece + 2) * rows]
        kept_ref[piece] = jnp.where(first, one, two)
        given_ref[piece] = jnp.where(first, two, one)


def parted_product(left, right, half, taken, which, pieces, tile=384):
    rows = left.shape[1]
    columns, left_spec, right_spec = product_specs(left, right, tile)
    height = rows // (2 * pieces)
    steps = rows // tile
    part = pl.BlockSpec((pieces // steps, height, columns), lambda step, bits_ref: (step, 0, 0))
    shape = jax.ShapeDtypeStruct((pieces, height, columns), jnp.float32)
    return pl.pallas_call(
        parted_product_kernel,
        grid_spec=pltpu.PrefetchScalarGridSpec(
            num_scalar_prefetch=1,
            grid=(steps,),
            in_specs=[
                left_spec,
                right_spec,
                pl.BlockSpec((tile, columns), lambda step, bits_ref: (step, 0)),
            ],
            out_specs=(part, part),
        ),
        out_shape=(shape, shape),
        compiler_params=kernel_parameters(),
        cost_estimate=NO_COST,
        name="parted_product",
    )(jnp.concatenate([half, which]), left, right, taken)


def fold_kernel(bit_ref, kept_ref, taken_ref, kept_out_ref, given_out_ref):
    total = kept_ref[...] + taken_ref[...]
    first = bit_ref[0] == 0
    kept_out_ref[0] = jnp.where(first, total[0], total[1])
    given_out_ref[0] = jnp.where(first, total[1], total[0])


def fold(kept, taken, which):
    count, rows, columns = kept.shape
    pair = pl.BlockSpec((2, rows, columns), lambda step: (step, 0, 0))
    one = pl.BlockSpec((1, rows, columns), lambda step: (step, 0, 0))
    shape = jax.ShapeDtypeStruct((count // 2, rows, columns), jnp.float32)
    return pl.pallas_call(
        fold_kernel,
        grid=(count // 2,),
        in_specs=[pl.BlockSpec(memory_space=pltpu.SMEM), pair, pair],
        out_specs=(one, one),
        out_shape=(shape, shape),
        compiler_params=kernel_parameters(),
        cost_estimate=NO_COST,
        name="fold",
    )(which, kept, taken)


def swapped(array, axis, by):
    count = lax.axis_size(axis)
    return lax.ppermute(array, axis, [(i, i ^ by) for i in range(count)])


def bit(axis, by):
    return (lax.axis_index(axis) // by) % 2


def doubled(array, dim, axis, by):
    other = swapped(array, axis, by)
    first = bit(axis, by) == 0
    return jnp.concatenate(
        [jnp.where(first, array, other), jnp.where(first, other, array)], axis=dim
    )


def dp_gathered(share):
    return doubled(doubled(share, 0, "dp", 2), 1, "dp", 1)


def product(left, columns):
    return lax.dot_general(left, columns, (((0,), (0,)), ((), ())), preferred_element_type=jnp.float32)


def flag(axis, by):
    return bit(axis, by).astype(jnp.int32).reshape(1)


def shards(array, seq_parts):
    rows, columns = array.shape
    return array.reshape(2 * seq_parts, rows // (2 * seq_parts), columns)


def reduced(kept, given, steps):
    for (axis, by), following in zip(steps, steps[1:] + [None]):
        taken = swapped(given, axis, by)
        if following is None:
            return dp_gathered((kept + taken)[0])
        kept, given = fold(kept, taken, flag(*following))


def by_sequences(
    tokens,
    offsets,
    norm_gain,
    norm_bias,
    proj_weight,
    proj_bias,
    short_filter,
    short_bias,
    long_kernel,
    skip_bias,
    out_weight,
    out_bias,
    second_gain,
    second_bias,
    up_weight,
    up_bias,
    down_weight,
    down_bias,
    cotangent,
):
    parts, width, features = tokens.shape
    length = parts * width
    hidden_units = up_weight.shape[1]
    hold = lax.optimization_barrier
    tables = tuple(jnp.asarray(table) for table in block_tables(width))
    start = lax.dynamic_slice_in_dim(offsets, lax.axis_index("seq"), 1, 0)
    core, other_core = flag("dp", 1), 1 - flag("dp", 1)
    low, single = jnp.bfloat16, jnp.float32
    y_step, x_step = ("dp", 2), ("seq", 1)
    z_steps = [("seq", 1 << place) for place in range(1, parts.bit_length() - 1)]

    share = features // 4
    chunk = bit("dp", 1) * 2 + bit("dp", 2)
    piece = lax.dynamic_slice_in_dim(long_kernel, chunk * share, share, 0)[None]
    for axis, by in z_steps[::-1]:
        piece = doubled(piece[:, None], 1, axis, by)
        piece = piece.reshape((-1,) + piece.shape[2:])
    hidden = tokens.astype(single)
    hidden, piece = hold((hidden, piece))
    hidden = lax.all_to_all(hidden, "seq", 0, 0, tiled=True)
    piece = doubled(piece[:, None], 1, *x_step).reshape(parts, share, width)
    kernel = doubled(doubled(piece, 1, "dp", 2), 1, "dp", 1)
    upstream = cotangent.astype(single)
    taps = jnp.concatenate([short_filter.T, short_bias[None]], axis=0)
    taps = jnp.swapaxes(taps.reshape(4, 3, features), 0, 1)
    skip = skip_bias[None]
    hidden, kernel, upstream, taps, start = hold((hidden, kernel, upstream, taps, start))

    upstream = lax.all_to_all(upstream, "seq", 0, 0, tiled=True)
    hidden = hidden.reshape(length, features)
    normed_low, mixed = by_rows(
        project_kernel,
        "project",
        length,
        [
            (hidden, False),
            (norm_gain[None], True),
            (norm_bias[None], True),
            (proj_weight, True),
            (proj_bias[None], True),
        ],
        [((length, features), low), ((length, 3 * features), single)],
    )
    convolved, branch_low = forward_convolution(start, mixed, kernel, taps, skip, tables)
    residual, normed_two_low, activated_low, slope, *output = by_rows(
        feed_kernel,
        "feed",
        length,
        [
            (hidden, False),
            (branch_low, False),
            (out_weight, True),
            (out_bias[None], True),
            (second_gain[None], True),
            (second_bias[None], True),
            (up_weight, True),
            (up_bias[None], True),
            (down_weight, True),
            (down_bias[None], True),
        ],
        [
            ((length, features), single),
            ((length, features), low),
            ((length, hidden_units), low),
            ((length, hidden_units), single),
            ((length, features // 2), single),
            ((length, features // 2), single),
        ],
    )
    upstream, output = hold((upstream, output))

    def sent(half):
        half = half.reshape(parts, width, features // 2)
        return lax.all_to_all(half, "seq", 0, 0, tiled=True)

    output[0] = sent(output[0])
    upstream = upstream.reshape(length, features)
    upstream_low = upstream.astype(low)
    down_given = half_product(activated_low, upstream_low, other_core)
    upstream, down_given = hold((upstream, down_given))

    down_taken = swapped(down_given, "dp", 1)
    expanded_low, residual_grad, residual_low, branch_grad, sums_two, wide_sums = by_rows(
        feed_back_kernel,
        "feed_back",
        length,
        [
            (upstream, False),
            (residual, False),
            (slope, False),
            (second_gain[None], True),
            (out_weight, True),
            (up_weight, True),
            (down_weight, True),
        ],
        [
            ((length, hidden_units), low),
            ((length, features), single),
            ((length, features), low),
            ((length, features), single),
            ((4, features), single),
            ((1, hidden_units), single),
        ],
    )
    up_given = half_product(normed_two_low, expanded_low, other_core)
    out_given = half_product(branch_low, residual_low, other_core)
    output, up_given, out_given, down_taken = hold((output, up_given, out_given, down_taken))

    up_taken = swapped(up_given, "dp", 1)
    out_taken = swapped(out_given, "dp", 1)
    down_kept, down_given = parted_product(
        activated_low, upstream_low, core, down_taken, flag(*y_step), parts
    )
    output, down_given, up_taken, out_taken = hold((output, down_given, up_taken, out_taken))

    output[1] = sent(output[1])
    down_taken = swapped(down_given, *y_step)
    up_kept, up_given = parted_product(
        normed_two_low, expanded_low, core, up_taken, flag(*x_step), parts // 2
    )
    branch_grad, up_given = hold((branch_grad, up_given))
    up_taken = swapped(up_given, *x_step)
    mixed_low, kernel_grad, sums = backward_convolution(
        start, branch_grad, convolved, mixed, kernel, taps, skip, tables
    )
    mixed_low, kernel_grad, down_taken, output = hold((mixed_low, kernel_grad, down_taken, output))

    down_kept, down_given = fold(down_kept, down_taken, flag(*x_step))
    kernel_kept = lax.dynamic_index_in_dim(kernel_grad, core[0], 0, keepdims=False)
    kernel_given = lax.dynamic_index_in_dim(kernel_grad, other_core[0], 0, keepdims=False)
    mixed_low, down_given, kernel_given = hold((mixed_low, down_given, kernel_given))
    down_taken = swapped(down_given, *x_step)
    kernel_taken = swapped(kernel_given, "dp", 1)
    *input_grad, sums_one = by_rows(
        input_grad_kernel,
        "input_grad",
        length,
        [
            (mixed_low, False),
            (proj_weight, True),
            (hidden, False),
            (norm_gain[None], True),
            (residual_grad, False),
        ],
        [
            ((length, features // 2), single),
            ((length, features // 2), single),
            ((2, features), single),
        ],
    )
    input_grad, mixed_low, kernel_taken, up_taken, sums_one, out_taken = hold(
        (input_grad, mixed_low, kernel_taken, up_taken, sums_one, out_taken)
    )

    input_grad[0] = sent(input_grad[0])
    proj_given = half_product(normed_low, mixed_low, other_core)
    proj_taken = swapped(proj_given, "dp", 1)
    rows = features // (2 * parts)
    up_kept, up_taken = [array.reshape(parts, rows, -1) for array in (up_kept, up_taken)]
    up_kept, up_given = fold(up_kept, up_taken, flag(*y_step))
    up_taken = swapped(up_given, *y_step)
    out_kept, out_given = parted_product(
        branch_low, residual_low, core, out_taken, flag(*y_step), parts
    )
    kernel_sum = shards(kernel_kept + kernel_taken, parts)
    input_grad, proj_taken, up_taken, down_taken, sums, out_given, kernel_sum = hold(
        (input_grad, proj_taken, up_taken, down_taken, sums, out_given, kernel_sum)
    )

    input_grad[1] = sent(input_grad[1])
    proj_kept, proj_given = parted_product(
        normed_low, mixed_low, core, proj_taken, flag(*y_step), parts
    )
    proj_taken = swapped(proj_given, *y_step)
    down_kept, down_given = fold(down_kept, down_taken, flag(*z_steps[0]))
    up_kept, up_given = fold(up_kept, up_taken, flag(*z_steps[0]))
    vectors = [
        sums_one[0],
        sums_one[1],
        sums[12:15].reshape(-1),
        jnp.swapaxes(sums[:9].reshape(3, 3, features), 1, 2).reshape(-1),
        sums[9:12].reshape(-1),
        sums[15],
        sums_two[2],
        sums_two[0],
        sums_two[1],
        wide_sums[0],
        sums_two[3],
    ]
    sizes = [vector.shape[0] // parts for vector in vectors]
    packed = jnp.concatenate([vector.reshape(parts, -1) for vector in vectors], axis=1)
    packed = jnp.pad(packed, ((0, 0), (0, 4 * rows * 128 - packed.shape[1])))
    packed = packed.reshape(parts, 2, 2 * rows, 128)
    packed_kept = lax.dynamic_index_in_dim(packed, core[0], 1, keepdims=False)
    packed_given = lax.dynamic_index_in_dim(packed, other_core[0], 1, keepdims=False)
    packed = packed_kept + swapped(packed_given, "dp", 1)
    rest = jnp.concatenate([kernel_sum, packed.reshape(2 * parts, rows, 128)], axis=2)
    rest = rest.reshape(parts, 2, rows, -1)
    rest_kept = lax.dynamic_index_in_dim(rest, flag(*y_step)[0], 1, keepdims=False)
    rest_given = lax.dynamic_index_in_dim(rest, 1 - flag(*y_step)[0], 1, keepdims=False)
    rest_kept = jnp.concatenate([out_kept, rest_kept], axis=2)
    rest_given = jnp.concatenate([out_given, rest_given], axis=2)

    rest_taken = swapped(rest_given, *y_step)
    input_grad, proj_taken, rest_taken, down_given, up_given = hold(
        (input_grad, proj_taken, rest_taken, down_given, up_given)
    )
    proj_share = reduced(*fold(proj_kept, proj_taken, flag(*x_step)), [x_step] + z_steps)
    rest = reduced(*fold(rest_kept, rest_taken, flag(*x_step)), [x_step] + z_steps)
    down_share = reduced(down_kept, down_given, z_steps)
    up_share = reduced(up_kept, up_given, z_steps)
    output = jnp.concatenate(output, axis=2)
    input_grad = jnp.concatenate(input_grad, axis=2)

    proj_share = proj_share.reshape(-1, 2, 3, features // 2)
    proj_share = jnp.swapaxes(proj_share, 1, 2).reshape(-1, 3 * features)
    columns = rest.shape[1] // 2
    ends = [features // 2, features // 2 + length // 2, columns]
    out_share, kernel_share, packed = [
        jnp.concatenate([rest[:, first:end], rest[:, columns + first : columns + end]], axis=1)
        for first, end in zip([0] + ends, ends)
    ]
    packed = jnp.swapaxes(packed.reshape(2, rows, 2, 128), 1, 2)
    packed = jnp.swapaxes(packed, 0, 1).reshape(-1)
    ends = np.cumsum(sizes)
    vectors = [packed[end - size : end] for size, end in zip(sizes, ends)]
    return (
        output,
        input_grad,
        vectors[0],
        vectors[1],
        proj_share,
        vectors[2],
        vectors[3].reshape(-1, 3),
        vectors[4],
        kernel_share,
        vectors[5],
        out_share,
        vectors[6],
        vectors[7],
        vectors[8],
        up_share,
        vectors[9],
        down_share,
        vectors[10],
    )


def per_device(tokens, offsets, *rest):
    fits = (
        tokens.shape[0] == lax.axis_size("seq")
        and lax.axis_size("dp") == 4
        and tokens.shape[0] % 2 == 0
        and tokens.shape[1] % 128 == 0
        and lax.axis_size("seq") & (lax.axis_size("seq") - 1) == 0
    )
    plan = by_sequences if fits else by_channels
    return plan(tokens, offsets, *rest)


def solution(mesh):
    return jax.shard_map(
        per_device,
        mesh=mesh,
        in_specs=(
            P("dp", "seq", None),
            P("dp"),
            P(),
            P(),
            P(),
            P(),
            P(),
            P(),
            P(None, "seq"),
            P(),
            P(),
            P(),
            P(),
            P(),
            P(),
            P(),
            P(),
            P(),
            P("dp", "seq", None),
        ),
        out_specs=(
            P("dp", "seq", None),
            P("dp", "seq", None),
            P("seq"),
            P("seq"),
            P("seq", None),
            P("seq"),
            P("seq", None),
            P("seq"),
            P("seq", None),
            P("seq"),
            P("seq", None),
            P("seq"),
            P("seq"),
            P("seq"),
            P("seq", None),
            P("seq"),
            P("seq", None),
            P("seq"),
        ),
        check_vma=False,
    )
```

```python
import functools
import math

import jax
import jax.numpy as jnp
import ml_dtypes
import numpy as np
from jax import lax
from jax.experimental import pallas as pl
from jax.experimental.pallas import tpu as pltpu
from jax.sharding import PartitionSpec as P

EPSILON = 1e-05
PRECISE = lax.Precision.HIGHEST
NO_COST = pl.CostEstimate(flops=0, bytes_accessed=0, transcendentals=0)


def passed_along(array, axis, by):
    count = lax.axis_size(axis)
    pairs = [(i, i + by) for i in range(count) if 0 <= i + by < count]
    return lax.ppermute(array, axis, pairs)


def layer_norm(values, gain, offset):
    centered = values - jnp.mean(values, axis=-1, keepdims=True)
    spread = lax.rsqrt(jnp.mean(centered * centered, axis=-1, keepdims=True) + EPSILON)
    return centered * spread * gain + offset


def angle_table(rows, cols, modulus):
    product = (
        jnp.arange(rows, dtype=jnp.int32)[:, None]
        * jnp.arange(cols, dtype=jnp.int32)[None, :]
        % modulus
    )
    angles = product.astype(jnp.float32) * (2.0 * math.pi / modulus)
    return (jnp.cos(angles), jnp.sin(angles))


def fourier_tables(blocks, width):
    coarse_cos, coarse_sin = angle_table(blocks, 2 * blocks, 2 * blocks)
    twist_cos, twist_sin = angle_table(2 * blocks, width, 2 * blocks * width)
    fine_cos, fine_sin = angle_table(width, width, width)
    return (coarse_cos, coarse_sin, twist_cos, twist_sin, fine_cos, fine_sin)


def forward_transform(signal, tables):
    coarse_cos, coarse_sin, twist_cos, twist_sin, fine_cos, fine_sin = tables
    first_real = jnp.einsum("rpc,pk->rkc", signal, coarse_cos, precision=PRECISE)
    first_imag = -jnp.einsum("rpc,pk->rkc", signal, coarse_sin, precision=PRECISE)
    turned_real = first_real * twist_cos + first_imag * twist_sin
    turned_imag = first_imag * twist_cos - first_real * twist_sin
    spectrum_real = jnp.einsum(
        "rkc,cm->rkm", turned_real, fine_cos, precision=PRECISE
    ) + jnp.einsum("rkc,cm->rkm", turned_imag, fine_sin, precision=PRECISE)
    spectrum_imag = jnp.einsum(
        "rkc,cm->rkm", turned_imag, fine_cos, precision=PRECISE
    ) - jnp.einsum("rkc,cm->rkm", turned_real, fine_sin, precision=PRECISE)
    return (spectrum_real, spectrum_imag)


def inverse_transform(spectrum_real, spectrum_imag, tables):
    coarse_cos, coarse_sin, twist_cos, twist_sin, fine_cos, fine_sin = tables
    back_real = jnp.einsum("rkm,cm->rkc", spectrum_real, fine_cos, precision=PRECISE) - jnp.einsum(
        "rkm,cm->rkc", spectrum_imag, fine_sin, precision=PRECISE
    )
    back_imag = jnp.einsum("rkm,cm->rkc", spectrum_real, fine_sin, precision=PRECISE) + jnp.einsum(
        "rkm,cm->rkc", spectrum_imag, fine_cos, precision=PRECISE
    )
    turned_real = back_real * twist_cos - back_imag * twist_sin
    turned_imag = back_real * twist_sin + back_imag * twist_cos
    total = 2 * coarse_cos.shape[0] * twist_cos.shape[1]
    signal = jnp.einsum("rkc,pk->rpc", turned_real, coarse_cos, precision=PRECISE) - jnp.einsum(
        "rkc,pk->rpc", turned_imag, coarse_sin, precision=PRECISE
    )
    return signal / total


def by_channels(
    tokens,
    offsets,
    norm_gain,
    norm_bias,
    proj_weight,
    proj_bias,
    short_filter,
    short_bias,
    long_kernel,
    skip_bias,
    out_weight,
    out_bias,
    second_gain,
    second_bias,
    up_weight,
    up_bias,
    down_weight,
    down_bias,
    cotangent,
):
    seq_count, tok_count, features = tokens.shape
    parts = lax.axis_size("seq")
    chans = features // parts
    length = parts * tok_count
    tables = fourier_tables(parts, tok_count)
    spectral = (seq_count, chans, 2 * parts, tok_count)
    positions = lax.axis_index("seq") * tok_count + jnp.arange(tok_count, dtype=jnp.int32)
    live = (positions[None, :] >= offsets[:, None]).astype(jnp.float32)[:, :, None]
    hidden = tokens.astype(jnp.float32)
    normed, norm_pull = jax.vjp(layer_norm, hidden, norm_gain, norm_bias)
    normed_low = normed.astype(jnp.bfloat16)
    mixed = (
        jnp.einsum("sti,ij->stj", normed_low, proj_weight, preferred_element_type=jnp.float32)
        + proj_bias
    )
    rim = passed_along(mixed[:, tok_count - 2 :, :], "seq", 1)
    extended = jnp.concatenate([rim, mixed], axis=1)
    filtered = (
        short_filter[:, 0] * extended[:, :tok_count]
        + short_filter[:, 1] * extended[:, 1 : tok_count + 1]
        + short_filter[:, 2] * extended[:, 2:]
        + short_bias
    )
    outer_gate = filtered[:, :, :features]
    inner_gate = filtered[:, :, features : 2 * features]
    values = filtered[:, :, 2 * features :]
    gated = values * inner_gate * live
    gated_chan, kernel_chan = (
        lax.all_to_all(jnp.swapaxes(gated, 1, 2), "seq", split_axis=1, concat_axis=2, tiled=True),
        lax.all_to_all(long_kernel[None], "seq", split_axis=1, concat_axis=2, tiled=True),
    )
    gated_real, gated_imag = forward_transform(
        gated_chan.reshape(seq_count * chans, parts, tok_count), tables
    )
    gated_real = gated_real.reshape(spectral)
    gated_imag = gated_imag.reshape(spectral)
    kernel_real, kernel_imag = forward_transform(
        kernel_chan.reshape(chans, parts, tok_count), tables
    )
    prod_real = gated_real * kernel_real - gated_imag * kernel_imag
    prod_imag = gated_real * kernel_imag + gated_imag * kernel_real
    conv_chan = inverse_transform(
        prod_real.reshape(-1, 2 * parts, tok_count),
        prod_imag.reshape(-1, 2 * parts, tok_count),
        tables,
    )
    conv_chan = conv_chan.reshape(seq_count, chans, length)
    conv_tokens = jnp.swapaxes(
        lax.all_to_all(conv_chan, "seq", split_axis=2, concat_axis=1, tiled=True), 1, 2
    )
    convolved = conv_tokens + gated * skip_bias
    branch = convolved * outer_gate
    branch_low = branch.astype(jnp.bfloat16)
    residual = (
        hidden
        + jnp.einsum("sti,ij->stj", branch_low, out_weight, preferred_element_type=jnp.float32)
        + out_bias
    )
    normed_two, second_pull = jax.vjp(layer_norm, residual, second_gain, second_bias)
    normed_two_low = normed_two.astype(jnp.bfloat16)
    expanded = (
        jnp.einsum("sti,ij->stj", normed_two_low, up_weight, preferred_element_type=jnp.float32)
        + up_bias
    )
    activated, gelu_pull = jax.vjp(jax.nn.gelu, expanded)
    activated_low = activated.astype(jnp.bfloat16)
    output = (
        residual
        + jnp.einsum("sti,ij->stj", activated_low, down_weight, preferred_element_type=jnp.float32)
        + down_bias
    )
    upstream = cotangent.astype(jnp.float32)
    down_grad = jnp.einsum(
        "sti,stj->ij", activated_low, cotangent, preferred_element_type=jnp.float32
    )
    down_bias_grad = jnp.sum(upstream, axis=(0, 1))
    act_grad = jnp.einsum("stj,ij->sti", cotangent, down_weight, preferred_element_type=jnp.float32)
    (expanded_grad,) = gelu_pull(act_grad)
    expanded_low = expanded_grad.astype(jnp.bfloat16)
    up_grad = jnp.einsum(
        "sti,stj->ij", normed_two_low, expanded_low, preferred_element_type=jnp.float32
    )
    up_bias_grad = jnp.sum(expanded_low.astype(jnp.float32), axis=(0, 1))
    normed_two_grad = jnp.einsum(
        "stj,ij->sti", expanded_low, up_weight, preferred_element_type=jnp.float32
    )
    residual_part, second_gain_grad, second_bias_grad = second_pull(normed_two_grad)
    residual_grad = upstream + residual_part
    residual_low = residual_grad.astype(jnp.bfloat16)
    out_grad = jnp.einsum(
        "sti,stj->ij", branch_low, residual_low, preferred_element_type=jnp.float32
    )
    out_bias_grad = jnp.sum(residual_low.astype(jnp.float32), axis=(0, 1))
    branch_grad = jnp.einsum(
        "stj,ij->sti", residual_low, out_weight, preferred_element_type=jnp.float32
    )
    conv_grad = branch_grad * outer_gate
    outer_grad = branch_grad * convolved
    skip_bias_grad = jnp.sum(conv_grad * gated, axis=(0, 1))
    conv_grad_chan = lax.all_to_all(
        jnp.swapaxes(conv_grad, 1, 2), "seq", split_axis=1, concat_axis=2, tiled=True
    )
    grad_real, grad_imag = forward_transform(
        conv_grad_chan.reshape(seq_count * chans, parts, tok_count), tables
    )
    grad_real = grad_real.reshape(spectral)
    grad_imag = grad_imag.reshape(spectral)
    back_real = kernel_real * grad_real + kernel_imag * grad_imag
    back_imag = kernel_real * grad_imag - kernel_imag * grad_real
    gated_back_chan = inverse_transform(
        back_real.reshape(-1, 2 * parts, tok_count),
        back_imag.reshape(-1, 2 * parts, tok_count),
        tables,
    )
    gated_back_chan = gated_back_chan.reshape(seq_count, chans, length)
    tap_real = jnp.sum(gated_real * grad_real + gated_imag * grad_imag, axis=0)
    tap_imag = jnp.sum(gated_real * grad_imag - gated_imag * grad_real, axis=0)
    kernel_grad = inverse_transform(tap_real, tap_imag, tables).reshape(chans, length)
    gated_back = jnp.swapaxes(
        lax.all_to_all(gated_back_chan, "seq", split_axis=2, concat_axis=1, tiled=True), 1, 2
    )
    gated_grad = (gated_back + conv_grad * skip_bias) * live
    value_grad = gated_grad * inner_gate
    inner_grad = gated_grad * values
    filtered_grad = jnp.concatenate([outer_grad, inner_grad, value_grad], axis=2)
    following = passed_along(filtered_grad[:, :2, :], "seq", -1)
    grad_extended = jnp.concatenate([filtered_grad, following], axis=1)
    mixed_grad = (
        short_filter[:, 2] * grad_extended[:, :tok_count]
        + short_filter[:, 1] * grad_extended[:, 1 : tok_count + 1]
        + short_filter[:, 0] * grad_extended[:, 2:]
    )
    filter_grad = jnp.stack(
        [
            jnp.sum(filtered_grad * extended[:, position : position + tok_count], axis=(0, 1))
            for position in range(3)
        ],
        axis=1,
    )
    short_bias_grad = jnp.sum(filtered_grad, axis=(0, 1))
    mixed_low = mixed_grad.astype(jnp.bfloat16)
    proj_grad = jnp.einsum("sti,stj->ij", normed_low, mixed_low, preferred_element_type=jnp.float32)
    proj_bias_grad = jnp.sum(mixed_low.astype(jnp.float32), axis=(0, 1))
    normed_grad = jnp.einsum(
        "stj,ij->sti", mixed_low, proj_weight, preferred_element_type=jnp.float32
    )
    hidden_part, norm_gain_grad, norm_bias_grad = norm_pull(normed_grad)
    input_grad = residual_grad + hidden_part
    (
        norm_gain_share,
        norm_bias_share,
        proj_share,
        proj_bias_share,
        filter_share,
        short_bias_share,
        skip_share,
        out_share,
        out_bias_share,
        second_gain_share,
        second_bias_share,
        up_share,
        up_bias_share,
        down_share,
        down_bias_share,
    ) = (
        lax.psum_scatter(norm_gain_grad, "seq", scatter_dimension=0, tiled=True),
        lax.psum_scatter(norm_bias_grad, "seq", scatter_dimension=0, tiled=True),
        lax.psum_scatter(proj_grad, "seq", scatter_dimension=0, tiled=True),
        lax.psum_scatter(proj_bias_grad, "seq", scatter_dimension=0, tiled=True),
        lax.psum_scatter(filter_grad, "seq", scatter_dimension=0, tiled=True),
        lax.psum_scatter(short_bias_grad, "seq", scatter_dimension=0, tiled=True),
        lax.psum_scatter(skip_bias_grad, "seq", scatter_dimension=0, tiled=True),
        lax.psum_scatter(out_grad, "seq", scatter_dimension=0, tiled=True),
        lax.psum_scatter(out_bias_grad, "seq", scatter_dimension=0, tiled=True),
        lax.psum_scatter(second_gain_grad, "seq", scatter_dimension=0, tiled=True),
        lax.psum_scatter(second_bias_grad, "seq", scatter_dimension=0, tiled=True),
        lax.psum_scatter(up_grad, "seq", scatter_dimension=0, tiled=True),
        lax.psum_scatter(up_bias_grad, "seq", scatter_dimension=0, tiled=True),
        lax.psum_scatter(down_grad, "seq", scatter_dimension=0, tiled=True),
        lax.psum_scatter(down_bias_grad, "seq", scatter_dimension=0, tiled=True),
    )
    (
        norm_gain_grad,
        norm_bias_grad,
        proj_grad,
        proj_bias_grad,
        filter_grad,
        short_bias_grad,
        skip_bias_grad,
        out_grad,
        out_bias_grad,
        second_gain_grad,
        second_bias_grad,
        up_grad,
        up_bias_grad,
        down_grad,
        down_bias_grad,
        kernel_grad,
    ) = lax.psum(
        (
            norm_gain_share,
            norm_bias_share,
            proj_share,
            proj_bias_share,
            filter_share,
            short_bias_share,
            skip_share,
            out_share,
            out_bias_share,
            second_gain_share,
            second_bias_share,
            up_share,
            up_bias_share,
            down_share,
            down_bias_share,
            kernel_grad,
        ),
        "dp",
    )
    return (
        output,
        input_grad,
        norm_gain_grad,
        norm_bias_grad,
        proj_grad,
        proj_bias_grad,
        filter_grad,
        short_bias_grad,
        kernel_grad,
        skip_bias_grad,
        out_grad,
        out_bias_grad,
        second_gain_grad,
        second_bias_grad,
        up_grad,
        up_bias_grad,
        down_grad,
        down_bias_grad,
    )


def block_tables(width):
    def stacked(matrix):
        high = matrix.astype(np.float32).astype(ml_dtypes.bfloat16)
        low = (matrix - high.astype(np.float64)).astype(ml_dtypes.bfloat16)
        return np.concatenate([high, high, low], axis=1)

    odd = 2 * np.arange(width) + 1
    angles = np.pi / (2 * width) * (odd[:, None] * np.arange(width)[None, :] % (4 * width))
    analysis = np.concatenate([np.cos(angles), -np.sin(angles)], axis=0)
    angles = np.pi / (2 * width) * (np.arange(2 * width)[:, None] * odd[None, :] % (4 * width))
    synthesis = np.concatenate([np.cos(angles), -np.sin(angles)], axis=1) / width
    return stacked(analysis), stacked(synthesis)


def in_parts(values):
    high = values.astype(jnp.bfloat16)
    low = (values - high.astype(jnp.float32)).astype(jnp.bfloat16)
    return high, low


def earlier(values, by):
    rows = lax.broadcasted_iota(jnp.int32, values.shape, 0)
    return jnp.where(rows >= by, pltpu.roll(values, by, 0), 0.0)


def later(values, by):
    count = values.shape[0]
    rows = lax.broadcasted_iota(jnp.int32, values.shape, 0)
    return jnp.where(rows < count - by, pltpu.roll(values, count - by, 0), 0.0)


def short_filtered(mixed, taps):
    return (
        taps[0:1] * earlier(mixed, 2) + taps[1:2] * earlier(mixed, 1) + taps[2:3] * mixed + taps[3:4]
    )


def analyse(signal, table_ref, spectra_ref):
    blocks, double, lanes = spectra_ref.shape
    width = double // 2
    high, low = in_parts(signal)
    for first in range(0, blocks, 2):
        columns = []
        for block in (first, first + 1):
            rows = slice(block * width, (block + 1) * width)
            columns.append(jnp.concatenate([high[rows], low[rows], high[rows]], axis=0))
        found = jnp.dot(
            table_ref[...], jnp.concatenate(columns, axis=1), preferred_element_type=jnp.float32
        )
        spectra_ref[first] = found[:, :lanes]
        spectra_ref[first + 1] = found[:, lanes:]


def analyse_kernel(kernel_ref, table_ref, spectra_ref):
    blocks, double, lanes = spectra_ref.shape
    for first in range(0, blocks, 2):
        rows = []
        for block in (first, first + 1):
            high, low = in_parts(kernel_ref[block])
            rows.append(jnp.concatenate([high, low, high], axis=1))
        found = lax.dot_general(
            table_ref[...],
            jnp.concatenate(rows, axis=0),
            (((1,), (1,)), ((), ())),
            preferred_element_type=jnp.float32,
        )
        spectra_ref[first] = found[:, :lanes]
        spectra_ref[first + 1] = found[:, lanes:]


def synthesise(spectra_ref, table_ref):
    blocks, double, lanes = spectra_ref.shape
    found = []
    for first in range(0, blocks, 2):
        columns = []
        for block in (first, first + 1):
            high, low = in_parts(spectra_ref[block])
            columns.append(jnp.concatenate([high, low, high], axis=0))
        pair = jnp.dot(
            table_ref[...], jnp.concatenate(columns, axis=1), preferred_element_type=jnp.float32
        )
        found.append(pair[:, :lanes])
        found.append(pair[:, lanes:])
    return found


def multiply(left_ref, right_ref, out_ref, reverse):
    blocks, double, lanes = out_ref.shape
    width = double // 2

    def step(index, carry):
        real_rows = pl.ds(pl.multiple_of(index * 8, 8), 8)
        imag_rows = pl.ds(pl.multiple_of(width + index * 8, 8), 8)
        left_real = [left_ref[block, real_rows] for block in range(blocks)]
        left_imag = [left_ref[block, imag_rows] for block in range(blocks)]
        right_real = [right_ref[block, real_rows] for block in range(blocks)]
        right_imag = [right_ref[block, imag_rows] for block in range(blocks)]
        for m in range(blocks):
            real = imag = None
            for l in range(blocks - m if reverse else m + 1):
                r = m + l if reverse else m - l
                if reverse:
                    new_real = left_real[l] * right_real[r] + left_imag[l] * right_imag[r]
                    new_imag = left_real[l] * right_imag[r] - left_imag[l] * right_real[r]
                else:
                    new_real = left_real[l] * right_real[r] - left_imag[l] * right_imag[r]
                    new_imag = left_real[l] * right_imag[r] + left_imag[l] * right_real[r]
                real = new_real if real is None else real + new_real
                imag = new_imag if imag is None else imag + new_imag
            out_ref[m, real_rows] = real
            out_ref[m, imag_rows] = imag
        return carry

    lax.fori_loop(0, width // 8, step, 0)


def gates(start_ref, mixed_refs, taps_ref):
    outer, inner, values = [
        short_filtered(ref[...], taps_ref[group]) for group, ref in enumerate(mixed_refs)
    ]
    rows = lax.broadcasted_iota(jnp.int32, outer.shape, 0)
    live = (rows >= start_ref[0]).astype(jnp.float32)
    return outer, inner, values, live


def forward_kernel(
    start_ref,
    outer_ref,
    inner_ref,
    value_ref,
    kernel_ref,
    taps_ref,
    skip_ref,
    analysis_ref,
    synthesis_ref,
    convolved_ref,
    branch_ref,
    signal_spectra,
    kernel_spectra,
    spectra,
):
    width = kernel_ref.shape[2]
    outer, inner, values, live = gates(start_ref, (outer_ref, inner_ref, value_ref), taps_ref)
    gated = values * inner * live
    analyse(gated, analysis_ref, signal_spectra)
    analyse_kernel(kernel_ref, analysis_ref, kernel_spectra)
    multiply(kernel_spectra, signal_spectra, spectra, False)
    found = synthesise(spectra, synthesis_ref)
    pieces = [found[0][:width]]
    for block in range(1, len(found)):
        pieces.append(found[block][:width] + found[block - 1][width:])
    convolved = jnp.concatenate(pieces, axis=0) + gated * skip_ref[...]
    convolved_ref[...] = convolved
    branch_ref[...] = (convolved * outer).astype(jnp.bfloat16)


def lag_blocks(found, width):
    pieces = []
    for block in range(len(found)):
        piece = found[block][:width]
        if block + 1 < len(found):
            piece = piece - found[block + 1][width:]
        pieces.append(piece)
    return pieces


def backward_kernel(
    start_ref,
    grad_ref,
    convolved_ref,
    outer_ref,
    inner_ref,
    value_ref,
    kernel_ref,
    taps_ref,
    skip_ref,
    analysis_ref,
    synthesis_ref,
    mixed_grad_ref,
    kernel_kept_ref,
    kernel_given_ref,
    sums_ref,
    signal_spectra,
    kernel_spectra,
    grad_spectra,
    spectra,
):
    width = kernel_ref.shape[2]
    mixed_refs = (outer_ref, inner_ref, value_ref)
    outer, inner, values, live = gates(start_ref, mixed_refs, taps_ref)
    gated = values * inner * live
    branch_grad = grad_ref[...]
    conv_grad = branch_grad * outer
    outer_grad = branch_grad * convolved_ref[...]
    analyse(gated, analysis_ref, signal_spectra)
    analyse_kernel(kernel_ref, analysis_ref, kernel_spectra)
    analyse(conv_grad, analysis_ref, grad_spectra)
    multiply(signal_spectra, grad_spectra, spectra, True)
    lags = lag_blocks(synthesise(spectra, synthesis_ref), width)
    half = len(lags) // 2
    first = start_ref[1] == 0
    for block in range(half):
        columns = slice(block * width, (block + 1) * width)
        one, two = lags[block].T, lags[half + block].T
        kernel_kept_ref[:, columns] = jnp.where(first, one, two)
        kernel_given_ref[:, columns] = jnp.where(first, two, one)
    multiply(kernel_spectra, grad_spectra, spectra, True)
    back = jnp.concatenate(lag_blocks(synthesise(spectra, synthesis_ref), width), axis=0)
    gated_grad = (back + conv_grad * skip_ref[...]) * live

    def total(array):
        return jnp.sum(array, axis=0, keepdims=True)

    filter_rows, bias_rows, low_rows = [], [], []
    grads = (outer_grad, gated_grad * values, gated_grad * inner)
    for group in range(3):
        grad, mixed, taps = grads[group], mixed_refs[group][...], taps_ref[group]
        next_one, next_two = later(grad, 1), later(grad, 2)
        mixed_grad = taps[2:3] * grad + taps[1:2] * next_one + taps[0:1] * next_two
        low = mixed_grad.astype(jnp.bfloat16)
        mixed_grad_ref[group] = low
        filter_rows.append([total(next_two * mixed), total(next_one * mixed), total(grad * mixed)])
        bias_rows.append(total(grad))
        low_rows.append(total(low.astype(jnp.float32)))
    rows = [filter_rows[group][tap] for tap in range(3) for group in range(3)]
    rows = rows + bias_rows + low_rows + [total(conv_grad * gated)]
    sums_ref[...] = jnp.concatenate(rows, axis=0)


def kernel_parameters():
    return pltpu.CompilerParams(
        vmem_limit_bytes=56 * 1024 * 1024
    )


def kernel_specs(tokens, parts, width, lanes, features):
    groups = features // lanes

    def mixed(group):
        return pl.BlockSpec((tokens, lanes), lambda tile, *_: (0, group * groups + tile))

    return (
        [pl.BlockSpec(memory_space=pltpu.SMEM)],
        [mixed(0), mixed(1), mixed(2)],
        [
            pl.BlockSpec((parts, lanes, width), lambda tile, *_: (0, tile, 0)),
            pl.BlockSpec((3, 4, lanes), lambda tile, *_: (0, 0, tile)),
            pl.BlockSpec((1, lanes), lambda tile, *_: (0, tile)),
            pl.BlockSpec((2 * width, 3 * width), lambda *_: (0, 0)),
            pl.BlockSpec((2 * width, 6 * width), lambda *_: (0, 0)),
        ],
        pl.BlockSpec((tokens, lanes), lambda tile, *_: (0, tile)),
        pltpu.VMEM((parts, 2 * width, lanes), jnp.float32),
    )


def forward_convolution(start, mixed, kernel, taps, skip, tables, lanes=128):
    parts, features, width = kernel.shape
    tokens = mixed.shape[0]
    start_spec, mixed_specs, rest, plain, spectra = kernel_specs(tokens, parts, width, lanes, features)
    return pl.pallas_call(
        forward_kernel,
        grid=(features // lanes,),
        in_specs=start_spec + mixed_specs + rest,
        out_specs=(plain, plain),
        out_shape=(
            jax.ShapeDtypeStruct((tokens, features), jnp.float32),
            jax.ShapeDtypeStruct((tokens, features), jnp.bfloat16),
        ),
        scratch_shapes=[spectra] * 3,
        compiler_params=kernel_parameters(),
        cost_estimate=NO_COST,
        name="forward_convolution",
    )(start, mixed, mixed, mixed, kernel, taps, skip, *tables)


def backward_convolution(start, grad, convolved, mixed, kernel, taps, skip, tables, lanes=128):
    parts, features, width = kernel.shape
    tokens = mixed.shape[0]
    start_spec, mixed_specs, rest, plain, spectra = kernel_specs(tokens, parts, width, lanes, features)
    return pl.pallas_call(
        backward_kernel,
        grid=(features // lanes,),
        in_specs=start_spec + [plain, plain] + mixed_specs + rest,
        out_specs=(
            pl.BlockSpec((3, tokens, lanes), lambda tile: (0, 0, tile)),
            pl.BlockSpec((lanes, tokens // 2), lambda tile: (tile, 0)),
            pl.BlockSpec((lanes, tokens // 2), lambda tile: (tile, 0)),
            pl.BlockSpec((16, lanes), lambda tile: (0, tile)),
        ),
        out_shape=(
            jax.ShapeDtypeStruct((3, tokens, features), jnp.bfloat16),
            jax.ShapeDtypeStruct((features, tokens // 2), jnp.float32),
            jax.ShapeDtypeStruct((features, tokens // 2), jnp.float32),
            jax.ShapeDtypeStruct((16, features), jnp.float32),
        ),
        scratch_shapes=[spectra] * 4,
        compiler_params=kernel_parameters(),
        cost_estimate=NO_COST,
        name="backward_convolution",
    )(start, grad, convolved, mixed, mixed, mixed, kernel, taps, skip, *tables)


def unit_rows(values):
    centered = values - jnp.mean(values, axis=-1, keepdims=True)
    spread = lax.rsqrt(jnp.mean(centered * centered, axis=-1, keepdims=True) + EPSILON)
    return centered * spread, spread


def unit_rows_back(grad, unit, spread, gain):
    scaled = grad * gain
    inner = scaled - jnp.mean(scaled, axis=-1, keepdims=True)
    return (inner - unit * jnp.mean(scaled * unit, axis=-1, keepdims=True)) * spread


def matmul(left, right):
    return jnp.dot(left, right, preferred_element_type=jnp.float32)


def matmul_back(left, right):
    return lax.dot_general(left, right, (((1,), (1,)), ((), ())), preferred_element_type=jnp.float32)


def columns_of(array, refs):
    first = 0
    for ref in refs:
        ref[...] = array[:, first : first + ref.shape[1]]
        first += ref.shape[1]


def column_sums(array):
    return jnp.sum(array, axis=0, keepdims=True)


def project_kernel(x_ref, gain_ref, bias_ref, weight_ref, offset_ref, normed_ref, mixed_ref):
    unit, _ = unit_rows(x_ref[...])
    normed = (unit * gain_ref[...] + bias_ref[...]).astype(jnp.bfloat16)
    normed_ref[...] = normed
    mixed_ref[...] = matmul(normed, weight_ref[...]) + offset_ref[...]


def feed_kernel(
    x_ref,
    branch_ref,
    out_weight_ref,
    out_bias_ref,
    gain_ref,
    bias_ref,
    up_weight_ref,
    up_bias_ref,
    down_weight_ref,
    down_bias_ref,
    residual_ref,
    normed_ref,
    activated_ref,
    slope_ref,
    *output_refs,
):
    residual = x_ref[...] + matmul(branch_ref[...], out_weight_ref[...]) + out_bias_ref[...]
    residual_ref[...] = residual
    unit, _ = unit_rows(residual)
    normed = (unit * gain_ref[...] + bias_ref[...]).astype(jnp.bfloat16)
    normed_ref[...] = normed
    total = residual + down_bias_ref[...]
    factor = math.sqrt(2.0 / math.pi)
    chunk = residual.shape[1]
    for first in range(0, up_weight_ref.shape[1], chunk):
        columns = slice(first, first + chunk)
        expanded = matmul(normed, up_weight_ref[:, columns]) + up_bias_ref[:, columns]
        square = expanded * expanded
        turned = jnp.tanh(factor * (expanded + 0.044715 * (square * expanded)))
        half = 0.5 + 0.5 * turned
        activated = (expanded * half).astype(jnp.bfloat16)
        activated_ref[:, columns] = activated
        slope_ref[:, columns] = half + (0.5 * factor) * expanded * (1.0 - turned * turned) * (
            1.0 + (3 * 0.044715) * square
        )
        total = total + matmul(activated, down_weight_ref[columns, :])
    columns_of(total, output_refs)


def feed_back_kernel(
    grad_ref,
    residual_ref,
    slope_ref,
    gain_ref,
    out_weight_ref,
    up_weight_ref,
    down_weight_ref,
    expanded_ref,
    residual_grad_ref,
    residual_low_ref,
    branch_grad_ref,
    sums_ref,
    wide_sums_ref,
):
    grad = grad_ref[...]
    grad_low = grad.astype(jnp.bfloat16)
    chunk = grad.shape[1]
    normed_grad = None
    wide = []
    for first in range(0, up_weight_ref.shape[1], chunk):
        columns = slice(first, first + chunk)
        expanded = matmul_back(grad_low, down_weight_ref[columns, :]) * slope_ref[:, columns]
        low = expanded.astype(jnp.bfloat16)
        expanded_ref[:, columns] = low
        wide.append(column_sums(low.astype(jnp.float32)))
        part = matmul_back(low, up_weight_ref[:, columns])
        normed_grad = part if normed_grad is None else normed_grad + part
    unit, spread = unit_rows(residual_ref[...])
    residual_grad = grad + unit_rows_back(normed_grad, unit, spread, gain_ref[...])
    residual_grad_ref[...] = residual_grad
    low = residual_grad.astype(jnp.bfloat16)
    residual_low_ref[...] = low
    branch_grad_ref[...] = matmul_back(low, out_weight_ref[...])
    sums = [
        column_sums(normed_grad * unit),
        column_sums(normed_grad),
        column_sums(low.astype(jnp.float32)),
        column_sums(grad),
    ]

    @pl.when(pl.program_id(0) == 0)
    def _():
        sums_ref[...] = jnp.zeros_like(sums_ref)
        wide_sums_ref[...] = jnp.zeros_like(wide_sums_ref)

    sums_ref[...] += jnp.concatenate(sums, axis=0)
    wide_sums_ref[...] += jnp.concatenate(wide, axis=1)


def input_grad_kernel(
    mixed_ref, weight_ref, x_ref, gain_ref, residual_grad_ref, first_ref, second_ref, sums_ref
):
    features = x_ref.shape[1]
    normed_grad = None
    for group in range(3):
        columns = slice(group * features, (group + 1) * features)
        part = matmul_back(mixed_ref[group], weight_ref[:, columns])
        normed_grad = part if normed_grad is None else normed_grad + part
    unit, spread = unit_rows(x_ref[...])
    total = residual_grad_ref[...] + unit_rows_back(normed_grad, unit, spread, gain_ref[...])
    columns_of(total, (first_ref, second_ref))
    sums = jnp.concatenate([column_sums(normed_grad * unit), column_sums(normed_grad)], axis=0)

    @pl.when(pl.program_id(0) == 0)
    def _():
        sums_ref[...] = jnp.zeros_like(sums_ref)

    sums_ref[...] += sums


def by_rows(kernel, name, rows, inputs, outputs, height=256):
    def spec(shape, held):
        if len(shape) == 3:
            return pl.BlockSpec((shape[0], height, shape[2]), lambda step: (0, step, 0))
        if shape[0] == rows and not held:
            return pl.BlockSpec((height, shape[1]), lambda step: (step, 0))
        return pl.BlockSpec(shape, lambda step: (0, 0))

    return pl.pallas_call(
        kernel,
        grid=(rows // height,),
        in_specs=[spec(array.shape, held) for array, held in inputs],
        out_specs=tuple(spec(shape, False) for shape, _ in outputs),
        out_shape=tuple(jax.ShapeDtypeStruct(shape, kind) for shape, kind in outputs),
        compiler_params=kernel_parameters(),
        cost_estimate=NO_COST,
        name=name,
    )(*[array for array, _ in inputs])


def product_kernel(half_ref, left_ref, right_ref, out_ref):
    out_ref[...] = product_tile(left_ref, right_ref)


def product_tile(left_ref, right_ref):
    if len(right_ref.shape) == 2:
        return product(left_ref[...], right_ref[...].astype(jnp.bfloat16))
    return jnp.concatenate(
        [product(left_ref[...], right_ref[group]) for group in range(right_ref.shape[0])], axis=1
    )


def product_specs(left, right, tile):
    tokens = left.shape[0]
    half = right.shape[-1] // 2
    left_spec = pl.BlockSpec((tokens, tile), lambda step, half_ref: (0, step))
    if right.ndim == 2:
        right_spec = pl.BlockSpec((tokens, half), lambda step, half_ref: (0, half_ref[0]))
        return half, left_spec, right_spec
    right_spec = pl.BlockSpec((right.shape[0], tokens, half), lambda step, half_ref: (0, 0, half_ref[0]))
    return half * right.shape[0], left_spec, right_spec


def half_product(left, right, half, tile=384):
    rows = left.shape[1]
    columns, left_spec, right_spec = product_specs(left, right, tile)
    return pl.pallas_call(
        product_kernel,
        grid_spec=pltpu.PrefetchScalarGridSpec(
            num_scalar_prefetch=1,
            grid=(rows // tile,),
            in_specs=[left_spec, right_spec],
            out_specs=pl.BlockSpec((tile, columns), lambda step, half_ref: (step, 0)),
        ),
        out_shape=jax.ShapeDtypeStruct((rows, columns), jnp.float32),
        compiler_params=kernel_parameters(),
        cost_estimate=NO_COST,
        name="half_product",
    )(half, left, right)


def parted_product_kernel(bits_ref, left_ref, right_ref, taken_ref, kept_ref, given_ref):
    total = product_tile(left_ref, right_ref) + taken_ref[...]
    pieces, rows, _ = kept_ref.shape
    first = bits_ref[1] == 0
    for piece in range(pieces):
        one = total[2 * piece * rows : (2 * piece + 1) * rows]
        two = total[(2 * piece + 1) * rows : (2 * piece + 2) * rows]
        kept_ref[piece] = jnp.where(first, one, two)
        given_ref[piece] = jnp.where(first, two, one)


def parted_product(left, right, half, taken, which, pieces, tile=384):
    rows = left.shape[1]
    columns, left_spec, right_spec = product_specs(left, right, tile)
    height = rows // (2 * pieces)
    steps = rows // tile
    part = pl.BlockSpec((pieces // steps, height, columns), lambda step, bits_ref: (step, 0, 0))
    shape = jax.ShapeDtypeStruct((pieces, height, columns), jnp.float32)
    return pl.pallas_call(
        parted_product_kernel,
        grid_spec=pltpu.PrefetchScalarGridSpec(
            num_scalar_prefetch=1,
            grid=(steps,),
            in_specs=[
                left_spec,
                right_spec,
                pl.BlockSpec((tile, columns), lambda step, bits_ref: (step, 0)),
            ],
            out_specs=(part, part),
        ),
        out_shape=(shape, shape),
        compiler_params=kernel_parameters(),
        cost_estimate=NO_COST,
        name="parted_product",
    )(jnp.concatenate([half, which]), left, right, taken)


def fold_kernel(bit_ref, *refs):
    *sources, kept_ref, given_ref = refs
    first = bit_ref[0] == 0
    height, lane = kept_ref.shape[1], 0
    for kept, taken in zip(sources[::2], sources[1::2]):
        total = kept[...] + taken[...]
        for row in range(0, total.shape[1], height):
            columns = slice(lane, lane + total.shape[2])
            one, two = total[0, row : row + height], total[1, row : row + height]
            kept_ref[0, :, columns] = jnp.where(first, one, two)
            given_ref[0, :, columns] = jnp.where(first, two, one)
            lane += total.shape[2]


def fold(pairs, which, height):
    count = pairs[0][0].shape[0]
    operands = [array for pair in pairs for array in pair]
    columns = sum(kept.shape[1] // height * kept.shape[2] for kept, _ in pairs)
    one = pl.BlockSpec((1, height, columns), lambda step: (step, 0, 0))
    shape = jax.ShapeDtypeStruct((count // 2, height, columns), jnp.float32)
    return pl.pallas_call(
        fold_kernel,
        grid=(count // 2,),
        in_specs=[pl.BlockSpec(memory_space=pltpu.SMEM)]
        + [pl.BlockSpec((2,) + array.shape[1:], lambda step: (step, 0, 0)) for array in operands],
        out_specs=(one, one),
        out_shape=(shape, shape),
        compiler_params=kernel_parameters(),
        cost_estimate=NO_COST,
        name="fold",
    )(which, *operands)


def unpack_kernel(bits_ref, own_ref, y_ref, core_ref, both_ref, *out_refs):
    core_first, y_first = bits_ref[0] == 0, bits_ref[1] == 0
    own, beside = own_ref[...], y_ref[...]
    mine = [jnp.where(y_first, own, beside), jnp.where(y_first, beside, own)]
    own, beside = core_ref[...], both_ref[...]
    theirs = [jnp.where(y_first, own, beside), jnp.where(y_first, beside, own)]
    height = own.shape[0]
    for y in range(2):
        for core in range(2):
            block = jnp.where(core_first, mine[y], theirs[y])
            if core == 1:
                block = jnp.where(core_first, theirs[y], mine[y])
            lane = 0
            for ref in out_refs:
                rows, columns = ref.shape
                if columns == 128:
                    ref[(2 * core + y) * height : (2 * core + y + 1) * height] = block[:, lane:]
                    continue
                groups = 3 if columns == 3 * height * 16 and rows == 2 * height else 1
                half = columns // (2 * groups)
                for place in range(rows // (2 * height)):
                    for group in range(groups):
                        top = y * (rows // 2) + place * height
                        left = group * 2 * half + core * half
                        ref[top : top + height, left : left + half] = block[:, lane : lane + half]
                        lane += half


def gathered(share):
    y_other, core_other = swapped(share, "dp", 2), swapped(share, "dp", 1)
    return share, y_other, core_other, swapped(y_other, "dp", 1)


def unpacked(shares, shapes):
    return pl.pallas_call(
        unpack_kernel,
        in_specs=[pl.BlockSpec(memory_space=pltpu.SMEM)] + [pl.BlockSpec(memory_space=pltpu.VMEM)] * 4,
        out_specs=[pl.BlockSpec(memory_space=pltpu.VMEM)] * len(shapes),
        out_shape=[jax.ShapeDtypeStruct(shape, jnp.float32) for shape in shapes],
        compiler_params=kernel_parameters(),
        cost_estimate=NO_COST,
        name="unpack",
    )(jnp.concatenate([flag("dp", 1), flag("dp", 2)]), *shares)


def swapped(array, axis, by):
    count = lax.axis_size(axis)
    return lax.ppermute(array, axis, [(i, i ^ by) for i in range(count)])


def bit(axis, by):
    return (lax.axis_index(axis) // by) % 2


def doubled(array, dim, axis, by):
    other = swapped(array, axis, by)
    first = bit(axis, by) == 0
    return jnp.concatenate(
        [jnp.where(first, array, other), jnp.where(first, other, array)], axis=dim
    )


def product(left, columns):
    return lax.dot_general(left, columns, (((0,), (0,)), ((), ())), preferred_element_type=jnp.float32)


def flag(axis, by):
    return bit(axis, by).astype(jnp.int32).reshape(1)


def reduced(kept, given, steps):
    for (axis, by), following in zip(steps, steps[1:] + [None]):
        taken = swapped(given, axis, by)
        if following is None:
            return (kept + taken)[0]
        kept, given = fold([(kept, taken)], flag(*following), kept.shape[1])


def by_sequences(
    tokens,
    offsets,
    norm_gain,
    norm_bias,
    proj_weight,
    proj_bias,
    short_filter,
    short_bias,
    long_kernel,
    skip_bias,
    out_weight,
    out_bias,
    second_gain,
    second_bias,
    up_weight,
    up_bias,
    down_weight,
    down_bias,
    cotangent,
):
    parts, width, features = tokens.shape
    length = parts * width
    hidden_units = up_weight.shape[1]
    hold = lax.optimization_barrier
    tables = tuple(jnp.asarray(table) for table in block_tables(width))
    start = lax.dynamic_slice_in_dim(offsets, lax.axis_index("seq"), 1, 0)
    core, other_core = flag("dp", 1), 1 - flag("dp", 1)
    scalars = jnp.concatenate([start, core])
    low, single = jnp.bfloat16, jnp.float32
    y_step, x_step = ("dp", 2), ("seq", 1)
    z_steps = [("seq", 1 << place) for place in range(1, parts.bit_length() - 1)]

    share = features // 4
    chunk = bit("dp", 1) * 2 + bit("dp", 2)
    piece = lax.dynamic_slice_in_dim(long_kernel, chunk * share, share, 0)
    pieces = jnp.stack([piece] + [swapped(piece, "seq", by) for by in range(2, parts, 2)])
    z = lax.axis_index("seq") // 2
    pieces = jnp.concatenate(
        [lax.dynamic_index_in_dim(pieces, z ^ other, 0) for other in range(parts // 2)]
    )
    hidden, pieces = hold((tokens.astype(single), pieces))
    hidden = lax.all_to_all(hidden, "seq", 0, 0, tiled=True)
    pieces = doubled(pieces[:, None], 1, *x_step).reshape(parts, share, width)
    kernel = doubled(doubled(pieces, 1, "dp", 2), 1, "dp", 1)
    upstream = cotangent.astype(single)
    taps = jnp.concatenate([short_filter.T, short_bias[None]], axis=0)
    taps = jnp.swapaxes(taps.reshape(4, 3, features), 0, 1)
    skip = skip_bias[None]
    hidden, kernel, upstream, taps, scalars = hold((hidden, kernel, upstream, taps, scalars))

    upstream = lax.all_to_all(upstream, "seq", 0, 0, tiled=True)
    hidden = hidden.reshape(length, features)
    normed_low, mixed = by_rows(
        project_kernel,
        "project",
        length,
        [
            (hidden, False),
            (norm_gain[None], True),
            (norm_bias[None], True),
            (proj_weight, True),
            (proj_bias[None], True),
        ],
        [((length, features), low), ((length, 3 * features), single)],
    )
    convolved, branch_low = forward_convolution(scalars, mixed, kernel, taps, skip, tables)
    residual, normed_two_low, activated_low, slope, *output = by_rows(
        feed_kernel,
        "feed",
        length,
        [
            (hidden, False),
            (branch_low, False),
            (out_weight, True),
            (out_bias[None], True),
            (second_gain[None], True),
            (second_bias[None], True),
            (up_weight, True),
            (up_bias[None], True),
            (down_weight, True),
            (down_bias[None], True),
        ],
        [
            ((length, features), single),
            ((length, features), low),
            ((length, hidden_units), low),
            ((length, hidden_units), single),
            ((length, features // 2), single),
            ((length, features // 3), single),
            ((length, features // 6), single),
        ],
    )
    upstream, output = hold((upstream, output))

    def sent(columns):
        columns = columns.reshape(parts, width, -1)
        return lax.all_to_all(columns, "seq", 0, 0, tiled=True)

    output[0] = sent(output[0])
    upstream = upstream.reshape(length, features)
    down_given = half_product(activated_low, upstream, other_core, 768)
    upstream, down_given = hold((upstream, down_given))

    down_taken = swapped(down_given, "dp", 1)
    expanded_low, residual_grad, residual_low, branch_grad, sums_two, wide_sums = by_rows(
        feed_back_kernel,
        "feed_back",
        length,
        [
            (upstream, False),
            (residual, False),
            (slope, False),
            (second_gain[None], True),
            (out_weight, True),
            (up_weight, True),
            (down_weight, True),
        ],
        [
            ((length, hidden_units), low),
            ((length, features), single),
            ((length, features), low),
            ((length, features), single),
            ((4, features), single),
            ((1, hidden_units), single),
        ],
    )
    up_given = half_product(normed_two_low, expanded_low, other_core)
    out_given = half_product(branch_low, residual_low, other_core, 768)
    branch_grad, up_given, out_given, down_taken, output = hold(
        (branch_grad, up_given, out_given, down_taken, output)
    )

    output[1] = sent(output[1])
    up_taken = swapped(up_given, "dp", 1)
    out_taken = swapped(out_given, "dp", 1)
    down_kept, down_given = parted_product(
        activated_low, upstream, core, down_taken, flag(*y_step), parts, 768
    )
    up_kept, up_given = parted_product(
        normed_two_low, expanded_low, core, up_taken, flag(*x_step), parts // 2
    )
    out_kept, out_given = parted_product(
        branch_low, residual_low, core, out_taken, flag(*y_step), parts, 768
    )
    branch_grad, down_given, up_given, out_given, output = hold(
        (branch_grad, down_given, up_given, out_given, output)
    )

    output[2] = sent(output[2])
    down_taken = swapped(down_given, *y_step)
    up_taken = swapped(up_given, *x_step)
    mixed_low, kernel_kept, kernel_given, sums = backward_convolution(
        scalars, branch_grad, convolved, mixed, kernel, taps, skip, tables
    )
    proj_given = half_product(normed_low, mixed_low, other_core)
    *input_grad, sums_one = by_rows(
        input_grad_kernel,
        "input_grad",
        length,
        [
            (mixed_low, False),
            (proj_weight, True),
            (hidden, False),
            (norm_gain[None], True),
            (residual_grad, False),
        ],
        [
            ((length, features * 2 // 3), single),
            ((length, features // 3), single),
            ((2, features), single),
        ],
    )
    input_grad, mixed_low, proj_given, kernel_given, down_taken, up_taken, sums_one, sums, output = hold(
        (input_grad, mixed_low, proj_given, kernel_given, down_taken, up_taken, sums_one, sums, output)
    )

    rows = features // (2 * parts)
    input_grad[0] = sent(input_grad[0])
    out_taken = swapped(out_given, *y_step)
    up_kept, up_taken = [array.reshape(parts, rows, -1) for array in (up_kept, up_taken)]
    up_kept, up_given = fold([(up_kept, up_taken)], flag(*y_step), rows)
    up_taken = swapped(up_given, *y_step)
    down_kept, down_given = fold([(down_kept, down_taken)], flag(*x_step), down_kept.shape[1])
    down_taken = swapped(down_given, *x_step)
    kernel_taken = swapped(kernel_given, "dp", 1)
    proj_taken = swapped(proj_given, "dp", 1)
    proj_kept, proj_given = parted_product(
        normed_low, mixed_low, core, proj_taken, flag(*y_step), parts
    )
    output = jnp.concatenate(output, axis=2)
    vectors = [sums_one[0], sums_one[1]]
    vectors += [sums[first : first + 3].reshape(-1) for first in range(0, 15, 3)]
    vectors += [sums[15], sums_two[2], sums_two[0], sums_two[1], wide_sums[0], sums_two[3]]
    sizes = [vector.shape[0] // parts for vector in vectors]
    packed = jnp.concatenate([vector.reshape(parts, -1) for vector in vectors], axis=1)
    packed = jnp.pad(packed, ((0, 0), (0, 4 * rows * 128 - packed.shape[1])))
    packed = packed.reshape(parts, 2, 2 * rows, 128)
    packed_kept = lax.dynamic_index_in_dim(packed, core[0], 1, keepdims=False)
    packed_given = lax.dynamic_index_in_dim(packed, other_core[0], 1, keepdims=False)
    packed_taken = swapped(packed_given, "dp", 1)
    kernel_kept, kernel_taken = [
        array.reshape(parts, 2 * rows, -1) for array in (kernel_kept, kernel_taken)
    ]
    rest_kept, rest_given = fold(
        [(kernel_kept, kernel_taken), (packed_kept, packed_taken)], flag(*x_step), 2 * rows
    )
    input_grad, down_taken, up_taken, out_taken, proj_given, rest_given, output = hold(
        (input_grad, down_taken, up_taken, out_taken, proj_given, rest_given, output)
    )

    input_grad[1] = sent(input_grad[1])
    proj_taken = swapped(proj_given, *y_step)
    rest_taken = swapped(rest_given, *x_step)
    feed_kept, feed_given = fold(
        [(down_kept, down_taken), (up_kept, up_taken)], flag(*z_steps[0]), rows
    )
    feed_taken = swapped(feed_given, *z_steps[0])
    out_kept, out_given = fold([(out_kept, out_taken)], flag(*x_step), rows)
    input_grad, proj_taken, rest_taken, out_given, feed_taken = hold(
        (input_grad, proj_taken, rest_taken, out_given, feed_taken)
    )

    feed_kept, feed_given = fold([(feed_kept, feed_taken)], flag(*z_steps[1]), rows)
    feed_given, proj_taken, rest_taken = hold((feed_given, proj_taken, rest_taken))
    feed_taken = swapped(feed_given, *z_steps[1])
    out_taken = swapped(out_given, *x_step)
    proj_kept, proj_given = fold([(proj_kept, proj_taken)], flag(*x_step), rows)
    proj_taken = swapped(proj_given, *x_step)
    rest_kept, rest_taken = [array.reshape(parts, rows, -1) for array in (rest_kept, rest_taken)]
    rest_kept, rest_given = fold([(rest_kept, rest_taken)], flag(*y_step), rows)
    rest_taken = swapped(rest_given, *y_step)
    input_grad = jnp.concatenate(input_grad, axis=2)
    proj_taken, rest_taken, out_taken, feed_taken, input_grad = hold(
        (proj_taken, rest_taken, out_taken, feed_taken, input_grad)
    )

    mixer_kept, mixer_given = fold(
        [(proj_kept, proj_taken), (out_kept, out_taken), (rest_kept, rest_taken)],
        flag(*z_steps[0]),
        rows,
    )
    mixer_taken = swapped(mixer_given, *z_steps[0])
    feed_share = (feed_kept + feed_taken)[0]
    feed_shares = gathered(feed_share)
    mixer_taken, *feed_shares = hold((mixer_taken, *feed_shares))
    mixer_kept, mixer_given = fold([(mixer_kept, mixer_taken)], flag(*z_steps[1]), rows)
    mixer_taken = swapped(mixer_given, *z_steps[1])
    down_share, up_share = unpacked(
        feed_shares, [(hidden_units // parts, features), (features // parts, hidden_units)]
    )
    mixer_taken, down_share, up_share = hold((mixer_taken, down_share, up_share))
    mixer_share = (mixer_kept + mixer_taken)[0]
    proj_share, out_share, kernel_share, packed = unpacked(
        gathered(mixer_share),
        [
            (features // parts, 3 * features),
            (features // parts, features),
            (features // parts, length),
            (4 * rows, 128),
        ],
    )
    packed = packed.reshape(-1)
    ends = np.cumsum(sizes)
    vectors = [packed[end - size : end] for size, end in zip(sizes, ends)]
    return (
        output,
        input_grad,
        vectors[0],
        vectors[1],
        proj_share,
        vectors[6],
        jnp.stack(vectors[2:5], axis=1),
        vectors[5],
        kernel_share,
        vectors[7],
        out_share,
        vectors[8],
        vectors[9],
        vectors[10],
        up_share,
        vectors[11],
        down_share,
        vectors[12],
    )


def per_device(tokens, offsets, *rest):
    fits = (
        tokens.shape[0] == lax.axis_size("seq")
        and lax.axis_size("dp") == 4
        and tokens.shape[0] % 2 == 0
        and tokens.shape[1] % 128 == 0
        and lax.axis_size("seq") & (lax.axis_size("seq") - 1) == 0
    )
    plan = by_sequences if fits else by_channels
    return plan(tokens, offsets, *rest)


def solution(mesh):
    return jax.shard_map(
        per_device,
        mesh=mesh,
        in_specs=(
            P("dp", "seq", None),
            P("dp"),
            P(),
            P(),
            P(),
            P(),
            P(),
            P(),
            P(None, "seq"),
            P(),
            P(),
            P(),
            P(),
            P(),
            P(),
            P(),
            P(),
            P(),
            P("dp", "seq", None),
        ),
        out_specs=(
            P("dp", "seq", None),
            P("dp", "seq", None),
            P("seq"),
            P("seq"),
            P("seq", None),
            P("seq"),
            P("seq", None),
            P("seq"),
            P("seq", None),
            P("seq"),
            P("seq", None),
            P("seq"),
            P("seq"),
            P("seq"),
            P("seq", None),
            P("seq"),
            P("seq", None),
            P("seq"),
        ),
        check_vma=False,
    )
```

```python
import functools
import math

import jax
import jax.numpy as jnp
import ml_dtypes
import numpy as np
from jax import lax
from jax.experimental import pallas as pl
from jax.experimental.pallas import tpu as pltpu
from jax.sharding import PartitionSpec as P

EPSILON = 1e-05
PRECISE = lax.Precision.HIGHEST
NO_COST = pl.CostEstimate(flops=0, bytes_accessed=0, transcendentals=0)


def passed_along(array, axis, by):
    count = lax.axis_size(axis)
    pairs = [(i, i + by) for i in range(count) if 0 <= i + by < count]
    return lax.ppermute(array, axis, pairs)


def layer_norm(values, gain, offset):
    centered = values - jnp.mean(values, axis=-1, keepdims=True)
    spread = lax.rsqrt(jnp.mean(centered * centered, axis=-1, keepdims=True) + EPSILON)
    return centered * spread * gain + offset


def angle_table(rows, cols, modulus):
    product = (
        jnp.arange(rows, dtype=jnp.int32)[:, None]
        * jnp.arange(cols, dtype=jnp.int32)[None, :]
        % modulus
    )
    angles = product.astype(jnp.float32) * (2.0 * math.pi / modulus)
    return (jnp.cos(angles), jnp.sin(angles))


def fourier_tables(blocks, width):
    coarse_cos, coarse_sin = angle_table(blocks, 2 * blocks, 2 * blocks)
    twist_cos, twist_sin = angle_table(2 * blocks, width, 2 * blocks * width)
    fine_cos, fine_sin = angle_table(width, width, width)
    return (coarse_cos, coarse_sin, twist_cos, twist_sin, fine_cos, fine_sin)


def forward_transform(signal, tables):
    coarse_cos, coarse_sin, twist_cos, twist_sin, fine_cos, fine_sin = tables
    first_real = jnp.einsum("rpc,pk->rkc", signal, coarse_cos, precision=PRECISE)
    first_imag = -jnp.einsum("rpc,pk->rkc", signal, coarse_sin, precision=PRECISE)
    turned_real = first_real * twist_cos + first_imag * twist_sin
    turned_imag = first_imag * twist_cos - first_real * twist_sin
    spectrum_real = jnp.einsum(
        "rkc,cm->rkm", turned_real, fine_cos, precision=PRECISE
    ) + jnp.einsum("rkc,cm->rkm", turned_imag, fine_sin, precision=PRECISE)
    spectrum_imag = jnp.einsum(
        "rkc,cm->rkm", turned_imag, fine_cos, precision=PRECISE
    ) - jnp.einsum("rkc,cm->rkm", turned_real, fine_sin, precision=PRECISE)
    return (spectrum_real, spectrum_imag)


def inverse_transform(spectrum_real, spectrum_imag, tables):
    coarse_cos, coarse_sin, twist_cos, twist_sin, fine_cos, fine_sin = tables
    back_real = jnp.einsum("rkm,cm->rkc", spectrum_real, fine_cos, precision=PRECISE) - jnp.einsum(
        "rkm,cm->rkc", spectrum_imag, fine_sin, precision=PRECISE
    )
    back_imag = jnp.einsum("rkm,cm->rkc", spectrum_real, fine_sin, precision=PRECISE) + jnp.einsum(
        "rkm,cm->rkc", spectrum_imag, fine_cos, precision=PRECISE
    )
    turned_real = back_real * twist_cos - back_imag * twist_sin
    turned_imag = back_real * twist_sin + back_imag * twist_cos
    total = 2 * coarse_cos.shape[0] * twist_cos.shape[1]
    signal = jnp.einsum("rkc,pk->rpc", turned_real, coarse_cos, precision=PRECISE) - jnp.einsum(
        "rkc,pk->rpc", turned_imag, coarse_sin, precision=PRECISE
    )
    return signal / total


def by_channels(
    tokens,
    offsets,
    norm_gain,
    norm_bias,
    proj_weight,
    proj_bias,
    short_filter,
    short_bias,
    long_kernel,
    skip_bias,
    out_weight,
    out_bias,
    second_gain,
    second_bias,
    up_weight,
    up_bias,
    down_weight,
    down_bias,
    cotangent,
):
    seq_count, tok_count, features = tokens.shape
    parts = lax.axis_size("seq")
    chans = features // parts
    length = parts * tok_count
    tables = fourier_tables(parts, tok_count)
    spectral = (seq_count, chans, 2 * parts, tok_count)
    positions = lax.axis_index("seq") * tok_count + jnp.arange(tok_count, dtype=jnp.int32)
    live = (positions[None, :] >= offsets[:, None]).astype(jnp.float32)[:, :, None]
    hidden = tokens.astype(jnp.float32)
    normed, norm_pull = jax.vjp(layer_norm, hidden, norm_gain, norm_bias)
    normed_low = normed.astype(jnp.bfloat16)
    mixed = (
        jnp.einsum("sti,ij->stj", normed_low, proj_weight, preferred_element_type=jnp.float32)
        + proj_bias
    )
    rim = passed_along(mixed[:, tok_count - 2 :, :], "seq", 1)
    extended = jnp.concatenate([rim, mixed], axis=1)
    filtered = (
        short_filter[:, 0] * extended[:, :tok_count]
        + short_filter[:, 1] * extended[:, 1 : tok_count + 1]
        + short_filter[:, 2] * extended[:, 2:]
        + short_bias
    )
    outer_gate = filtered[:, :, :features]
    inner_gate = filtered[:, :, features : 2 * features]
    values = filtered[:, :, 2 * features :]
    gated = values * inner_gate * live
    gated_chan, kernel_chan = (
        lax.all_to_all(jnp.swapaxes(gated, 1, 2), "seq", split_axis=1, concat_axis=2, tiled=True),
        lax.all_to_all(long_kernel[None], "seq", split_axis=1, concat_axis=2, tiled=True),
    )
    gated_real, gated_imag = forward_transform(
        gated_chan.reshape(seq_count * chans, parts, tok_count), tables
    )
    gated_real = gated_real.reshape(spectral)
    gated_imag = gated_imag.reshape(spectral)
    kernel_real, kernel_imag = forward_transform(
        kernel_chan.reshape(chans, parts, tok_count), tables
    )
    prod_real = gated_real * kernel_real - gated_imag * kernel_imag
    prod_imag = gated_real * kernel_imag + gated_imag * kernel_real
    conv_chan = inverse_transform(
        prod_real.reshape(-1, 2 * parts, tok_count),
        prod_imag.reshape(-1, 2 * parts, tok_count),
        tables,
    )
    conv_chan = conv_chan.reshape(seq_count, chans, length)
    conv_tokens = jnp.swapaxes(
        lax.all_to_all(conv_chan, "seq", split_axis=2, concat_axis=1, tiled=True), 1, 2
    )
    convolved = conv_tokens + gated * skip_bias
    branch = convolved * outer_gate
    branch_low = branch.astype(jnp.bfloat16)
    residual = (
        hidden
        + jnp.einsum("sti,ij->stj", branch_low, out_weight, preferred_element_type=jnp.float32)
        + out_bias
    )
    normed_two, second_pull = jax.vjp(layer_norm, residual, second_gain, second_bias)
    normed_two_low = normed_two.astype(jnp.bfloat16)
    expanded = (
        jnp.einsum("sti,ij->stj", normed_two_low, up_weight, preferred_element_type=jnp.float32)
        + up_bias
    )
    activated, gelu_pull = jax.vjp(jax.nn.gelu, expanded)
    activated_low = activated.astype(jnp.bfloat16)
    output = (
        residual
        + jnp.einsum("sti,ij->stj", activated_low, down_weight, preferred_element_type=jnp.float32)
        + down_bias
    )
    upstream = cotangent.astype(jnp.float32)
    down_grad = jnp.einsum(
        "sti,stj->ij", activated_low, cotangent, preferred_element_type=jnp.float32
    )
    down_bias_grad = jnp.sum(upstream, axis=(0, 1))
    act_grad = jnp.einsum("stj,ij->sti", cotangent, down_weight, preferred_element_type=jnp.float32)
    (expanded_grad,) = gelu_pull(act_grad)
    expanded_low = expanded_grad.astype(jnp.bfloat16)
    up_grad = jnp.einsum(
        "sti,stj->ij", normed_two_low, expanded_low, preferred_element_type=jnp.float32
    )
    up_bias_grad = jnp.sum(expanded_low.astype(jnp.float32), axis=(0, 1))
    normed_two_grad = jnp.einsum(
        "stj,ij->sti", expanded_low, up_weight, preferred_element_type=jnp.float32
    )
    residual_part, second_gain_grad, second_bias_grad = second_pull(normed_two_grad)
    residual_grad = upstream + residual_part
    residual_low = residual_grad.astype(jnp.bfloat16)
    out_grad = jnp.einsum(
        "sti,stj->ij", branch_low, residual_low, preferred_element_type=jnp.float32
    )
    out_bias_grad = jnp.sum(residual_low.astype(jnp.float32), axis=(0, 1))
    branch_grad = jnp.einsum(
        "stj,ij->sti", residual_low, out_weight, preferred_element_type=jnp.float32
    )
    conv_grad = branch_grad * outer_gate
    outer_grad = branch_grad * convolved
    skip_bias_grad = jnp.sum(conv_grad * gated, axis=(0, 1))
    conv_grad_chan = lax.all_to_all(
        jnp.swapaxes(conv_grad, 1, 2), "seq", split_axis=1, concat_axis=2, tiled=True
    )
    grad_real, grad_imag = forward_transform(
        conv_grad_chan.reshape(seq_count * chans, parts, tok_count), tables
    )
    grad_real = grad_real.reshape(spectral)
    grad_imag = grad_imag.reshape(spectral)
    back_real = kernel_real * grad_real + kernel_imag * grad_imag
    back_imag = kernel_real * grad_imag - kernel_imag * grad_real
    gated_back_chan = inverse_transform(
        back_real.reshape(-1, 2 * parts, tok_count),
        back_imag.reshape(-1, 2 * parts, tok_count),
        tables,
    )
    gated_back_chan = gated_back_chan.reshape(seq_count, chans, length)
    tap_real = jnp.sum(gated_real * grad_real + gated_imag * grad_imag, axis=0)
    tap_imag = jnp.sum(gated_real * grad_imag - gated_imag * grad_real, axis=0)
    kernel_grad = inverse_transform(tap_real, tap_imag, tables).reshape(chans, length)
    gated_back = jnp.swapaxes(
        lax.all_to_all(gated_back_chan, "seq", split_axis=2, concat_axis=1, tiled=True), 1, 2
    )
    gated_grad = (gated_back + conv_grad * skip_bias) * live
    value_grad = gated_grad * inner_gate
    inner_grad = gated_grad * values
    filtered_grad = jnp.concatenate([outer_grad, inner_grad, value_grad], axis=2)
    following = passed_along(filtered_grad[:, :2, :], "seq", -1)
    grad_extended = jnp.concatenate([filtered_grad, following], axis=1)
    mixed_grad = (
        short_filter[:, 2] * grad_extended[:, :tok_count]
        + short_filter[:, 1] * grad_extended[:, 1 : tok_count + 1]
        + short_filter[:, 0] * grad_extended[:, 2:]
    )
    filter_grad = jnp.stack(
        [
            jnp.sum(filtered_grad * extended[:, position : position + tok_count], axis=(0, 1))
            for position in range(3)
        ],
        axis=1,
    )
    short_bias_grad = jnp.sum(filtered_grad, axis=(0, 1))
    mixed_low = mixed_grad.astype(jnp.bfloat16)
    proj_grad = jnp.einsum("sti,stj->ij", normed_low, mixed_low, preferred_element_type=jnp.float32)
    proj_bias_grad = jnp.sum(mixed_low.astype(jnp.float32), axis=(0, 1))
    normed_grad = jnp.einsum(
        "stj,ij->sti", mixed_low, proj_weight, preferred_element_type=jnp.float32
    )
    hidden_part, norm_gain_grad, norm_bias_grad = norm_pull(normed_grad)
    input_grad = residual_grad + hidden_part
    (
        norm_gain_share,
        norm_bias_share,
        proj_share,
        proj_bias_share,
        filter_share,
        short_bias_share,
        skip_share,
        out_share,
        out_bias_share,
        second_gain_share,
        second_bias_share,
        up_share,
        up_bias_share,
        down_share,
        down_bias_share,
    ) = (
        lax.psum_scatter(norm_gain_grad, "seq", scatter_dimension=0, tiled=True),
        lax.psum_scatter(norm_bias_grad, "seq", scatter_dimension=0, tiled=True),
        lax.psum_scatter(proj_grad, "seq", scatter_dimension=0, tiled=True),
        lax.psum_scatter(proj_bias_grad, "seq", scatter_dimension=0, tiled=True),
        lax.psum_scatter(filter_grad, "seq", scatter_dimension=0, tiled=True),
        lax.psum_scatter(short_bias_grad, "seq", scatter_dimension=0, tiled=True),
        lax.psum_scatter(skip_bias_grad, "seq", scatter_dimension=0, tiled=True),
        lax.psum_scatter(out_grad, "seq", scatter_dimension=0, tiled=True),
        lax.psum_scatter(out_bias_grad, "seq", scatter_dimension=0, tiled=True),
        lax.psum_scatter(second_gain_grad, "seq", scatter_dimension=0, tiled=True),
        lax.psum_scatter(second_bias_grad, "seq", scatter_dimension=0, tiled=True),
        lax.psum_scatter(up_grad, "seq", scatter_dimension=0, tiled=True),
        lax.psum_scatter(up_bias_grad, "seq", scatter_dimension=0, tiled=True),
        lax.psum_scatter(down_grad, "seq", scatter_dimension=0, tiled=True),
        lax.psum_scatter(down_bias_grad, "seq", scatter_dimension=0, tiled=True),
    )
    (
        norm_gain_grad,
        norm_bias_grad,
        proj_grad,
        proj_bias_grad,
        filter_grad,
        short_bias_grad,
        skip_bias_grad,
        out_grad,
        out_bias_grad,
        second_gain_grad,
        second_bias_grad,
        up_grad,
        up_bias_grad,
        down_grad,
        down_bias_grad,
        kernel_grad,
    ) = lax.psum(
        (
            norm_gain_share,
            norm_bias_share,
            proj_share,
            proj_bias_share,
            filter_share,
            short_bias_share,
            skip_share,
            out_share,
            out_bias_share,
            second_gain_share,
            second_bias_share,
            up_share,
            up_bias_share,
            down_share,
            down_bias_share,
            kernel_grad,
        ),
        "dp",
    )
    return (
        output,
        input_grad,
        norm_gain_grad,
        norm_bias_grad,
        proj_grad,
        proj_bias_grad,
        filter_grad,
        short_bias_grad,
        kernel_grad,
        skip_bias_grad,
        out_grad,
        out_bias_grad,
        second_gain_grad,
        second_bias_grad,
        up_grad,
        up_bias_grad,
        down_grad,
        down_bias_grad,
    )


def block_tables(width):
    def stacked(matrix):
        high = matrix.astype(np.float32).astype(ml_dtypes.bfloat16)
        low = (matrix - high.astype(np.float64)).astype(ml_dtypes.bfloat16)
        return np.concatenate([high, high, low], axis=1)

    odd = 2 * np.arange(width) + 1
    angles = np.pi / (2 * width) * (odd[:, None] * np.arange(width)[None, :] % (4 * width))
    analysis = np.concatenate([np.cos(angles), -np.sin(angles)], axis=0)
    angles = np.pi / (2 * width) * (np.arange(2 * width)[:, None] * odd[None, :] % (4 * width))
    synthesis = np.concatenate([np.cos(angles), -np.sin(angles)], axis=1) / width
    return stacked(analysis), stacked(synthesis)


def in_parts(values):
    high = values.astype(jnp.bfloat16)
    low = (values - high.astype(jnp.float32)).astype(jnp.bfloat16)
    return high, low


def short_filtered(padded_ref, mixed_ref, taps):
    count, lanes = mixed_ref.shape
    padded_ref[:8] = jnp.zeros((8, lanes), jnp.float32)
    padded_ref[8 : 8 + count] = mixed_ref[...]
    return (
        taps[0:1] * padded_ref[6 : 6 + count]
        + taps[1:2] * padded_ref[7 : 7 + count]
        + taps[2:3] * mixed_ref[...]
        + taps[3:4]
    )


def analyse(signal, table_ref, spectra_ref):
    blocks, double, lanes = spectra_ref.shape
    width = double // 2
    high, low = in_parts(signal)
    for first in range(0, blocks, 2):
        columns = []
        for block in (first, first + 1):
            rows = slice(block * width, (block + 1) * width)
            columns.append(jnp.concatenate([high[rows], low[rows], high[rows]], axis=0))
        found = jnp.dot(
            table_ref[...], jnp.concatenate(columns, axis=1), preferred_element_type=jnp.float32
        )
        spectra_ref[first] = found[:, :lanes]
        spectra_ref[first + 1] = found[:, lanes:]


def analyse_kernel(kernel_ref, table_ref, spectra_ref):
    blocks, double, lanes = spectra_ref.shape
    for first in range(0, blocks, 2):
        rows = []
        for block in (first, first + 1):
            high, low = in_parts(kernel_ref[block])
            rows.append(jnp.concatenate([high, low, high], axis=1))
        found = lax.dot_general(
            table_ref[...],
            jnp.concatenate(rows, axis=0),
            (((1,), (1,)), ((), ())),
            preferred_element_type=jnp.float32,
        )
        spectra_ref[first] = found[:, :lanes]
        spectra_ref[first + 1] = found[:, lanes:]


def synthesise(spectra_ref, table_ref):
    blocks, double, lanes = spectra_ref.shape
    found = []
    for first in range(0, blocks, 2):
        columns = []
        for block in (first, first + 1):
            high, low = in_parts(spectra_ref[block])
            columns.append(jnp.concatenate([high, low, high], axis=0))
        pair = jnp.dot(
            table_ref[...], jnp.concatenate(columns, axis=1), preferred_element_type=jnp.float32
        )
        found.append(pair[:, :lanes])
        found.append(pair[:, lanes:])
    return found


def multiply(left_ref, right_ref, out_ref, reverse):
    blocks, double, lanes = out_ref.shape
    width = double // 2

    def step(index, carry):
        real_rows = pl.ds(pl.multiple_of(index * 8, 8), 8)
        imag_rows = pl.ds(pl.multiple_of(width + index * 8, 8), 8)
        left_real = [left_ref[block, real_rows] for block in range(blocks)]
        left_imag = [left_ref[block, imag_rows] for block in range(blocks)]
        right_real = [right_ref[block, real_rows] for block in range(blocks)]
        right_imag = [right_ref[block, imag_rows] for block in range(blocks)]
        left_sum = [
            real - imag if reverse else real + imag for real, imag in zip(left_real, left_imag)
        ]
        right_sum = [real + imag for real, imag in zip(right_real, right_imag)]
        right_gap = [imag - real for real, imag in zip(right_real, right_imag)]
        for m in range(blocks):
            one = two = three = 0.0
            for l in range(blocks - m if reverse else m + 1):
                r = m + l if reverse else m - l
                one = one + right_real[r] * left_sum[l]
                two = two + left_real[l] * right_gap[r]
                three = three + left_imag[l] * right_sum[r]
            out_ref[m, real_rows] = one + three if reverse else one - three
            out_ref[m, imag_rows] = one + two
        return carry

    lax.fori_loop(0, width // 8, step, 0, unroll=2)


def gates(start_ref, mixed_refs, taps_ref, padded_ref):
    outer, inner, values = [
        short_filtered(padded_ref.at[group], ref, taps_ref[group])
        for group, ref in enumerate(mixed_refs)
    ]
    rows = lax.broadcasted_iota(jnp.int32, outer.shape, 0)
    live = (rows >= start_ref[0]).astype(jnp.float32)
    return outer, inner, values, live


def forward_kernel(
    start_ref,
    outer_ref,
    inner_ref,
    value_ref,
    kernel_ref,
    taps_ref,
    skip_ref,
    analysis_ref,
    synthesis_ref,
    convolved_ref,
    branch_ref,
    signal_spectra,
    kernel_spectra,
    spectra,
    padded,
):
    width = kernel_ref.shape[2]
    outer, inner, values, live = gates(start_ref, (outer_ref, inner_ref, value_ref), taps_ref, padded)
    gated = values * inner * live
    analyse(gated, analysis_ref, signal_spectra)
    analyse_kernel(kernel_ref, analysis_ref, kernel_spectra)
    multiply(kernel_spectra, signal_spectra, spectra, False)
    found = synthesise(spectra, synthesis_ref)
    pieces = [found[0][:width]]
    for block in range(1, len(found)):
        pieces.append(found[block][:width] + found[block - 1][width:])
    convolved = jnp.concatenate(pieces, axis=0) + gated * skip_ref[...]
    convolved_ref[...] = convolved
    branch_ref[...] = (convolved * outer).astype(jnp.bfloat16)


def lag_blocks(found, width):
    pieces = []
    for block in range(len(found)):
        piece = found[block][:width]
        if block + 1 < len(found):
            piece = piece - found[block + 1][width:]
        pieces.append(piece)
    return pieces


def backward_kernel(
    start_ref,
    grad_ref,
    convolved_ref,
    outer_ref,
    inner_ref,
    value_ref,
    kernel_ref,
    taps_ref,
    skip_ref,
    analysis_ref,
    synthesis_ref,
    mixed_grad_ref,
    kernel_kept_ref,
    kernel_given_ref,
    sums_ref,
    signal_spectra,
    kernel_spectra,
    grad_spectra,
    spectra,
    padded,
):
    width = kernel_ref.shape[2]
    mixed_refs = (outer_ref, inner_ref, value_ref)
    outer, inner, values, live = gates(start_ref, mixed_refs, taps_ref, padded)
    gated = values * inner * live
    branch_grad = grad_ref[...]
    conv_grad = branch_grad * outer
    outer_grad = branch_grad * convolved_ref[...]
    analyse(gated, analysis_ref, signal_spectra)
    analyse_kernel(kernel_ref, analysis_ref, kernel_spectra)
    analyse(conv_grad, analysis_ref, grad_spectra)
    multiply(signal_spectra, grad_spectra, spectra, True)
    lags = lag_blocks(synthesise(spectra, synthesis_ref), width)
    half = len(lags) // 2
    first = start_ref[1] == 0
    for block in range(half):
        columns = slice(block * width, (block + 1) * width)
        one, two = lags[block].T, lags[half + block].T
        kernel_kept_ref[:, columns] = jnp.where(first, one, two)
        kernel_given_ref[:, columns] = jnp.where(first, two, one)
    multiply(kernel_spectra, grad_spectra, spectra, True)
    back = jnp.concatenate(lag_blocks(synthesise(spectra, synthesis_ref), width), axis=0)
    gated_grad = (back + conv_grad * skip_ref[...]) * live

    def total(array):
        return jnp.sum(array, axis=0, keepdims=True)

    count = outer.shape[0]
    filter_rows, bias_rows, low_rows = [], [], []
    grads = (outer_grad, gated_grad * values, gated_grad * inner)
    for group in range(3):
        grad, mixed, taps = grads[group], mixed_refs[group][...], taps_ref[group]
        padded[group, :count] = grad
        padded[group, count : count + 8] = jnp.zeros((8, grad.shape[1]), jnp.float32)
        next_one, next_two = padded[group, 1 : 1 + count], padded[group, 2 : 2 + count]
        mixed_grad = taps[2:3] * grad + taps[1:2] * next_one + taps[0:1] * next_two
        low = mixed_grad.astype(jnp.bfloat16)
        mixed_grad_ref[group] = low
        filter_rows.append([total(next_two * mixed), total(next_one * mixed), total(grad * mixed)])
        bias_rows.append(total(grad))
        low_rows.append(total(low.astype(jnp.float32)))
    rows = [filter_rows[group][tap] for tap in range(3) for group in range(3)]
    rows = rows + bias_rows + low_rows + [total(conv_grad * gated)]
    sums_ref[...] = jnp.concatenate(rows, axis=0)


def kernel_parameters():
    return pltpu.CompilerParams(
        vmem_limit_bytes=56 * 1024 * 1024
    )


def kernel_specs(tokens, parts, width, lanes, features):
    groups = features // lanes

    def mixed(group):
        return pl.BlockSpec((tokens, lanes), lambda tile, *_: (0, group * groups + tile))

    return (
        [pl.BlockSpec(memory_space=pltpu.SMEM)],
        [mixed(0), mixed(1), mixed(2)],
        [
            pl.BlockSpec((parts, lanes, width), lambda tile, *_: (0, tile, 0)),
            pl.BlockSpec((3, 4, lanes), lambda tile, *_: (0, 0, tile)),
            pl.BlockSpec((1, lanes), lambda tile, *_: (0, tile)),
            pl.BlockSpec((2 * width, 3 * width), lambda *_: (0, 0)),
            pl.BlockSpec((2 * width, 6 * width), lambda *_: (0, 0)),
        ],
        pl.BlockSpec((tokens, lanes), lambda tile, *_: (0, tile)),
        pltpu.VMEM((parts, 2 * width, lanes), jnp.float32),
    )


def forward_convolution(start, mixed, kernel, taps, skip, tables, lanes=128):
    parts, features, width = kernel.shape
    tokens = mixed.shape[0]
    start_spec, mixed_specs, rest, plain, spectra = kernel_specs(tokens, parts, width, lanes, features)
    return pl.pallas_call(
        forward_kernel,
        grid=(features // lanes,),
        in_specs=start_spec + mixed_specs + rest,
        out_specs=(plain, plain),
        out_shape=(
            jax.ShapeDtypeStruct((tokens, features), jnp.float32),
            jax.ShapeDtypeStruct((tokens, features), jnp.bfloat16),
        ),
        scratch_shapes=[spectra] * 3 + [pltpu.VMEM((3, tokens + 8, lanes), jnp.float32)],
        compiler_params=kernel_parameters(),
        cost_estimate=NO_COST,
        name="forward_convolution",
    )(start, mixed, mixed, mixed, kernel, taps, skip, *tables)


def backward_convolution(start, grad, convolved, mixed, kernel, taps, skip, tables, lanes=128):
    parts, features, width = kernel.shape
    tokens = mixed.shape[0]
    start_spec, mixed_specs, rest, plain, spectra = kernel_specs(tokens, parts, width, lanes, features)
    return pl.pallas_call(
        backward_kernel,
        grid=(features // lanes,),
        in_specs=start_spec + [plain, plain] + mixed_specs + rest,
        out_specs=(
            pl.BlockSpec((3, tokens, lanes), lambda tile: (0, 0, tile)),
            pl.BlockSpec((lanes, tokens // 2), lambda tile: (tile, 0)),
            pl.BlockSpec((lanes, tokens // 2), lambda tile: (tile, 0)),
            pl.BlockSpec((16, lanes), lambda tile: (0, tile)),
        ),
        out_shape=(
            jax.ShapeDtypeStruct((3, tokens, features), jnp.bfloat16),
            jax.ShapeDtypeStruct((features, tokens // 2), jnp.float32),
            jax.ShapeDtypeStruct((features, tokens // 2), jnp.float32),
            jax.ShapeDtypeStruct((16, features), jnp.float32),
        ),
        scratch_shapes=[spectra] * 4 + [pltpu.VMEM((3, tokens + 8, lanes), jnp.float32)],
        compiler_params=kernel_parameters(),
        cost_estimate=NO_COST,
        name="backward_convolution",
    )(start, grad, convolved, mixed, mixed, mixed, kernel, taps, skip, *tables)


def unit_rows(values):
    centered = values - jnp.mean(values, axis=-1, keepdims=True)
    spread = lax.rsqrt(jnp.mean(centered * centered, axis=-1, keepdims=True) + EPSILON)
    return centered * spread, spread


def unit_rows_back(grad, unit, spread, gain):
    scaled = grad * gain
    inner = scaled - jnp.mean(scaled, axis=-1, keepdims=True)
    return (inner - unit * jnp.mean(scaled * unit, axis=-1, keepdims=True)) * spread


def matmul(left, right):
    return jnp.dot(left, right, preferred_element_type=jnp.float32)


def matmul_back(left, right):
    return lax.dot_general(left, right, (((1,), (1,)), ((), ())), preferred_element_type=jnp.float32)


def columns_of(array, refs):
    first = 0
    for ref in refs:
        ref[...] = array[:, first : first + ref.shape[1]]
        first += ref.shape[1]


def column_sums(array):
    return jnp.sum(array, axis=0, keepdims=True)


def project_kernel(x_ref, gain_ref, bias_ref, weight_ref, offset_ref, normed_ref, mixed_ref):
    unit, _ = unit_rows(x_ref[...])
    normed = (unit * gain_ref[...] + bias_ref[...]).astype(jnp.bfloat16)
    normed_ref[...] = normed
    mixed_ref[...] = matmul(normed, weight_ref[...]) + offset_ref[...]


def feed_kernel(
    x_ref,
    branch_ref,
    out_weight_ref,
    out_bias_ref,
    gain_ref,
    bias_ref,
    up_weight_ref,
    up_bias_ref,
    down_weight_ref,
    down_bias_ref,
    residual_ref,
    normed_ref,
    activated_ref,
    slope_ref,
    *output_refs,
):
    residual = x_ref[...] + matmul(branch_ref[...], out_weight_ref[...]) + out_bias_ref[...]
    residual_ref[...] = residual
    unit, _ = unit_rows(residual)
    normed = (unit * gain_ref[...] + bias_ref[...]).astype(jnp.bfloat16)
    normed_ref[...] = normed
    total = residual + down_bias_ref[...]
    factor = math.sqrt(2.0 / math.pi)
    chunk = residual.shape[1]
    for first in range(0, up_weight_ref.shape[1], chunk):
        columns = slice(first, first + chunk)
        expanded = matmul(normed, up_weight_ref[:, columns]) + up_bias_ref[:, columns]
        square = expanded * expanded
        turned = jnp.tanh(factor * (expanded + 0.044715 * (square * expanded)))
        half = 0.5 + 0.5 * turned
        activated = (expanded * half).astype(jnp.bfloat16)
        activated_ref[:, columns] = activated
        slope_ref[:, columns] = half + (0.5 * factor) * expanded * (1.0 - turned * turned) * (
            1.0 + (3 * 0.044715) * square
        )
        total = total + matmul(activated, down_weight_ref[columns, :])
    columns_of(total, output_refs)


def feed_back_kernel(
    grad_ref,
    residual_ref,
    slope_ref,
    gain_ref,
    out_weight_ref,
    up_weight_ref,
    down_weight_ref,
    expanded_ref,
    residual_grad_ref,
    residual_low_ref,
    branch_grad_ref,
    sums_ref,
    wide_sums_ref,
):
    grad = grad_ref[...]
    grad_low = grad.astype(jnp.bfloat16)
    chunk = grad.shape[1]
    normed_grad = None
    wide = []
    for first in range(0, up_weight_ref.shape[1], chunk):
        columns = slice(first, first + chunk)
        expanded = matmul_back(grad_low, down_weight_ref[columns, :]) * slope_ref[:, columns]
        low = expanded.astype(jnp.bfloat16)
        expanded_ref[:, columns] = low
        wide.append(column_sums(low.astype(jnp.float32)))
        part = matmul_back(low, up_weight_ref[:, columns])
        normed_grad = part if normed_grad is None else normed_grad + part
    unit, spread = unit_rows(residual_ref[...])
    residual_grad = grad + unit_rows_back(normed_grad, unit, spread, gain_ref[...])
    residual_grad_ref[...] = residual_grad
    low = residual_grad.astype(jnp.bfloat16)
    residual_low_ref[...] = low
    branch_grad_ref[...] = matmul_back(low, out_weight_ref[...])
    sums = [
        column_sums(normed_grad * unit),
        column_sums(normed_grad),
        column_sums(low.astype(jnp.float32)),
        column_sums(grad),
    ]

    @pl.when(pl.program_id(0) == 0)
    def _():
        sums_ref[...] = jnp.zeros_like(sums_ref)
        wide_sums_ref[...] = jnp.zeros_like(wide_sums_ref)

    sums_ref[...] += jnp.concatenate(sums, axis=0)
    wide_sums_ref[...] += jnp.concatenate(wide, axis=1)


def input_grad_kernel(
    mixed_ref, weight_ref, x_ref, gain_ref, residual_grad_ref, first_ref, second_ref, sums_ref
):
    features = x_ref.shape[1]
    normed_grad = None
    for group in range(3):
        columns = slice(group * features, (group + 1) * features)
        part = matmul_back(mixed_ref[group], weight_ref[:, columns])
        normed_grad = part if normed_grad is None else normed_grad + part
    unit, spread = unit_rows(x_ref[...])
    total = residual_grad_ref[...] + unit_rows_back(normed_grad, unit, spread, gain_ref[...])
    columns_of(total, (first_ref, second_ref))
    sums = jnp.concatenate([column_sums(normed_grad * unit), column_sums(normed_grad)], axis=0)

    @pl.when(pl.program_id(0) == 0)
    def _():
        sums_ref[...] = jnp.zeros_like(sums_ref)

    sums_ref[...] += sums


def by_rows(kernel, name, rows, inputs, outputs, height=256):
    def spec(shape, held):
        if len(shape) == 3:
            return pl.BlockSpec((shape[0], height, shape[2]), lambda step: (0, step, 0))
        if shape[0] == rows and not held:
            return pl.BlockSpec((height, shape[1]), lambda step: (step, 0))
        return pl.BlockSpec(shape, lambda step: (0, 0))

    return pl.pallas_call(
        kernel,
        grid=(rows // height,),
        in_specs=[spec(array.shape, held) for array, held in inputs],
        out_specs=tuple(spec(shape, False) for shape, _ in outputs),
        out_shape=tuple(jax.ShapeDtypeStruct(shape, kind) for shape, kind in outputs),
        compiler_params=kernel_parameters(),
        cost_estimate=NO_COST,
        name=name,
    )(*[array for array, _ in inputs])


def product_kernel(half_ref, left_ref, right_ref, out_ref):
    out_ref[...] = product_tile(left_ref, right_ref)


def product_tile(left_ref, right_ref):
    if len(right_ref.shape) == 2:
        return product(left_ref[...], right_ref[...].astype(jnp.bfloat16))
    return jnp.concatenate(
        [product(left_ref[...], right_ref[group]) for group in range(right_ref.shape[0])], axis=1
    )


def product_specs(left, right, tile):
    tokens = left.shape[0]
    half = right.shape[-1] // 2
    left_spec = pl.BlockSpec((tokens, tile), lambda step, half_ref: (0, step))
    if right.ndim == 2:
        right_spec = pl.BlockSpec((tokens, half), lambda step, half_ref: (0, half_ref[0]))
        return half, left_spec, right_spec
    right_spec = pl.BlockSpec((right.shape[0], tokens, half), lambda step, half_ref: (0, 0, half_ref[0]))
    return half * right.shape[0], left_spec, right_spec


def half_product(left, right, half, tile=384):
    rows = left.shape[1]
    columns, left_spec, right_spec = product_specs(left, right, tile)
    return pl.pallas_call(
        product_kernel,
        grid_spec=pltpu.PrefetchScalarGridSpec(
            num_scalar_prefetch=1,
            grid=(rows // tile,),
            in_specs=[left_spec, right_spec],
            out_specs=pl.BlockSpec((tile, columns), lambda step, half_ref: (step, 0)),
        ),
        out_shape=jax.ShapeDtypeStruct((rows, columns), jnp.float32),
        compiler_params=kernel_parameters(),
        cost_estimate=NO_COST,
        name="half_product",
    )(half, left, right)


def whole_product_kernel(left_ref, right_ref, out_ref):
    out_ref[...] = product(left_ref[...], right_ref[...])


def whole_product(left, right):
    tokens, rows = left.shape
    return pl.pallas_call(
        whole_product_kernel,
        grid=(right.shape[1] // rows,),
        in_specs=[
            pl.BlockSpec((tokens, rows), lambda step: (0, 0)),
            pl.BlockSpec((tokens, rows), lambda step: (0, step)),
        ],
        out_specs=pl.BlockSpec((rows, rows), lambda step: (0, step)),
        out_shape=jax.ShapeDtypeStruct((rows, right.shape[1]), jnp.float32),
        compiler_params=kernel_parameters(),
        cost_estimate=NO_COST,
        name="whole_product",
    )(left, right)


def parted_product_kernel(bits_ref, left_ref, right_ref, taken_ref, *out_refs):
    total = product_tile(left_ref, right_ref) + taken_ref[...]
    left = 0
    for part in range(len(out_refs) // 2):
        kept_ref, given_ref = out_refs[2 * part : 2 * part + 2]
        pieces, rows, columns = kept_ref.shape
        first = bits_ref[1 + part] == 0
        for piece in range(pieces):
            one = total[2 * piece * rows : (2 * piece + 1) * rows, left : left + columns]
            two = total[(2 * piece + 1) * rows : (2 * piece + 2) * rows, left : left + columns]
            kept_ref[piece] = jnp.where(first, one, two)
            given_ref[piece] = jnp.where(first, two, one)
        left += columns


def parted_product(left, right, half, taken, plan, tile=384):
    rows = left.shape[1]
    columns, left_spec, right_spec = product_specs(left, right, tile)
    steps = rows // tile
    specs, shapes = [], []
    for _, pieces in plan:
        shape = (pieces, rows // (2 * pieces), columns // len(plan))
        block = (pieces // steps,) + shape[1:]
        specs += [pl.BlockSpec(block, lambda step, bits_ref: (step, 0, 0))] * 2
        shapes += [jax.ShapeDtypeStruct(shape, jnp.float32)] * 2
    return pl.pallas_call(
        parted_product_kernel,
        grid_spec=pltpu.PrefetchScalarGridSpec(
            num_scalar_prefetch=1,
            grid=(steps,),
            in_specs=[
                left_spec,
                right_spec,
                pl.BlockSpec((tile, columns), lambda step, bits_ref: (step, 0)),
            ],
            out_specs=tuple(specs),
        ),
        out_shape=tuple(shapes),
        compiler_params=kernel_parameters(),
        cost_estimate=NO_COST,
        name="parted_product",
    )(jnp.concatenate([half] + [which for which, _ in plan]), left, right, taken)


def fold_kernel(bit_ref, *refs):
    *sources, kept_ref, given_ref = refs
    first = bit_ref[0] == 0
    height, lane = kept_ref.shape[1], 0
    for kept, taken in zip(sources[::2], sources[1::2]):
        total = kept[...] + taken[...]
        for row in range(0, total.shape[1], height):
            columns = slice(lane, lane + total.shape[2])
            one, two = total[0, row : row + height], total[1, row : row + height]
            kept_ref[0, :, columns] = jnp.where(first, one, two)
            given_ref[0, :, columns] = jnp.where(first, two, one)
            lane += total.shape[2]


def fold(pairs, which, height):
    count = pairs[0][0].shape[0]
    operands, specs, columns = [], [], 0
    for kept, taken, *share in pairs:
        place, shares = share if share else (0, 1)
        block = (2, kept.shape[1], kept.shape[2] // shares)
        operands += [kept, taken]
        specs += [pl.BlockSpec(block, lambda step, place=place: (step, 0, place))] * 2
        columns += block[1] // height * block[2]
    one = pl.BlockSpec((1, height, columns), lambda step: (step, 0, 0))
    shape = jax.ShapeDtypeStruct((count // 2, height, columns), jnp.float32)
    return pl.pallas_call(
        fold_kernel,
        grid=(count // 2,),
        in_specs=[pl.BlockSpec(memory_space=pltpu.SMEM)] + specs,
        out_specs=(one, one),
        out_shape=(shape, shape),
        compiler_params=kernel_parameters(),
        cost_estimate=NO_COST,
        name="fold",
    )(which, *operands)


def unpack_kernel(bits_ref, own_ref, y_ref, core_ref, both_ref, *out_refs):
    core_first, y_first = bits_ref[0] == 0, bits_ref[1] == 0
    own, beside = own_ref[...], y_ref[...]
    mine = [jnp.where(y_first, own, beside), jnp.where(y_first, beside, own)]
    own, beside = core_ref[...], both_ref[...]
    theirs = [jnp.where(y_first, own, beside), jnp.where(y_first, beside, own)]
    height = own.shape[0]
    for y in range(2):
        for core in range(2):
            block = jnp.where(core_first, mine[y], theirs[y])
            if core == 1:
                block = jnp.where(core_first, theirs[y], mine[y])
            lane = 0
            for ref in out_refs:
                rows, columns = ref.shape
                if columns == 128:
                    ref[(2 * core + y) * height : (2 * core + y + 1) * height] = block[:, lane:]
                    continue
                groups = 3 if columns == 3 * height * 16 and rows == 2 * height else 1
                half = columns // (2 * groups)
                for place in range(rows // (2 * height)):
                    for group in range(groups):
                        top = y * (rows // 2) + place * height
                        left = group * 2 * half + core * half
                        ref[top : top + height, left : left + half] = block[:, lane : lane + half]
                        lane += half


def gathered(share):
    y_other, core_other = swapped(share, "dp", 2), swapped(share, "dp", 1)
    return share, y_other, core_other, swapped(y_other, "dp", 1)


def unpacked(shares, shapes):
    return pl.pallas_call(
        unpack_kernel,
        in_specs=[pl.BlockSpec(memory_space=pltpu.SMEM)] + [pl.BlockSpec(memory_space=pltpu.VMEM)] * 4,
        out_specs=[pl.BlockSpec(memory_space=pltpu.VMEM)] * len(shapes),
        out_shape=[jax.ShapeDtypeStruct(shape, jnp.float32) for shape in shapes],
        compiler_params=kernel_parameters(),
        cost_estimate=NO_COST,
        name="unpack",
    )(jnp.concatenate([flag("dp", 1), flag("dp", 2)]), *shares)


def swapped(array, axis, by):
    count = lax.axis_size(axis)
    return lax.ppermute(array, axis, [(i, i ^ by) for i in range(count)])


def bit(axis, by):
    return (lax.axis_index(axis) // by) % 2


def doubled(array, dim, axis, by):
    other = swapped(array, axis, by)
    first = bit(axis, by) == 0
    return jnp.concatenate(
        [jnp.where(first, array, other), jnp.where(first, other, array)], axis=dim
    )


def product(left, columns):
    return lax.dot_general(left, columns, (((0,), (0,)), ((), ())), preferred_element_type=jnp.float32)


def flag(axis, by):
    return bit(axis, by).astype(jnp.int32).reshape(1)


def reduced(kept, given, steps):
    for (axis, by), following in zip(steps, steps[1:] + [None]):
        taken = swapped(given, axis, by)
        if following is None:
            return (kept + taken)[0]
        kept, given = fold([(kept, taken)], flag(*following), kept.shape[1])


def by_sequences(
    tokens,
    offsets,
    norm_gain,
    norm_bias,
    proj_weight,
    proj_bias,
    short_filter,
    short_bias,
    long_kernel,
    skip_bias,
    out_weight,
    out_bias,
    second_gain,
    second_bias,
    up_weight,
    up_bias,
    down_weight,
    down_bias,
    cotangent,
):
    parts, width, features = tokens.shape
    length = parts * width
    hidden_units = up_weight.shape[1]
    hold = lax.optimization_barrier
    tables = tuple(jnp.asarray(table) for table in block_tables(width))
    start = lax.dynamic_slice_in_dim(offsets, lax.axis_index("seq"), 1, 0)
    core, other_core = flag("dp", 1), 1 - flag("dp", 1)
    scalars = jnp.concatenate([start, core])
    low, single = jnp.bfloat16, jnp.float32
    y_step, x_step = ("dp", 2), ("seq", 1)
    z_steps = [("seq", 1 << place) for place in range(1, parts.bit_length() - 1)]

    share = features // 4
    chunk = bit("dp", 1) * 2 + bit("dp", 2)
    piece = lax.dynamic_slice_in_dim(long_kernel, chunk * share, share, 0)
    pieces = jnp.stack([piece] + [swapped(piece, "seq", by) for by in range(2, parts, 2)])
    z = lax.axis_index("seq") // 2
    pieces = jnp.concatenate(
        [lax.dynamic_index_in_dim(pieces, z ^ other, 0) for other in range(parts // 2)]
    )
    hidden, pieces = hold((tokens.astype(single), pieces))
    hidden = lax.all_to_all(hidden, "seq", 0, 0, tiled=True)
    pieces = doubled(pieces[:, None], 1, *x_step).reshape(parts, share, width)
    kernel = doubled(doubled(pieces, 1, "dp", 2), 1, "dp", 1)
    upstream = cotangent.astype(single)
    taps = jnp.concatenate([short_filter.T, short_bias[None]], axis=0)
    taps = jnp.swapaxes(taps.reshape(4, 3, features), 0, 1)
    skip = skip_bias[None]
    hidden, kernel, upstream, taps, scalars = hold((hidden, kernel, upstream, taps, scalars))

    upstream = lax.all_to_all(upstream, "seq", 0, 0, tiled=True)
    hidden = hidden.reshape(length, features)
    normed_low, mixed = by_rows(
        project_kernel,
        "project",
        length,
        [
            (hidden, False),
            (norm_gain[None], True),
            (norm_bias[None], True),
            (proj_weight, True),
            (proj_bias[None], True),
        ],
        [((length, features), low), ((length, 3 * features), single)],
    )
    convolved, branch_low = forward_convolution(scalars, mixed, kernel, taps, skip, tables)
    residual, normed_two_low, activated_low, slope, *output = by_rows(
        feed_kernel,
        "feed",
        length,
        [
            (hidden, False),
            (branch_low, False),
            (out_weight, True),
            (out_bias[None], True),
            (second_gain[None], True),
            (second_bias[None], True),
            (up_weight, True),
            (up_bias[None], True),
            (down_weight, True),
            (down_bias[None], True),
        ],
        [
            ((length, features), single),
            ((length, features), low),
            ((length, hidden_units), low),
            ((length, hidden_units), single),
            ((length, features // 3), single),
            ((length, features * 2 // 3), single),
        ],
    )
    upstream, output = hold((upstream, output))

    def sent(columns):
        columns = columns.reshape(parts, width, -1)
        return lax.all_to_all(columns, "seq", 0, 0, tiled=True)

    output[0] = sent(output[0])
    upstream = upstream.reshape(length, features)
    down_given = half_product(activated_low, upstream, other_core, 768)
    upstream, down_given = hold((upstream, down_given))
    down_taken = swapped(down_given, "dp", 1)
    expanded_low, residual_grad, residual_low, branch_grad, sums_two, wide_sums = by_rows(
        feed_back_kernel,
        "feed_back",
        length,
        [
            (upstream, False),
            (residual, False),
            (slope, False),
            (second_gain[None], True),
            (out_weight, True),
            (up_weight, True),
            (down_weight, True),
        ],
        [
            ((length, hidden_units), low),
            ((length, features), single),
            ((length, features), low),
            ((length, features), single),
            ((4, features), single),
            ((1, hidden_units), single),
        ],
    )
    expanded_low, residual_low, branch_grad = hold((expanded_low, residual_low, branch_grad))
    side = whole_product(normed_two_low, expanded_low)
    side, down_taken, output = hold((side, down_taken, output))
    side = lax.psum_scatter(side, ("seq", "dp"), scatter_dimension=0, tiled=True)
    down_kept, down_given = parted_product(
        activated_low, upstream, core, down_taken, [(flag(*y_step), parts)], 768
    )
    branch_grad, down_given = hold((branch_grad, down_given))

    output[1] = sent(output[1])
    down_taken = swapped(down_given, *y_step)
    mixed_low, kernel_kept, kernel_given, sums = backward_convolution(
        scalars, branch_grad, convolved, mixed, kernel, taps, skip, tables
    )
    proj_given = half_product(normed_low, mixed_low, other_core)
    *input_grad, sums_one = by_rows(
        input_grad_kernel,
        "input_grad",
        length,
        [
            (mixed_low, False),
            (proj_weight, True),
            (hidden, False),
            (norm_gain[None], True),
            (residual_grad, False),
        ],
        [
            ((length, features * 2 // 3), single),
            ((length, features // 3), single),
            ((2, features), single),
        ],
    )
    input_grad, mixed_low, proj_given, kernel_given, down_taken, sums_one, sums, output = hold(
        (input_grad, mixed_low, proj_given, kernel_given, down_taken, sums_one, sums, output)
    )

    rows = features // (2 * parts)
    input_grad[0] = sent(input_grad[0])
    down_kept, down_given = fold([(down_kept, down_taken)], flag(*x_step), down_kept.shape[1])
    down_taken = swapped(down_given, *x_step)
    kernel_taken = swapped(kernel_given, "dp", 1)
    proj_taken = swapped(proj_given, "dp", 1)
    proj_kept, proj_given = parted_product(
        normed_low, mixed_low, core, proj_taken, [(flag(*y_step), parts)]
    )
    proj_given, residual_low = hold((proj_given, residual_low))
    proj_taken = swapped(proj_given, *y_step)
    out_given = half_product(branch_low, residual_low, other_core, 768)
    out_taken = swapped(out_given, "dp", 1)
    out_kept, out_given = parted_product(
        branch_low, residual_low, core, out_taken, [(flag(*y_step), parts)], 768
    )
    output = jnp.concatenate(output, axis=2)
    vectors = [sums_one[0], sums_one[1]]
    vectors += [sums[first : first + 3].reshape(-1) for first in range(0, 15, 3)]
    vectors += [sums[15], sums_two[2], sums_two[0], sums_two[1], wide_sums[0], sums_two[3]]
    sizes = [vector.shape[0] // parts for vector in vectors]
    packed = jnp.concatenate([vector.reshape(parts, -1) for vector in vectors], axis=1)
    packed = jnp.pad(packed, ((0, 0), (0, 4 * rows * 128 - packed.shape[1])))
    packed = packed.reshape(parts, 2, 2 * rows, 128)
    packed_kept = lax.dynamic_index_in_dim(packed, core[0], 1, keepdims=False)
    packed_given = lax.dynamic_index_in_dim(packed, other_core[0], 1, keepdims=False)
    packed_taken = swapped(packed_given, "dp", 1)
    kernel_kept, kernel_taken = [
        array.reshape(parts, 2 * rows, -1) for array in (kernel_kept, kernel_taken)
    ]
    kernel_kept, kernel_taken, packed_kept, packed_taken = [
        array.reshape(2 * parts, rows, -1)
        for array in (kernel_kept, kernel_taken, packed_kept, packed_taken)
    ]
    rest_kept, rest_given = fold(
        [(kernel_kept, kernel_taken), (packed_kept, packed_taken)], flag(*y_step), rows
    )
    input_grad, down_taken, proj_taken, rest_given, out_given, output = hold(
        (input_grad, down_taken, proj_taken, rest_given, out_given, output)
    )

    input_grad[1] = sent(input_grad[1])
    rest_taken = swapped(rest_given, *y_step)
    out_taken = swapped(out_given, *y_step)
    proj_kept, proj_given = fold([(proj_kept, proj_taken)], flag(*x_step), rows)
    proj_taken = swapped(proj_given, *x_step)
    feed_kept, feed_given = fold([(down_kept, down_taken)], flag(*z_steps[0]), rows)
    feed_taken = swapped(feed_given, *z_steps[0])
    input_grad, proj_taken, rest_taken, out_taken, feed_taken = hold(
        (input_grad, proj_taken, rest_taken, out_taken, feed_taken)
    )

    rest_kept, rest_given = fold(
        [(out_kept, out_taken), (rest_kept, rest_taken)], flag(*x_step), rows
    )
    rest_given, feed_taken = hold((rest_given, feed_taken))
    rest_taken = swapped(rest_given, *x_step)
    feed_kept, feed_given = fold([(feed_kept, feed_taken)], flag(*z_steps[1]), rows)
    feed_taken = swapped(feed_given, *z_steps[1])
    input_grad = jnp.concatenate(input_grad, axis=2)
    mixer_kept, mixer_given = fold(
        [(proj_kept, proj_taken), (rest_kept, rest_taken)], flag(*z_steps[0]), rows
    )
    feed_kept, mixer_given = hold((feed_kept, mixer_given))
    mixer_taken = swapped(mixer_given, *z_steps[0])
    feed_share = (feed_kept + feed_taken)[0]
    feed_shares = gathered(feed_share)
    mixer_taken, input_grad, *feed_shares = hold((mixer_taken, input_grad, *feed_shares))
    mixer_kept, mixer_given = fold([(mixer_kept, mixer_taken)], flag(*z_steps[1]), rows)
    mixer_taken = swapped(mixer_given, *z_steps[1])
    (down_share,) = unpacked(feed_shares, [(hidden_units // parts, features)])
    side = lax.all_gather(side, "dp", axis=0, tiled=True)
    mixer_taken, down_share, up_share = hold((mixer_taken, down_share, side))
    mixer_share = (mixer_kept + mixer_taken)[0]
    proj_share, out_share, kernel_share, packed = unpacked(
        gathered(mixer_share),
        [
            (features // parts, 3 * features),
            (features // parts, features),
            (features // parts, length),
            (4 * rows, 128),
        ],
    )
    packed = packed.reshape(-1)
    ends = np.cumsum(sizes)
    vectors = [packed[end - size : end] for size, end in zip(sizes, ends)]
    return (
        output,
        input_grad,
        vectors[0],
        vectors[1],
        proj_share,
        vectors[6],
        jnp.stack(vectors[2:5], axis=1),
        vectors[5],
        kernel_share,
        vectors[7],
        out_share,
        vectors[8],
        vectors[9],
        vectors[10],
        up_share,
        vectors[11],
        down_share,
        vectors[12],
    )


def per_device(tokens, offsets, *rest):
    fits = (
        tokens.shape[0] == lax.axis_size("seq")
        and lax.axis_size("dp") == 4
        and tokens.shape[0] % 2 == 0
        and tokens.shape[1] % 128 == 0
        and lax.axis_size("seq") & (lax.axis_size("seq") - 1) == 0
    )
    plan = by_sequences if fits else by_channels
    return plan(tokens, offsets, *rest)


def solution(mesh):
    return jax.shard_map(
        per_device,
        mesh=mesh,
        in_specs=(
            P("dp", "seq", None),
            P("dp"),
            P(),
            P(),
            P(),
            P(),
            P(),
            P(),
            P(None, "seq"),
            P(),
            P(),
            P(),
            P(),
            P(),
            P(),
            P(),
            P(),
            P(),
            P("dp", "seq", None),
        ),
        out_specs=(
            P("dp", "seq", None),
            P("dp", "seq", None),
            P("seq"),
            P("seq"),
            P("seq", None),
            P("seq"),
            P("seq", None),
            P("seq"),
            P("seq", None),
            P("seq"),
            P("seq", None),
            P("seq"),
            P("seq"),
            P("seq"),
            P("seq", None),
            P("seq"),
            P("seq", None),
            P("seq"),
        ),
        check_vma=False,
    )
```

```python
import functools
import math

import jax
import jax.numpy as jnp
import ml_dtypes
import numpy as np
from jax import lax
from jax.experimental import pallas as pl
from jax.experimental.pallas import tpu as pltpu
from jax.sharding import PartitionSpec as P

EPSILON = 1e-05
PRECISE = lax.Precision.HIGHEST
NO_COST = pl.CostEstimate(flops=0, bytes_accessed=0, transcendentals=0)


def passed_along(array, axis, by):
    count = lax.axis_size(axis)
    pairs = [(i, i + by) for i in range(count) if 0 <= i + by < count]
    return lax.ppermute(array, axis, pairs)


def layer_norm(values, gain, offset):
    centered = values - jnp.mean(values, axis=-1, keepdims=True)
    spread = lax.rsqrt(jnp.mean(centered * centered, axis=-1, keepdims=True) + EPSILON)
    return centered * spread * gain + offset


def angle_table(rows, cols, modulus):
    product = (
        jnp.arange(rows, dtype=jnp.int32)[:, None]
        * jnp.arange(cols, dtype=jnp.int32)[None, :]
        % modulus
    )
    angles = product.astype(jnp.float32) * (2.0 * math.pi / modulus)
    return (jnp.cos(angles), jnp.sin(angles))


def fourier_tables(blocks, width):
    coarse_cos, coarse_sin = angle_table(blocks, 2 * blocks, 2 * blocks)
    twist_cos, twist_sin = angle_table(2 * blocks, width, 2 * blocks * width)
    fine_cos, fine_sin = angle_table(width, width, width)
    return (coarse_cos, coarse_sin, twist_cos, twist_sin, fine_cos, fine_sin)


def forward_transform(signal, tables):
    coarse_cos, coarse_sin, twist_cos, twist_sin, fine_cos, fine_sin = tables
    first_real = jnp.einsum("rpc,pk->rkc", signal, coarse_cos, precision=PRECISE)
    first_imag = -jnp.einsum("rpc,pk->rkc", signal, coarse_sin, precision=PRECISE)
    turned_real = first_real * twist_cos + first_imag * twist_sin
    turned_imag = first_imag * twist_cos - first_real * twist_sin
    spectrum_real = jnp.einsum(
        "rkc,cm->rkm", turned_real, fine_cos, precision=PRECISE
    ) + jnp.einsum("rkc,cm->rkm", turned_imag, fine_sin, precision=PRECISE)
    spectrum_imag = jnp.einsum(
        "rkc,cm->rkm", turned_imag, fine_cos, precision=PRECISE
    ) - jnp.einsum("rkc,cm->rkm", turned_real, fine_sin, precision=PRECISE)
    return (spectrum_real, spectrum_imag)


def inverse_transform(spectrum_real, spectrum_imag, tables):
    coarse_cos, coarse_sin, twist_cos, twist_sin, fine_cos, fine_sin = tables
    back_real = jnp.einsum("rkm,cm->rkc", spectrum_real, fine_cos, precision=PRECISE) - jnp.einsum(
        "rkm,cm->rkc", spectrum_imag, fine_sin, precision=PRECISE
    )
    back_imag = jnp.einsum("rkm,cm->rkc", spectrum_real, fine_sin, precision=PRECISE) + jnp.einsum(
        "rkm,cm->rkc", spectrum_imag, fine_cos, precision=PRECISE
    )
    turned_real = back_real * twist_cos - back_imag * twist_sin
    turned_imag = back_real * twist_sin + back_imag * twist_cos
    total = 2 * coarse_cos.shape[0] * twist_cos.shape[1]
    signal = jnp.einsum("rkc,pk->rpc", turned_real, coarse_cos, precision=PRECISE) - jnp.einsum(
        "rkc,pk->rpc", turned_imag, coarse_sin, precision=PRECISE
    )
    return signal / total


def by_channels(
    tokens,
    offsets,
    norm_gain,
    norm_bias,
    proj_weight,
    proj_bias,
    short_filter,
    short_bias,
    long_kernel,
    skip_bias,
    out_weight,
    out_bias,
    second_gain,
    second_bias,
    up_weight,
    up_bias,
    down_weight,
    down_bias,
    cotangent,
):
    seq_count, tok_count, features = tokens.shape
    parts = lax.axis_size("seq")
    chans = features // parts
    length = parts * tok_count
    tables = fourier_tables(parts, tok_count)
    spectral = (seq_count, chans, 2 * parts, tok_count)
    positions = lax.axis_index("seq") * tok_count + jnp.arange(tok_count, dtype=jnp.int32)
    live = (positions[None, :] >= offsets[:, None]).astype(jnp.float32)[:, :, None]
    hidden = tokens.astype(jnp.float32)
    normed, norm_pull = jax.vjp(layer_norm, hidden, norm_gain, norm_bias)
    normed_low = normed.astype(jnp.bfloat16)
    mixed = (
        jnp.einsum("sti,ij->stj", normed_low, proj_weight, preferred_element_type=jnp.float32)
        + proj_bias
    )
    rim = passed_along(mixed[:, tok_count - 2 :, :], "seq", 1)
    extended = jnp.concatenate([rim, mixed], axis=1)
    filtered = (
        short_filter[:, 0] * extended[:, :tok_count]
        + short_filter[:, 1] * extended[:, 1 : tok_count + 1]
        + short_filter[:, 2] * extended[:, 2:]
        + short_bias
    )
    outer_gate = filtered[:, :, :features]
    inner_gate = filtered[:, :, features : 2 * features]
    values = filtered[:, :, 2 * features :]
    gated = values * inner_gate * live
    gated_chan, kernel_chan = (
        lax.all_to_all(jnp.swapaxes(gated, 1, 2), "seq", split_axis=1, concat_axis=2, tiled=True),
        lax.all_to_all(long_kernel[None], "seq", split_axis=1, concat_axis=2, tiled=True),
    )
    gated_real, gated_imag = forward_transform(
        gated_chan.reshape(seq_count * chans, parts, tok_count), tables
    )
    gated_real = gated_real.reshape(spectral)
    gated_imag = gated_imag.reshape(spectral)
    kernel_real, kernel_imag = forward_transform(
        kernel_chan.reshape(chans, parts, tok_count), tables
    )
    prod_real = gated_real * kernel_real - gated_imag * kernel_imag
    prod_imag = gated_real * kernel_imag + gated_imag * kernel_real
    conv_chan = inverse_transform(
        prod_real.reshape(-1, 2 * parts, tok_count),
        prod_imag.reshape(-1, 2 * parts, tok_count),
        tables,
    )
    conv_chan = conv_chan.reshape(seq_count, chans, length)
    conv_tokens = jnp.swapaxes(
        lax.all_to_all(conv_chan, "seq", split_axis=2, concat_axis=1, tiled=True), 1, 2
    )
    convolved = conv_tokens + gated * skip_bias
    branch = convolved * outer_gate
    branch_low = branch.astype(jnp.bfloat16)
    residual = (
        hidden
        + jnp.einsum("sti,ij->stj", branch_low, out_weight, preferred_element_type=jnp.float32)
        + out_bias
    )
    normed_two, second_pull = jax.vjp(layer_norm, residual, second_gain, second_bias)
    normed_two_low = normed_two.astype(jnp.bfloat16)
    expanded = (
        jnp.einsum("sti,ij->stj", normed_two_low, up_weight, preferred_element_type=jnp.float32)
        + up_bias
    )
    activated, gelu_pull = jax.vjp(jax.nn.gelu, expanded)
    activated_low = activated.astype(jnp.bfloat16)
    output = (
        residual
        + jnp.einsum("sti,ij->stj", activated_low, down_weight, preferred_element_type=jnp.float32)
        + down_bias
    )
    upstream = cotangent.astype(jnp.float32)
    down_grad = jnp.einsum(
        "sti,stj->ij", activated_low, cotangent, preferred_element_type=jnp.float32
    )
    down_bias_grad = jnp.sum(upstream, axis=(0, 1))
    act_grad = jnp.einsum("stj,ij->sti", cotangent, down_weight, preferred_element_type=jnp.float32)
    (expanded_grad,) = gelu_pull(act_grad)
    expanded_low = expanded_grad.astype(jnp.bfloat16)
    up_grad = jnp.einsum(
        "sti,stj->ij", normed_two_low, expanded_low, preferred_element_type=jnp.float32
    )
    up_bias_grad = jnp.sum(expanded_low.astype(jnp.float32), axis=(0, 1))
    normed_two_grad = jnp.einsum(
        "stj,ij->sti", expanded_low, up_weight, preferred_element_type=jnp.float32
    )
    residual_part, second_gain_grad, second_bias_grad = second_pull(normed_two_grad)
    residual_grad = upstream + residual_part
    residual_low = residual_grad.astype(jnp.bfloat16)
    out_grad = jnp.einsum(
        "sti,stj->ij", branch_low, residual_low, preferred_element_type=jnp.float32
    )
    out_bias_grad = jnp.sum(residual_low.astype(jnp.float32), axis=(0, 1))
    branch_grad = jnp.einsum(
        "stj,ij->sti", residual_low, out_weight, preferred_element_type=jnp.float32
    )
    conv_grad = branch_grad * outer_gate
    outer_grad = branch_grad * convolved
    skip_bias_grad = jnp.sum(conv_grad * gated, axis=(0, 1))
    conv_grad_chan = lax.all_to_all(
        jnp.swapaxes(conv_grad, 1, 2), "seq", split_axis=1, concat_axis=2, tiled=True
    )
    grad_real, grad_imag = forward_transform(
        conv_grad_chan.reshape(seq_count * chans, parts, tok_count), tables
    )
    grad_real = grad_real.reshape(spectral)
    grad_imag = grad_imag.reshape(spectral)
    back_real = kernel_real * grad_real + kernel_imag * grad_imag
    back_imag = kernel_real * grad_imag - kernel_imag * grad_real
    gated_back_chan = inverse_transform(
        back_real.reshape(-1, 2 * parts, tok_count),
        back_imag.reshape(-1, 2 * parts, tok_count),
        tables,
    )
    gated_back_chan = gated_back_chan.reshape(seq_count, chans, length)
    tap_real = jnp.sum(gated_real * grad_real + gated_imag * grad_imag, axis=0)
    tap_imag = jnp.sum(gated_real * grad_imag - gated_imag * grad_real, axis=0)
    kernel_grad = inverse_transform(tap_real, tap_imag, tables).reshape(chans, length)
    gated_back = jnp.swapaxes(
        lax.all_to_all(gated_back_chan, "seq", split_axis=2, concat_axis=1, tiled=True), 1, 2
    )
    gated_grad = (gated_back + conv_grad * skip_bias) * live
    value_grad = gated_grad * inner_gate
    inner_grad = gated_grad * values
    filtered_grad = jnp.concatenate([outer_grad, inner_grad, value_grad], axis=2)
    following = passed_along(filtered_grad[:, :2, :], "seq", -1)
    grad_extended = jnp.concatenate([filtered_grad, following], axis=1)
    mixed_grad = (
        short_filter[:, 2] * grad_extended[:, :tok_count]
        + short_filter[:, 1] * grad_extended[:, 1 : tok_count + 1]
        + short_filter[:, 0] * grad_extended[:, 2:]
    )
    filter_grad = jnp.stack(
        [
            jnp.sum(filtered_grad * extended[:, position : position + tok_count], axis=(0, 1))
            for position in range(3)
        ],
        axis=1,
    )
    short_bias_grad = jnp.sum(filtered_grad, axis=(0, 1))
    mixed_low = mixed_grad.astype(jnp.bfloat16)
    proj_grad = jnp.einsum("sti,stj->ij", normed_low, mixed_low, preferred_element_type=jnp.float32)
    proj_bias_grad = jnp.sum(mixed_low.astype(jnp.float32), axis=(0, 1))
    normed_grad = jnp.einsum(
        "stj,ij->sti", mixed_low, proj_weight, preferred_element_type=jnp.float32
    )
    hidden_part, norm_gain_grad, norm_bias_grad = norm_pull(normed_grad)
    input_grad = residual_grad + hidden_part
    (
        norm_gain_share,
        norm_bias_share,
        proj_share,
        proj_bias_share,
        filter_share,
        short_bias_share,
        skip_share,
        out_share,
        out_bias_share,
        second_gain_share,
        second_bias_share,
        up_share,
        up_bias_share,
        down_share,
        down_bias_share,
    ) = (
        lax.psum_scatter(norm_gain_grad, "seq", scatter_dimension=0, tiled=True),
        lax.psum_scatter(norm_bias_grad, "seq", scatter_dimension=0, tiled=True),
        lax.psum_scatter(proj_grad, "seq", scatter_dimension=0, tiled=True),
        lax.psum_scatter(proj_bias_grad, "seq", scatter_dimension=0, tiled=True),
        lax.psum_scatter(filter_grad, "seq", scatter_dimension=0, tiled=True),
        lax.psum_scatter(short_bias_grad, "seq", scatter_dimension=0, tiled=True),
        lax.psum_scatter(skip_bias_grad, "seq", scatter_dimension=0, tiled=True),
        lax.psum_scatter(out_grad, "seq", scatter_dimension=0, tiled=True),
        lax.psum_scatter(out_bias_grad, "seq", scatter_dimension=0, tiled=True),
        lax.psum_scatter(second_gain_grad, "seq", scatter_dimension=0, tiled=True),
        lax.psum_scatter(second_bias_grad, "seq", scatter_dimension=0, tiled=True),
        lax.psum_scatter(up_grad, "seq", scatter_dimension=0, tiled=True),
        lax.psum_scatter(up_bias_grad, "seq", scatter_dimension=0, tiled=True),
        lax.psum_scatter(down_grad, "seq", scatter_dimension=0, tiled=True),
        lax.psum_scatter(down_bias_grad, "seq", scatter_dimension=0, tiled=True),
    )
    (
        norm_gain_grad,
        norm_bias_grad,
        proj_grad,
        proj_bias_grad,
        filter_grad,
        short_bias_grad,
        skip_bias_grad,
        out_grad,
        out_bias_grad,
        second_gain_grad,
        second_bias_grad,
        up_grad,
        up_bias_grad,
        down_grad,
        down_bias_grad,
        kernel_grad,
    ) = lax.psum(
        (
            norm_gain_share,
            norm_bias_share,
            proj_share,
            proj_bias_share,
            filter_share,
            short_bias_share,
            skip_share,
            out_share,
            out_bias_share,
            second_gain_share,
            second_bias_share,
            up_share,
            up_bias_share,
            down_share,
            down_bias_share,
            kernel_grad,
        ),
        "dp",
    )
    return (
        output,
        input_grad,
        norm_gain_grad,
        norm_bias_grad,
        proj_grad,
        proj_bias_grad,
        filter_grad,
        short_bias_grad,
        kernel_grad,
        skip_bias_grad,
        out_grad,
        out_bias_grad,
        second_gain_grad,
        second_bias_grad,
        up_grad,
        up_bias_grad,
        down_grad,
        down_bias_grad,
    )


def block_tables(width):
    def stacked(matrix):
        high = matrix.astype(np.float32).astype(ml_dtypes.bfloat16)
        low = (matrix - high.astype(np.float64)).astype(ml_dtypes.bfloat16)
        return np.concatenate([high, high, low], axis=1)

    odd = 2 * np.arange(width) + 1
    angles = np.pi / (2 * width) * (odd[:, None] * np.arange(width)[None, :] % (4 * width))
    analysis = np.concatenate([np.cos(angles), -np.sin(angles)], axis=0)
    angles = np.pi / (2 * width) * (np.arange(2 * width)[:, None] * odd[None, :] % (4 * width))
    synthesis = np.concatenate([np.cos(angles), -np.sin(angles)], axis=1) / width
    return stacked(analysis), stacked(synthesis)


def in_parts(values):
    high = values.astype(jnp.bfloat16)
    low = (values - high.astype(jnp.float32)).astype(jnp.bfloat16)
    return high, low


def short_filtered(padded_ref, mixed_ref, taps):
    count, lanes = mixed_ref.shape
    padded_ref[:8] = jnp.zeros((8, lanes), jnp.float32)
    padded_ref[8 : 8 + count] = mixed_ref[...]
    return (
        taps[0:1] * padded_ref[6 : 6 + count]
        + taps[1:2] * padded_ref[7 : 7 + count]
        + taps[2:3] * mixed_ref[...]
        + taps[3:4]
    )


def analyse(signal, table_ref, spectra_ref):
    blocks, double, lanes = spectra_ref.shape
    width = double // 2
    high, low = in_parts(signal)
    for first in range(0, blocks, 2):
        columns = []
        for block in (first, first + 1):
            rows = slice(block * width, (block + 1) * width)
            columns.append(jnp.concatenate([high[rows], low[rows], high[rows]], axis=0))
        found = jnp.dot(
            table_ref[...], jnp.concatenate(columns, axis=1), preferred_element_type=jnp.float32
        )
        spectra_ref[first] = found[:, :lanes]
        spectra_ref[first + 1] = found[:, lanes:]


def analyse_kernel(kernel_ref, table_ref, spectra_ref):
    blocks, double, lanes = spectra_ref.shape
    for first in range(0, blocks, 2):
        rows = []
        for block in (first, first + 1):
            high, low = in_parts(kernel_ref[block])
            rows.append(jnp.concatenate([high, low, high], axis=1))
        found = lax.dot_general(
            table_ref[...],
            jnp.concatenate(rows, axis=0),
            (((1,), (1,)), ((), ())),
            preferred_element_type=jnp.float32,
        )
        spectra_ref[first] = found[:, :lanes]
        spectra_ref[first + 1] = found[:, lanes:]


def synthesise(spectra_ref, table_ref):
    blocks, double, lanes = spectra_ref.shape
    found = []
    for first in range(0, blocks, 2):
        columns = []
        for block in (first, first + 1):
            high, low = in_parts(spectra_ref[block])
            columns.append(jnp.concatenate([high, low, high], axis=0))
        pair = jnp.dot(
            table_ref[...], jnp.concatenate(columns, axis=1), preferred_element_type=jnp.float32
        )
        found.append(pair[:, :lanes])
        found.append(pair[:, lanes:])
    return found


def multiply(left_ref, right_ref, out_ref, reverse):
    blocks, double, lanes = out_ref.shape
    width = double // 2

    def step(index, carry):
        real_rows = pl.ds(pl.multiple_of(index * 8, 8), 8)
        imag_rows = pl.ds(pl.multiple_of(width + index * 8, 8), 8)
        left_real = [left_ref[block, real_rows] for block in range(blocks)]
        left_imag = [left_ref[block, imag_rows] for block in range(blocks)]
        right_real = [right_ref[block, real_rows] for block in range(blocks)]
        right_imag = [right_ref[block, imag_rows] for block in range(blocks)]
        left_sum = [
            real - imag if reverse else real + imag for real, imag in zip(left_real, left_imag)
        ]
        right_sum = [real + imag for real, imag in zip(right_real, right_imag)]
        right_gap = [imag - real for real, imag in zip(right_real, right_imag)]
        for m in range(blocks):
            one = two = three = 0.0
            for l in range(blocks - m if reverse else m + 1):
                r = m + l if reverse else m - l
                one = one + right_real[r] * left_sum[l]
                two = two + left_real[l] * right_gap[r]
                three = three + left_imag[l] * right_sum[r]
            out_ref[m, real_rows] = one + three if reverse else one - three
            out_ref[m, imag_rows] = one + two
        return carry

    lax.fori_loop(0, width // 8, step, 0, unroll=2)


def gates(start_ref, mixed_refs, taps_ref, padded_ref):
    outer, inner, values = [
        short_filtered(padded_ref.at[group], ref, taps_ref[group])
        for group, ref in enumerate(mixed_refs)
    ]
    rows = lax.broadcasted_iota(jnp.int32, outer.shape, 0)
    live = (rows >= start_ref[0]).astype(jnp.float32)
    return outer, inner, values, live


def forward_kernel(
    start_ref,
    outer_ref,
    inner_ref,
    value_ref,
    kernel_ref,
    taps_ref,
    skip_ref,
    analysis_ref,
    synthesis_ref,
    convolved_ref,
    branch_ref,
    signal_spectra,
    kernel_spectra,
    spectra,
    padded,
):
    width = kernel_ref.shape[2]
    outer, inner, values, live = gates(start_ref, (outer_ref, inner_ref, value_ref), taps_ref, padded)
    gated = values * inner * live
    analyse(gated, analysis_ref, signal_spectra)
    analyse_kernel(kernel_ref, analysis_ref, kernel_spectra)
    multiply(kernel_spectra, signal_spectra, spectra, False)
    found = synthesise(spectra, synthesis_ref)
    pieces = [found[0][:width]]
    for block in range(1, len(found)):
        pieces.append(found[block][:width] + found[block - 1][width:])
    convolved = jnp.concatenate(pieces, axis=0) + gated * skip_ref[...]
    convolved_ref[...] = convolved
    branch_ref[...] = (convolved * outer).astype(jnp.bfloat16)


def lag_blocks(found, width):
    pieces = []
    for block in range(len(found)):
        piece = found[block][:width]
        if block + 1 < len(found):
            piece = piece - found[block + 1][width:]
        pieces.append(piece)
    return pieces


def backward_kernel(
    start_ref,
    grad_ref,
    convolved_ref,
    outer_ref,
    inner_ref,
    value_ref,
    kernel_ref,
    taps_ref,
    skip_ref,
    analysis_ref,
    synthesis_ref,
    mixed_grad_ref,
    kernel_kept_ref,
    kernel_given_ref,
    sums_ref,
    signal_spectra,
    kernel_spectra,
    grad_spectra,
    spectra,
    padded,
):
    width = kernel_ref.shape[2]
    mixed_refs = (outer_ref, inner_ref, value_ref)
    outer, inner, values, live = gates(start_ref, mixed_refs, taps_ref, padded)
    gated = values * inner * live
    branch_grad = grad_ref[...]
    conv_grad = branch_grad * outer
    outer_grad = branch_grad * convolved_ref[...]
    analyse(gated, analysis_ref, signal_spectra)
    analyse_kernel(kernel_ref, analysis_ref, kernel_spectra)
    analyse(conv_grad, analysis_ref, grad_spectra)
    multiply(signal_spectra, grad_spectra, spectra, True)
    lags = lag_blocks(synthesise(spectra, synthesis_ref), width)
    half = len(lags) // 2
    first = start_ref[1] == 0
    for block in range(half):
        columns = slice(block * width, (block + 1) * width)
        one, two = lags[block].T, lags[half + block].T
        kernel_kept_ref[:, columns] = jnp.where(first, one, two)
        kernel_given_ref[:, columns] = jnp.where(first, two, one)
    multiply(kernel_spectra, grad_spectra, spectra, True)
    back = jnp.concatenate(lag_blocks(synthesise(spectra, synthesis_ref), width), axis=0)
    gated_grad = (back + conv_grad * skip_ref[...]) * live

    def total(array):
        return jnp.sum(array, axis=0, keepdims=True)

    count = outer.shape[0]
    filter_rows, bias_rows, low_rows = [], [], []
    grads = (outer_grad, gated_grad * values, gated_grad * inner)
    for group in range(3):
        grad, mixed, taps = grads[group], mixed_refs[group][...], taps_ref[group]
        padded[group, :count] = grad
        padded[group, count : count + 8] = jnp.zeros((8, grad.shape[1]), jnp.float32)
        next_one, next_two = padded[group, 1 : 1 + count], padded[group, 2 : 2 + count]
        mixed_grad = taps[2:3] * grad + taps[1:2] * next_one + taps[0:1] * next_two
        low = mixed_grad.astype(jnp.bfloat16)
        mixed_grad_ref[group] = low
        filter_rows.append([total(next_two * mixed), total(next_one * mixed), total(grad * mixed)])
        bias_rows.append(total(grad))
        low_rows.append(total(low.astype(jnp.float32)))
    rows = [filter_rows[group][tap] for tap in range(3) for group in range(3)]
    rows = rows + bias_rows + low_rows + [total(conv_grad * gated)]
    sums_ref[...] = jnp.concatenate(rows, axis=0)


def kernel_parameters(mebibytes=56):
    return pltpu.CompilerParams(vmem_limit_bytes=mebibytes * 1024 * 1024)


def kernel_specs(tokens, parts, width, lanes, features):
    groups = features // lanes

    def mixed(group):
        return pl.BlockSpec((tokens, lanes), lambda tile, *_: (0, group * groups + tile))

    return (
        [pl.BlockSpec(memory_space=pltpu.SMEM)],
        [mixed(0), mixed(1), mixed(2)],
        [
            pl.BlockSpec((parts, lanes, width), lambda tile, *_: (0, tile, 0)),
            pl.BlockSpec((3, 4, lanes), lambda tile, *_: (0, 0, tile)),
            pl.BlockSpec((1, lanes), lambda tile, *_: (0, tile)),
            pl.BlockSpec((2 * width, 3 * width), lambda *_: (0, 0)),
            pl.BlockSpec((2 * width, 6 * width), lambda *_: (0, 0)),
        ],
        pl.BlockSpec((tokens, lanes), lambda tile, *_: (0, tile)),
        pltpu.VMEM((parts, 2 * width, lanes), jnp.float32),
    )


def forward_convolution(start, mixed, kernel, taps, skip, tables, lanes=128):
    parts, features, width = kernel.shape
    tokens = mixed.shape[0]
    start_spec, mixed_specs, rest, plain, spectra = kernel_specs(tokens, parts, width, lanes, features)
    return pl.pallas_call(
        forward_kernel,
        grid=(features // lanes,),
        in_specs=start_spec + mixed_specs + rest,
        out_specs=(plain, plain),
        out_shape=(
            jax.ShapeDtypeStruct((tokens, features), jnp.float32),
            jax.ShapeDtypeStruct((tokens, features), jnp.bfloat16),
        ),
        scratch_shapes=[spectra] * 3 + [pltpu.VMEM((3, tokens + 8, lanes), jnp.float32)],
        compiler_params=kernel_parameters(),
        cost_estimate=NO_COST,
        name="forward_convolution",
    )(start, mixed, mixed, mixed, kernel, taps, skip, *tables)


def backward_convolution(start, grad, convolved, mixed, kernel, taps, skip, tables, lanes=128):
    parts, features, width = kernel.shape
    tokens = mixed.shape[0]
    start_spec, mixed_specs, rest, plain, spectra = kernel_specs(tokens, parts, width, lanes, features)
    return pl.pallas_call(
        backward_kernel,
        grid=(features // lanes,),
        in_specs=start_spec + [plain, plain] + mixed_specs + rest,
        out_specs=(
            pl.BlockSpec((3, tokens, lanes), lambda tile: (0, 0, tile)),
            pl.BlockSpec((lanes, tokens // 2), lambda tile: (tile, 0)),
            pl.BlockSpec((lanes, tokens // 2), lambda tile: (tile, 0)),
            pl.BlockSpec((16, lanes), lambda tile: (0, tile)),
        ),
        out_shape=(
            jax.ShapeDtypeStruct((3, tokens, features), jnp.bfloat16),
            jax.ShapeDtypeStruct((features, tokens // 2), jnp.float32),
            jax.ShapeDtypeStruct((features, tokens // 2), jnp.float32),
            jax.ShapeDtypeStruct((16, features), jnp.float32),
        ),
        scratch_shapes=[spectra] * 4 + [pltpu.VMEM((3, tokens + 8, lanes), jnp.float32)],
        compiler_params=kernel_parameters(),
        cost_estimate=NO_COST,
        name="backward_convolution",
    )(start, grad, convolved, mixed, mixed, mixed, kernel, taps, skip, *tables)


def unit_rows(values):
    centered = values - jnp.mean(values, axis=-1, keepdims=True)
    spread = lax.rsqrt(jnp.mean(centered * centered, axis=-1, keepdims=True) + EPSILON)
    return centered * spread, spread


def unit_rows_back(grad, unit, spread, gain):
    scaled = grad * gain
    inner = scaled - jnp.mean(scaled, axis=-1, keepdims=True)
    return (inner - unit * jnp.mean(scaled * unit, axis=-1, keepdims=True)) * spread


def matmul(left, right):
    return jnp.dot(left, right, preferred_element_type=jnp.float32)


def matmul_back(left, right):
    return lax.dot_general(left, right, (((1,), (1,)), ((), ())), preferred_element_type=jnp.float32)


def columns_of(array, refs):
    first = 0
    for ref in refs:
        ref[...] = array[:, first : first + ref.shape[1]]
        first += ref.shape[1]


def column_sums(array):
    return jnp.sum(array, axis=0, keepdims=True)


def project_kernel(x_ref, gain_ref, bias_ref, weight_ref, offset_ref, normed_ref, mixed_ref):
    unit, _ = unit_rows(x_ref[...])
    normed = (unit * gain_ref[...] + bias_ref[...]).astype(jnp.bfloat16)
    normed_ref[...] = normed
    mixed_ref[...] = matmul(normed, weight_ref[...]) + offset_ref[...]


def feed_kernel(
    x_ref,
    branch_ref,
    out_weight_ref,
    out_bias_ref,
    gain_ref,
    bias_ref,
    up_weight_ref,
    up_bias_ref,
    down_weight_ref,
    down_bias_ref,
    residual_ref,
    normed_ref,
    activated_ref,
    slope_ref,
    *output_refs,
):
    residual = x_ref[...] + matmul(branch_ref[...], out_weight_ref[...]) + out_bias_ref[...]
    residual_ref[...] = residual
    unit, _ = unit_rows(residual)
    normed = (unit * gain_ref[...] + bias_ref[...]).astype(jnp.bfloat16)
    normed_ref[...] = normed
    total = residual + down_bias_ref[...]
    factor = math.sqrt(2.0 / math.pi)
    chunk = residual.shape[1]
    for first in range(0, up_weight_ref.shape[1], chunk):
        columns = slice(first, first + chunk)
        expanded = matmul(normed, up_weight_ref[:, columns]) + up_bias_ref[:, columns]
        square = expanded * expanded
        turned = jnp.tanh(factor * (expanded + 0.044715 * (square * expanded)))
        half = 0.5 + 0.5 * turned
        activated = (expanded * half).astype(jnp.bfloat16)
        activated_ref[:, columns] = activated
        slope_ref[:, columns] = half + (0.5 * factor) * expanded * (1.0 - turned * turned) * (
            1.0 + (3 * 0.044715) * square
        )
        total = total + matmul(activated, down_weight_ref[columns, :])
    columns_of(total, output_refs)


def feed_back_kernel(
    grad_ref,
    residual_ref,
    slope_ref,
    gain_ref,
    out_weight_ref,
    up_weight_ref,
    down_weight_ref,
    expanded_ref,
    residual_grad_ref,
    residual_low_ref,
    branch_grad_ref,
    sums_ref,
    wide_sums_ref,
):
    grad = grad_ref[...]
    grad_low = grad.astype(jnp.bfloat16)
    chunk = grad.shape[1]
    normed_grad = None
    wide = []
    for first in range(0, up_weight_ref.shape[1], chunk):
        columns = slice(first, first + chunk)
        expanded = matmul_back(grad_low, down_weight_ref[columns, :]) * slope_ref[:, columns]
        low = expanded.astype(jnp.bfloat16)
        expanded_ref[:, columns] = low
        wide.append(column_sums(low.astype(jnp.float32)))
        part = matmul_back(low, up_weight_ref[:, columns])
        normed_grad = part if normed_grad is None else normed_grad + part
    unit, spread = unit_rows(residual_ref[...])
    residual_grad = grad + unit_rows_back(normed_grad, unit, spread, gain_ref[...])
    residual_grad_ref[...] = residual_grad
    low = residual_grad.astype(jnp.bfloat16)
    residual_low_ref[...] = low
    branch_grad_ref[...] = matmul_back(low, out_weight_ref[...])
    sums = [
        column_sums(normed_grad * unit),
        column_sums(normed_grad),
        column_sums(low.astype(jnp.float32)),
        column_sums(grad),
    ]

    @pl.when(pl.program_id(0) == 0)
    def _():
        sums_ref[...] = jnp.zeros_like(sums_ref)
        wide_sums_ref[...] = jnp.zeros_like(wide_sums_ref)

    sums_ref[...] += jnp.concatenate(sums, axis=0)
    wide_sums_ref[...] += jnp.concatenate(wide, axis=1)


def input_grad_kernel(
    mixed_ref, weight_ref, x_ref, gain_ref, residual_grad_ref, first_ref, second_ref, sums_ref
):
    features = x_ref.shape[1]
    normed_grad = None
    for group in range(3):
        columns = slice(group * features, (group + 1) * features)
        part = matmul_back(mixed_ref[group], weight_ref[:, columns])
        normed_grad = part if normed_grad is None else normed_grad + part
    unit, spread = unit_rows(x_ref[...])
    total = residual_grad_ref[...] + unit_rows_back(normed_grad, unit, spread, gain_ref[...])
    columns_of(total, (first_ref, second_ref))
    sums = jnp.concatenate([column_sums(normed_grad * unit), column_sums(normed_grad)], axis=0)

    @pl.when(pl.program_id(0) == 0)
    def _():
        sums_ref[...] = jnp.zeros_like(sums_ref)

    sums_ref[...] += sums


def by_rows(kernel, name, rows, inputs, outputs, height=256):
    def spec(shape, held):
        if len(shape) == 3:
            return pl.BlockSpec((shape[0], height, shape[2]), lambda step: (0, step, 0))
        if shape[0] == rows and not held:
            return pl.BlockSpec((height, shape[1]), lambda step: (step, 0))
        return pl.BlockSpec(shape, lambda step: (0, 0))

    return pl.pallas_call(
        kernel,
        grid=(rows // height,),
        in_specs=[spec(array.shape, held) for array, held in inputs],
        out_specs=tuple(spec(shape, False) for shape, _ in outputs),
        out_shape=tuple(jax.ShapeDtypeStruct(shape, kind) for shape, kind in outputs),
        compiler_params=kernel_parameters(),
        cost_estimate=NO_COST,
        name=name,
    )(*[array for array, _ in inputs])


def product_kernel(half_ref, left_ref, right_ref, out_ref):
    out_ref[...] = product_tile(left_ref, right_ref)


def product_tile(left_ref, right_ref):
    if len(right_ref.shape) == 2:
        return product(left_ref[...], right_ref[...].astype(jnp.bfloat16))
    return jnp.concatenate(
        [product(left_ref[...], right_ref[group]) for group in range(right_ref.shape[0])], axis=1
    )


def product_specs(left, right, tile):
    tokens = left.shape[0]
    half = right.shape[-1] // 2
    left_spec = pl.BlockSpec((tokens, tile), lambda step, half_ref: (0, step))
    if right.ndim == 2:
        right_spec = pl.BlockSpec((tokens, half), lambda step, half_ref: (0, half_ref[0]))
        return half, left_spec, right_spec
    right_spec = pl.BlockSpec((right.shape[0], tokens, half), lambda step, half_ref: (0, 0, half_ref[0]))
    return half * right.shape[0], left_spec, right_spec


def half_product(left, right, half, tile=384):
    rows = left.shape[1]
    columns, left_spec, right_spec = product_specs(left, right, tile)
    return pl.pallas_call(
        product_kernel,
        grid_spec=pltpu.PrefetchScalarGridSpec(
            num_scalar_prefetch=1,
            grid=(rows // tile,),
            in_specs=[left_spec, right_spec],
            out_specs=pl.BlockSpec((tile, columns), lambda step, half_ref: (step, 0)),
        ),
        out_shape=jax.ShapeDtypeStruct((rows, columns), jnp.float32),
        compiler_params=kernel_parameters(),
        cost_estimate=NO_COST,
        name="half_product",
    )(half, left, right)


def whole_product_kernel(left_ref, right_ref, out_ref):
    out_ref[...] = product(left_ref[...], right_ref[...])


def whole_product(left, right):
    tokens, rows = left.shape
    return pl.pallas_call(
        whole_product_kernel,
        grid=(right.shape[1] // rows,),
        in_specs=[
            pl.BlockSpec((tokens, rows), lambda step: (0, 0)),
            pl.BlockSpec((tokens, rows), lambda step: (0, step)),
        ],
        out_specs=pl.BlockSpec((rows, rows), lambda step: (0, step)),
        out_shape=jax.ShapeDtypeStruct((rows, right.shape[1]), jnp.float32),
        compiler_params=kernel_parameters(),
        cost_estimate=NO_COST,
        name="whole_product",
    )(left, right)


def parted_product_kernel(bits_ref, left_ref, right_ref, taken_ref, *out_refs):
    total = product_tile(left_ref, right_ref) + taken_ref[...]
    left = 0
    for part in range(len(out_refs) // 2):
        kept_ref, given_ref = out_refs[2 * part : 2 * part + 2]
        pieces, rows, columns = kept_ref.shape
        first = bits_ref[1 + part] == 0
        for piece in range(pieces):
            one = total[2 * piece * rows : (2 * piece + 1) * rows, left : left + columns]
            two = total[(2 * piece + 1) * rows : (2 * piece + 2) * rows, left : left + columns]
            kept_ref[piece] = jnp.where(first, one, two)
            given_ref[piece] = jnp.where(first, two, one)
        left += columns


def parted_product(left, right, half, taken, plan, tile=384):
    rows = left.shape[1]
    columns, left_spec, right_spec = product_specs(left, right, tile)
    steps = rows // tile
    specs, shapes = [], []
    for _, pieces in plan:
        shape = (pieces, rows // (2 * pieces), columns // len(plan))
        block = (pieces // steps,) + shape[1:]
        specs += [pl.BlockSpec(block, lambda step, bits_ref: (step, 0, 0))] * 2
        shapes += [jax.ShapeDtypeStruct(shape, jnp.float32)] * 2
    return pl.pallas_call(
        parted_product_kernel,
        grid_spec=pltpu.PrefetchScalarGridSpec(
            num_scalar_prefetch=1,
            grid=(steps,),
            in_specs=[
                left_spec,
                right_spec,
                pl.BlockSpec((tile, columns), lambda step, bits_ref: (step, 0)),
            ],
            out_specs=tuple(specs),
        ),
        out_shape=tuple(shapes),
        compiler_params=kernel_parameters(),
        cost_estimate=NO_COST,
        name="parted_product",
    )(jnp.concatenate([half] + [which for which, _ in plan]), left, right, taken)


def fold_kernel(bit_ref, *refs):
    *sources, kept_ref, given_ref = refs
    first = bit_ref[0] == 0
    height, lane = kept_ref.shape[1], 0
    for kept, taken in zip(sources[::2], sources[1::2]):
        total = kept[...] + taken[...]
        for row in range(0, total.shape[1], height):
            columns = slice(lane, lane + total.shape[2])
            one, two = total[0, row : row + height], total[1, row : row + height]
            kept_ref[0, :, columns] = jnp.where(first, one, two)
            given_ref[0, :, columns] = jnp.where(first, two, one)
            lane += total.shape[2]


def fold(pairs, which, height):
    count = pairs[0][0].shape[0]
    operands, specs, columns = [], [], 0
    for kept, taken, *share in pairs:
        place, shares = share if share else (0, 1)
        block = (2, kept.shape[1], kept.shape[2] // shares)
        operands += [kept, taken]
        specs += [pl.BlockSpec(block, lambda step, place=place: (step, 0, place))] * 2
        columns += block[1] // height * block[2]
    one = pl.BlockSpec((1, height, columns), lambda step: (step, 0, 0))
    shape = jax.ShapeDtypeStruct((count // 2, height, columns), jnp.float32)
    return pl.pallas_call(
        fold_kernel,
        grid=(count // 2,),
        in_specs=[pl.BlockSpec(memory_space=pltpu.SMEM)] + specs,
        out_specs=(one, one),
        out_shape=(shape, shape),
        compiler_params=kernel_parameters(24),
        cost_estimate=NO_COST,
        name="fold",
    )(which, *operands)


def unpack_kernel(bits_ref, own_ref, y_ref, core_ref, both_ref, *out_refs):
    core_first, y_first = bits_ref[0] == 0, bits_ref[1] == 0
    own, beside = own_ref[...], y_ref[...]
    mine = [jnp.where(y_first, own, beside), jnp.where(y_first, beside, own)]
    own, beside = core_ref[...], both_ref[...]
    theirs = [jnp.where(y_first, own, beside), jnp.where(y_first, beside, own)]
    height = own.shape[0]
    for y in range(2):
        for core in range(2):
            block = jnp.where(core_first, mine[y], theirs[y])
            if core == 1:
                block = jnp.where(core_first, theirs[y], mine[y])
            lane = 0
            for ref in out_refs:
                rows, columns = ref.shape
                if columns == 128:
                    ref[(2 * core + y) * height : (2 * core + y + 1) * height] = block[:, lane:]
                    continue
                groups = 3 if columns == 3 * height * 16 and rows == 2 * height else 1
                half = columns // (2 * groups)
                for place in range(rows // (2 * height)):
                    for group in range(groups):
                        top = y * (rows // 2) + place * height
                        left = group * 2 * half + core * half
                        ref[top : top + height, left : left + half] = block[:, lane : lane + half]
                        lane += half


def gathered(share):
    y_other, core_other = swapped(share, "dp", 2), swapped(share, "dp", 1)
    return share, y_other, core_other, swapped(y_other, "dp", 1)


def unpacked(shares, shapes):
    return pl.pallas_call(
        unpack_kernel,
        in_specs=[pl.BlockSpec(memory_space=pltpu.SMEM)] + [pl.BlockSpec(memory_space=pltpu.VMEM)] * 4,
        out_specs=[pl.BlockSpec(memory_space=pltpu.VMEM)] * len(shapes),
        out_shape=[jax.ShapeDtypeStruct(shape, jnp.float32) for shape in shapes],
        compiler_params=kernel_parameters(24),
        cost_estimate=NO_COST,
        name="unpack",
    )(jnp.concatenate([flag("dp", 1), flag("dp", 2)]), *shares)


def swapped(array, axis, by):
    count = lax.axis_size(axis)
    return lax.ppermute(array, axis, [(i, i ^ by) for i in range(count)])


def bit(axis, by):
    return (lax.axis_index(axis) // by) % 2


def doubled(array, dim, axis, by):
    other = swapped(array, axis, by)
    first = bit(axis, by) == 0
    return jnp.concatenate(
        [jnp.where(first, array, other), jnp.where(first, other, array)], axis=dim
    )


def product(left, columns):
    return lax.dot_general(left, columns, (((0,), (0,)), ((), ())), preferred_element_type=jnp.float32)


def flag(axis, by):
    return bit(axis, by).astype(jnp.int32).reshape(1)


def reduced(kept, given, steps):
    for (axis, by), following in zip(steps, steps[1:] + [None]):
        taken = swapped(given, axis, by)
        if following is None:
            return (kept + taken)[0]
        kept, given = fold([(kept, taken)], flag(*following), kept.shape[1])


def by_sequences(
    tokens,
    offsets,
    norm_gain,
    norm_bias,
    proj_weight,
    proj_bias,
    short_filter,
    short_bias,
    long_kernel,
    skip_bias,
    out_weight,
    out_bias,
    second_gain,
    second_bias,
    up_weight,
    up_bias,
    down_weight,
    down_bias,
    cotangent,
):
    parts, width, features = tokens.shape
    length = parts * width
    hidden_units = up_weight.shape[1]
    hold = lax.optimization_barrier
    tables = tuple(jnp.asarray(table) for table in block_tables(width))
    start = lax.dynamic_slice_in_dim(offsets, lax.axis_index("seq"), 1, 0)
    core, other_core = flag("dp", 1), 1 - flag("dp", 1)
    scalars = jnp.concatenate([start, core])
    low, single = jnp.bfloat16, jnp.float32
    y_step, x_step = ("dp", 2), ("seq", 1)
    z_steps = [("seq", 1 << place) for place in range(1, parts.bit_length() - 1)]

    share = features // 4
    chunk = bit("dp", 1) * 2 + bit("dp", 2)
    piece = lax.dynamic_slice_in_dim(long_kernel, chunk * share, share, 0)
    pieces = jnp.stack([piece] + [swapped(piece, "seq", by) for by in range(2, parts, 2)])
    z = lax.axis_index("seq") // 2
    pieces = jnp.concatenate(
        [lax.dynamic_index_in_dim(pieces, z ^ other, 0) for other in range(parts // 2)]
    )
    hidden, pieces = hold((tokens.astype(single), pieces))
    hidden = lax.all_to_all(hidden, "seq", 0, 0, tiled=True)
    pieces = doubled(pieces[:, None], 1, *x_step).reshape(parts, share, width)
    kernel = doubled(doubled(pieces, 1, "dp", 2), 1, "dp", 1)
    upstream = cotangent.astype(single)
    taps = jnp.concatenate([short_filter.T, short_bias[None]], axis=0)
    taps = jnp.swapaxes(taps.reshape(4, 3, features), 0, 1)
    skip = skip_bias[None]
    hidden, kernel, upstream, taps, scalars = hold((hidden, kernel, upstream, taps, scalars))

    upstream = lax.all_to_all(upstream, "seq", 0, 0, tiled=True)
    hidden = hidden.reshape(length, features)
    normed_low, mixed = by_rows(
        project_kernel,
        "project",
        length,
        [
            (hidden, False),
            (norm_gain[None], True),
            (norm_bias[None], True),
            (proj_weight, True),
            (proj_bias[None], True),
        ],
        [((length, features), low), ((length, 3 * features), single)],
    )
    convolved, branch_low = forward_convolution(scalars, mixed, kernel, taps, skip, tables)
    residual, normed_two_low, activated_low, slope, *output = by_rows(
        feed_kernel,
        "feed",
        length,
        [
            (hidden, False),
            (branch_low, False),
            (out_weight, True),
            (out_bias[None], True),
            (second_gain[None], True),
            (second_bias[None], True),
            (up_weight, True),
            (up_bias[None], True),
            (down_weight, True),
            (down_bias[None], True),
        ],
        [
            ((length, features), single),
            ((length, features), low),
            ((length, hidden_units), low),
            ((length, hidden_units), single),
            ((length, features // 3), single),
            ((length, features * 2 // 3), single),
        ],
    )
    upstream, output = hold((upstream, output))

    def sent(columns):
        columns = columns.reshape(parts, width, -1)
        return lax.all_to_all(columns, "seq", 0, 0, tiled=True)

    output[0] = sent(output[0])
    upstream = upstream.reshape(length, features)
    down_given = half_product(activated_low, upstream, other_core, 768)
    upstream, down_given = hold((upstream, down_given))
    down_taken = swapped(down_given, "dp", 1)
    expanded_low, residual_grad, residual_low, branch_grad, sums_two, wide_sums = by_rows(
        feed_back_kernel,
        "feed_back",
        length,
        [
            (upstream, False),
            (residual, False),
            (slope, False),
            (second_gain[None], True),
            (out_weight, True),
            (up_weight, True),
            (down_weight, True),
        ],
        [
            ((length, hidden_units), low),
            ((length, features), single),
            ((length, features), low),
            ((length, features), single),
            ((4, features), single),
            ((1, hidden_units), single),
        ],
    )
    expanded_low, residual_low, branch_grad = hold((expanded_low, residual_low, branch_grad))
    side = whole_product(normed_two_low, expanded_low)
    side, down_taken, output = hold((side, down_taken, output))
    side = lax.psum_scatter(side, ("seq", "dp"), scatter_dimension=0, tiled=True)
    down_kept, down_given = parted_product(
        activated_low, upstream, core, down_taken, [(flag(*y_step), parts)], 768
    )
    branch_grad, down_given = hold((branch_grad, down_given))

    output[1] = sent(output[1])
    down_taken = swapped(down_given, *y_step)
    mixed_low, kernel_kept, kernel_given, sums = backward_convolution(
        scalars, branch_grad, convolved, mixed, kernel, taps, skip, tables
    )
    proj_given = half_product(normed_low, mixed_low, other_core)
    *input_grad, sums_one = by_rows(
        input_grad_kernel,
        "input_grad",
        length,
        [
            (mixed_low, False),
            (proj_weight, True),
            (hidden, False),
            (norm_gain[None], True),
            (residual_grad, False),
        ],
        [
            ((length, features * 2 // 3), single),
            ((length, features // 3), single),
            ((2, features), single),
        ],
    )
    input_grad, mixed_low, proj_given, kernel_given, down_taken, sums_one, sums, output = hold(
        (input_grad, mixed_low, proj_given, kernel_given, down_taken, sums_one, sums, output)
    )

    rows = features // (2 * parts)
    input_grad[0] = sent(input_grad[0])
    down_kept, down_given = fold([(down_kept, down_taken)], flag(*x_step), down_kept.shape[1])
    down_taken = swapped(down_given, *x_step)
    kernel_taken = swapped(kernel_given, "dp", 1)
    proj_taken = swapped(proj_given, "dp", 1)
    proj_kept, proj_given = parted_product(
        normed_low, mixed_low, core, proj_taken, [(flag(*y_step), parts)]
    )
    proj_given, residual_low = hold((proj_given, residual_low))
    proj_taken = swapped(proj_given, *y_step)
    out_given = half_product(branch_low, residual_low, other_core, 768)
    out_taken = swapped(out_given, "dp", 1)
    out_kept, out_given = parted_product(
        branch_low, residual_low, core, out_taken, [(flag(*y_step), parts)], 768
    )
    output = jnp.concatenate(output, axis=2)
    vectors = [sums_one[0], sums_one[1]]
    vectors += [sums[first : first + 3].reshape(-1) for first in range(0, 15, 3)]
    vectors += [sums[15], sums_two[2], sums_two[0], sums_two[1], wide_sums[0], sums_two[3]]
    sizes = [vector.shape[0] // parts for vector in vectors]
    packed = jnp.concatenate([vector.reshape(parts, -1) for vector in vectors], axis=1)
    packed = jnp.pad(packed, ((0, 0), (0, 4 * rows * 128 - packed.shape[1])))
    packed = packed.reshape(parts, 2, 2 * rows, 128)
    packed_kept = lax.dynamic_index_in_dim(packed, core[0], 1, keepdims=False)
    packed_given = lax.dynamic_index_in_dim(packed, other_core[0], 1, keepdims=False)
    packed_taken = swapped(packed_given, "dp", 1)
    kernel_kept, kernel_taken = [
        array.reshape(parts, 2 * rows, -1) for array in (kernel_kept, kernel_taken)
    ]
    kernel_kept, kernel_taken, packed_kept, packed_taken = [
        array.reshape(2 * parts, rows, -1)
        for array in (kernel_kept, kernel_taken, packed_kept, packed_taken)
    ]
    rest_kept, rest_given = fold(
        [(kernel_kept, kernel_taken), (packed_kept, packed_taken)], flag(*y_step), rows
    )
    input_grad, down_taken, proj_taken, rest_given, out_given, output = hold(
        (input_grad, down_taken, proj_taken, rest_given, out_given, output)
    )

    input_grad[1] = sent(input_grad[1])
    rest_taken = swapped(rest_given, *y_step)
    out_taken = swapped(out_given, *y_step)
    proj_kept, proj_given = fold([(proj_kept, proj_taken)], flag(*x_step), rows)
    proj_taken = swapped(proj_given, *x_step)
    feed_kept, feed_given = fold([(down_kept, down_taken)], flag(*z_steps[0]), rows)
    feed_taken = swapped(feed_given, *z_steps[0])
    input_grad, proj_taken, rest_taken, out_taken, feed_taken = hold(
        (input_grad, proj_taken, rest_taken, out_taken, feed_taken)
    )

    rest_kept, rest_given = fold(
        [(out_kept, out_taken), (rest_kept, rest_taken)], flag(*x_step), rows
    )
    rest_given, feed_taken = hold((rest_given, feed_taken))
    rest_taken = swapped(rest_given, *x_step)
    feed_kept, feed_given = fold([(feed_kept, feed_taken)], flag(*z_steps[1]), rows)
    feed_taken = swapped(feed_given, *z_steps[1])
    input_grad = jnp.concatenate(input_grad, axis=2)
    mixer_kept, mixer_given = fold(
        [(proj_kept, proj_taken), (rest_kept, rest_taken)], flag(*z_steps[0]), rows
    )
    feed_kept, mixer_given = hold((feed_kept, mixer_given))
    mixer_taken = swapped(mixer_given, *z_steps[0])
    feed_share = (feed_kept + feed_taken)[0]
    feed_shares = gathered(feed_share)
    mixer_taken, input_grad, *feed_shares = hold((mixer_taken, input_grad, *feed_shares))
    mixer_kept, mixer_given = fold([(mixer_kept, mixer_taken)], flag(*z_steps[1]), rows)
    mixer_taken = swapped(mixer_given, *z_steps[1])
    (down_share,) = unpacked(feed_shares, [(hidden_units // parts, features)])
    side = lax.all_gather(side, "dp", axis=0, tiled=True)
    mixer_taken, down_share, up_share = hold((mixer_taken, down_share, side))
    mixer_share = (mixer_kept + mixer_taken)[0]
    proj_share, out_share, kernel_share, packed = unpacked(
        gathered(mixer_share),
        [
            (features // parts, 3 * features),
            (features // parts, features),
            (features // parts, length),
            (4 * rows, 128),
        ],
    )
    packed = packed.reshape(-1)
    ends = np.cumsum(sizes)
    vectors = [packed[end - size : end] for size, end in zip(sizes, ends)]
    return (
        output,
        input_grad,
        vectors[0],
        vectors[1],
        proj_share,
        vectors[6],
        jnp.stack(vectors[2:5], axis=1),
        vectors[5],
        kernel_share,
        vectors[7],
        out_share,
        vectors[8],
        vectors[9],
        vectors[10],
        up_share,
        vectors[11],
        down_share,
        vectors[12],
    )


def per_device(tokens, offsets, *rest):
    fits = (
        tokens.shape[0] == lax.axis_size("seq")
        and lax.axis_size("dp") == 4
        and tokens.shape[0] % 2 == 0
        and tokens.shape[1] % 128 == 0
        and lax.axis_size("seq") & (lax.axis_size("seq") - 1) == 0
    )
    plan = by_sequences if fits else by_channels
    return plan(tokens, offsets, *rest)


def solution(mesh):
    return jax.shard_map(
        per_device,
        mesh=mesh,
        in_specs=(
            P("dp", "seq", None),
            P("dp"),
            P(),
            P(),
            P(),
            P(),
            P(),
            P(),
            P(None, "seq"),
            P(),
            P(),
            P(),
            P(),
            P(),
            P(),
            P(),
            P(),
            P(),
            P("dp", "seq", None),
        ),
        out_specs=(
            P("dp", "seq", None),
            P("dp", "seq", None),
            P("seq"),
            P("seq"),
            P("seq", None),
            P("seq"),
            P("seq", None),
            P("seq"),
            P("seq", None),
            P("seq"),
            P("seq", None),
            P("seq"),
            P("seq"),
            P("seq"),
            P("seq", None),
            P("seq"),
            P("seq", None),
            P("seq"),
        ),
        check_vma=False,
    )
```

```python
import functools
import math

import jax
import jax.numpy as jnp
import ml_dtypes
import numpy as np
from jax import lax
from jax.experimental import pallas as pl
from jax.experimental.pallas import tpu as pltpu
from jax.sharding import PartitionSpec as P

EPSILON = 1e-05
PRECISE = lax.Precision.HIGHEST
NO_COST = pl.CostEstimate(flops=0, bytes_accessed=0, transcendentals=0)


def passed_along(array, axis, by):
    count = lax.axis_size(axis)
    pairs = [(i, i + by) for i in range(count) if 0 <= i + by < count]
    return lax.ppermute(array, axis, pairs)


def layer_norm(values, gain, offset):
    centered = values - jnp.mean(values, axis=-1, keepdims=True)
    spread = lax.rsqrt(jnp.mean(centered * centered, axis=-1, keepdims=True) + EPSILON)
    return centered * spread * gain + offset


def angle_table(rows, cols, modulus):
    product = (
        jnp.arange(rows, dtype=jnp.int32)[:, None]
        * jnp.arange(cols, dtype=jnp.int32)[None, :]
        % modulus
    )
    angles = product.astype(jnp.float32) * (2.0 * math.pi / modulus)
    return (jnp.cos(angles), jnp.sin(angles))


def fourier_tables(blocks, width):
    coarse_cos, coarse_sin = angle_table(blocks, 2 * blocks, 2 * blocks)
    twist_cos, twist_sin = angle_table(2 * blocks, width, 2 * blocks * width)
    fine_cos, fine_sin = angle_table(width, width, width)
    return (coarse_cos, coarse_sin, twist_cos, twist_sin, fine_cos, fine_sin)


def forward_transform(signal, tables):
    coarse_cos, coarse_sin, twist_cos, twist_sin, fine_cos, fine_sin = tables
    first_real = jnp.einsum("rpc,pk->rkc", signal, coarse_cos, precision=PRECISE)
    first_imag = -jnp.einsum("rpc,pk->rkc", signal, coarse_sin, precision=PRECISE)
    turned_real = first_real * twist_cos + first_imag * twist_sin
    turned_imag = first_imag * twist_cos - first_real * twist_sin
    spectrum_real = jnp.einsum(
        "rkc,cm->rkm", turned_real, fine_cos, precision=PRECISE
    ) + jnp.einsum("rkc,cm->rkm", turned_imag, fine_sin, precision=PRECISE)
    spectrum_imag = jnp.einsum(
        "rkc,cm->rkm", turned_imag, fine_cos, precision=PRECISE
    ) - jnp.einsum("rkc,cm->rkm", turned_real, fine_sin, precision=PRECISE)
    return (spectrum_real, spectrum_imag)


def inverse_transform(spectrum_real, spectrum_imag, tables):
    coarse_cos, coarse_sin, twist_cos, twist_sin, fine_cos, fine_sin = tables
    back_real = jnp.einsum("rkm,cm->rkc", spectrum_real, fine_cos, precision=PRECISE) - jnp.einsum(
        "rkm,cm->rkc", spectrum_imag, fine_sin, precision=PRECISE
    )
    back_imag = jnp.einsum("rkm,cm->rkc", spectrum_real, fine_sin, precision=PRECISE) + jnp.einsum(
        "rkm,cm->rkc", spectrum_imag, fine_cos, precision=PRECISE
    )
    turned_real = back_real * twist_cos - back_imag * twist_sin
    turned_imag = back_real * twist_sin + back_imag * twist_cos
    total = 2 * coarse_cos.shape[0] * twist_cos.shape[1]
    signal = jnp.einsum("rkc,pk->rpc", turned_real, coarse_cos, precision=PRECISE) - jnp.einsum(
        "rkc,pk->rpc", turned_imag, coarse_sin, precision=PRECISE
    )
    return signal / total


def by_channels(
    tokens,
    offsets,
    norm_gain,
    norm_bias,
    proj_weight,
    proj_bias,
    short_filter,
    short_bias,
    long_kernel,
    skip_bias,
    out_weight,
    out_bias,
    second_gain,
    second_bias,
    up_weight,
    up_bias,
    down_weight,
    down_bias,
    cotangent,
):
    seq_count, tok_count, features = tokens.shape
    parts = lax.axis_size("seq")
    chans = features // parts
    length = parts * tok_count
    tables = fourier_tables(parts, tok_count)
    spectral = (seq_count, chans, 2 * parts, tok_count)
    positions = lax.axis_index("seq") * tok_count + jnp.arange(tok_count, dtype=jnp.int32)
    live = (positions[None, :] >= offsets[:, None]).astype(jnp.float32)[:, :, None]
    hidden = tokens.astype(jnp.float32)
    normed, norm_pull = jax.vjp(layer_norm, hidden, norm_gain, norm_bias)
    normed_low = normed.astype(jnp.bfloat16)
    mixed = (
        jnp.einsum("sti,ij->stj", normed_low, proj_weight, preferred_element_type=jnp.float32)
        + proj_bias
    )
    rim = passed_along(mixed[:, tok_count - 2 :, :], "seq", 1)
    extended = jnp.concatenate([rim, mixed], axis=1)
    filtered = (
        short_filter[:, 0] * extended[:, :tok_count]
        + short_filter[:, 1] * extended[:, 1 : tok_count + 1]
        + short_filter[:, 2] * extended[:, 2:]
        + short_bias
    )
    outer_gate = filtered[:, :, :features]
    inner_gate = filtered[:, :, features : 2 * features]
    values = filtered[:, :, 2 * features :]
    gated = values * inner_gate * live
    gated_chan, kernel_chan = (
        lax.all_to_all(jnp.swapaxes(gated, 1, 2), "seq", split_axis=1, concat_axis=2, tiled=True),
        lax.all_to_all(long_kernel[None], "seq", split_axis=1, concat_axis=2, tiled=True),
    )
    gated_real, gated_imag = forward_transform(
        gated_chan.reshape(seq_count * chans, parts, tok_count), tables
    )
    gated_real = gated_real.reshape(spectral)
    gated_imag = gated_imag.reshape(spectral)
    kernel_real, kernel_imag = forward_transform(
        kernel_chan.reshape(chans, parts, tok_count), tables
    )
    prod_real = gated_real * kernel_real - gated_imag * kernel_imag
    prod_imag = gated_real * kernel_imag + gated_imag * kernel_real
    conv_chan = inverse_transform(
        prod_real.reshape(-1, 2 * parts, tok_count),
        prod_imag.reshape(-1, 2 * parts, tok_count),
        tables,
    )
    conv_chan = conv_chan.reshape(seq_count, chans, length)
    conv_tokens = jnp.swapaxes(
        lax.all_to_all(conv_chan, "seq", split_axis=2, concat_axis=1, tiled=True), 1, 2
    )
    convolved = conv_tokens + gated * skip_bias
    branch = convolved * outer_gate
    branch_low = branch.astype(jnp.bfloat16)
    residual = (
        hidden
        + jnp.einsum("sti,ij->stj", branch_low, out_weight, preferred_element_type=jnp.float32)
        + out_bias
    )
    normed_two, second_pull = jax.vjp(layer_norm, residual, second_gain, second_bias)
    normed_two_low = normed_two.astype(jnp.bfloat16)
    expanded = (
        jnp.einsum("sti,ij->stj", normed_two_low, up_weight, preferred_element_type=jnp.float32)
        + up_bias
    )
    activated, gelu_pull = jax.vjp(jax.nn.gelu, expanded)
    activated_low = activated.astype(jnp.bfloat16)
    output = (
        residual
        + jnp.einsum("sti,ij->stj", activated_low, down_weight, preferred_element_type=jnp.float32)
        + down_bias
    )
    upstream = cotangent.astype(jnp.float32)
    down_grad = jnp.einsum(
        "sti,stj->ij", activated_low, cotangent, preferred_element_type=jnp.float32
    )
    down_bias_grad = jnp.sum(upstream, axis=(0, 1))
    act_grad = jnp.einsum("stj,ij->sti", cotangent, down_weight, preferred_element_type=jnp.float32)
    (expanded_grad,) = gelu_pull(act_grad)
    expanded_low = expanded_grad.astype(jnp.bfloat16)
    up_grad = jnp.einsum(
        "sti,stj->ij", normed_two_low, expanded_low, preferred_element_type=jnp.float32
    )
    up_bias_grad = jnp.sum(expanded_low.astype(jnp.float32), axis=(0, 1))
    normed_two_grad = jnp.einsum(
        "stj,ij->sti", expanded_low, up_weight, preferred_element_type=jnp.float32
    )
    residual_part, second_gain_grad, second_bias_grad = second_pull(normed_two_grad)
    residual_grad = upstream + residual_part
    residual_low = residual_grad.astype(jnp.bfloat16)
    out_grad = jnp.einsum(
        "sti,stj->ij", branch_low, residual_low, preferred_element_type=jnp.float32
    )
    out_bias_grad = jnp.sum(residual_low.astype(jnp.float32), axis=(0, 1))
    branch_grad = jnp.einsum(
        "stj,ij->sti", residual_low, out_weight, preferred_element_type=jnp.float32
    )
    conv_grad = branch_grad * outer_gate
    outer_grad = branch_grad * convolved
    skip_bias_grad = jnp.sum(conv_grad * gated, axis=(0, 1))
    conv_grad_chan = lax.all_to_all(
        jnp.swapaxes(conv_grad, 1, 2), "seq", split_axis=1, concat_axis=2, tiled=True
    )
    grad_real, grad_imag = forward_transform(
        conv_grad_chan.reshape(seq_count * chans, parts, tok_count), tables
    )
    grad_real = grad_real.reshape(spectral)
    grad_imag = grad_imag.reshape(spectral)
    back_real = kernel_real * grad_real + kernel_imag * grad_imag
    back_imag = kernel_real * grad_imag - kernel_imag * grad_real
    gated_back_chan = inverse_transform(
        back_real.reshape(-1, 2 * parts, tok_count),
        back_imag.reshape(-1, 2 * parts, tok_count),
        tables,
    )
    gated_back_chan = gated_back_chan.reshape(seq_count, chans, length)
    tap_real = jnp.sum(gated_real * grad_real + gated_imag * grad_imag, axis=0)
    tap_imag = jnp.sum(gated_real * grad_imag - gated_imag * grad_real, axis=0)
    kernel_grad = inverse_transform(tap_real, tap_imag, tables).reshape(chans, length)
    gated_back = jnp.swapaxes(
        lax.all_to_all(gated_back_chan, "seq", split_axis=2, concat_axis=1, tiled=True), 1, 2
    )
    gated_grad = (gated_back + conv_grad * skip_bias) * live
    value_grad = gated_grad * inner_gate
    inner_grad = gated_grad * values
    filtered_grad = jnp.concatenate([outer_grad, inner_grad, value_grad], axis=2)
    following = passed_along(filtered_grad[:, :2, :], "seq", -1)
    grad_extended = jnp.concatenate([filtered_grad, following], axis=1)
    mixed_grad = (
        short_filter[:, 2] * grad_extended[:, :tok_count]
        + short_filter[:, 1] * grad_extended[:, 1 : tok_count + 1]
        + short_filter[:, 0] * grad_extended[:, 2:]
    )
    filter_grad = jnp.stack(
        [
            jnp.sum(filtered_grad * extended[:, position : position + tok_count], axis=(0, 1))
            for position in range(3)
        ],
        axis=1,
    )
    short_bias_grad = jnp.sum(filtered_grad, axis=(0, 1))
    mixed_low = mixed_grad.astype(jnp.bfloat16)
    proj_grad = jnp.einsum("sti,stj->ij", normed_low, mixed_low, preferred_element_type=jnp.float32)
    proj_bias_grad = jnp.sum(mixed_low.astype(jnp.float32), axis=(0, 1))
    normed_grad = jnp.einsum(
        "stj,ij->sti", mixed_low, proj_weight, preferred_element_type=jnp.float32
    )
    hidden_part, norm_gain_grad, norm_bias_grad = norm_pull(normed_grad)
    input_grad = residual_grad + hidden_part
    (
        norm_gain_share,
        norm_bias_share,
        proj_share,
        proj_bias_share,
        filter_share,
        short_bias_share,
        skip_share,
        out_share,
        out_bias_share,
        second_gain_share,
        second_bias_share,
        up_share,
        up_bias_share,
        down_share,
        down_bias_share,
    ) = (
        lax.psum_scatter(norm_gain_grad, "seq", scatter_dimension=0, tiled=True),
        lax.psum_scatter(norm_bias_grad, "seq", scatter_dimension=0, tiled=True),
        lax.psum_scatter(proj_grad, "seq", scatter_dimension=0, tiled=True),
        lax.psum_scatter(proj_bias_grad, "seq", scatter_dimension=0, tiled=True),
        lax.psum_scatter(filter_grad, "seq", scatter_dimension=0, tiled=True),
        lax.psum_scatter(short_bias_grad, "seq", scatter_dimension=0, tiled=True),
        lax.psum_scatter(skip_bias_grad, "seq", scatter_dimension=0, tiled=True),
        lax.psum_scatter(out_grad, "seq", scatter_dimension=0, tiled=True),
        lax.psum_scatter(out_bias_grad, "seq", scatter_dimension=0, tiled=True),
        lax.psum_scatter(second_gain_grad, "seq", scatter_dimension=0, tiled=True),
        lax.psum_scatter(second_bias_grad, "seq", scatter_dimension=0, tiled=True),
        lax.psum_scatter(up_grad, "seq", scatter_dimension=0, tiled=True),
        lax.psum_scatter(up_bias_grad, "seq", scatter_dimension=0, tiled=True),
        lax.psum_scatter(down_grad, "seq", scatter_dimension=0, tiled=True),
        lax.psum_scatter(down_bias_grad, "seq", scatter_dimension=0, tiled=True),
    )
    (
        norm_gain_grad,
        norm_bias_grad,
        proj_grad,
        proj_bias_grad,
        filter_grad,
        short_bias_grad,
        skip_bias_grad,
        out_grad,
        out_bias_grad,
        second_gain_grad,
        second_bias_grad,
        up_grad,
        up_bias_grad,
        down_grad,
        down_bias_grad,
        kernel_grad,
    ) = lax.psum(
        (
            norm_gain_share,
            norm_bias_share,
            proj_share,
            proj_bias_share,
            filter_share,
            short_bias_share,
            skip_share,
            out_share,
            out_bias_share,
            second_gain_share,
            second_bias_share,
            up_share,
            up_bias_share,
            down_share,
            down_bias_share,
            kernel_grad,
        ),
        "dp",
    )
    return (
        output,
        input_grad,
        norm_gain_grad,
        norm_bias_grad,
        proj_grad,
        proj_bias_grad,
        filter_grad,
        short_bias_grad,
        kernel_grad,
        skip_bias_grad,
        out_grad,
        out_bias_grad,
        second_gain_grad,
        second_bias_grad,
        up_grad,
        up_bias_grad,
        down_grad,
        down_bias_grad,
    )


def block_tables(width):
    def stacked(matrix):
        high = matrix.astype(np.float32).astype(ml_dtypes.bfloat16)
        low = (matrix - high.astype(np.float64)).astype(ml_dtypes.bfloat16)
        return np.concatenate([high, high, low], axis=1)

    odd = 2 * np.arange(width) + 1
    angles = np.pi / (2 * width) * (odd[:, None] * np.arange(width)[None, :] % (4 * width))
    analysis = np.concatenate([np.cos(angles), -np.sin(angles)], axis=0)
    angles = np.pi / (2 * width) * (np.arange(2 * width)[:, None] * odd[None, :] % (4 * width))
    synthesis = np.concatenate([np.cos(angles), -np.sin(angles)], axis=1) / width
    return stacked(analysis), stacked(synthesis)


def in_parts(values):
    high = values.astype(jnp.bfloat16)
    low = (values - high.astype(jnp.float32)).astype(jnp.bfloat16)
    return high, low


def short_filtered(padded_ref, mixed_ref, taps):
    count, lanes = mixed_ref.shape
    padded_ref[:8] = jnp.zeros((8, lanes), jnp.float32)
    padded_ref[8 : 8 + count] = mixed_ref[...]
    return (
        taps[0:1] * padded_ref[6 : 6 + count]
        + taps[1:2] * padded_ref[7 : 7 + count]
        + taps[2:3] * mixed_ref[...]
        + taps[3:4]
    )


def analyse(signal, table_ref, spectra_ref):
    blocks, double, lanes = spectra_ref.shape
    width = double // 2
    high, low = in_parts(signal)
    for first in range(0, blocks, 2):
        columns = []
        for block in (first, first + 1):
            rows = slice(block * width, (block + 1) * width)
            columns.append(jnp.concatenate([high[rows], low[rows], high[rows]], axis=0))
        found = jnp.dot(
            table_ref[...], jnp.concatenate(columns, axis=1), preferred_element_type=jnp.float32
        )
        spectra_ref[first] = found[:, :lanes]
        spectra_ref[first + 1] = found[:, lanes:]


def analyse_kernel(kernel_ref, table_ref, spectra_ref):
    blocks, double, lanes = spectra_ref.shape
    for first in range(0, blocks, 2):
        rows = []
        for block in (first, first + 1):
            high, low = in_parts(kernel_ref[block])
            rows.append(jnp.concatenate([high, low, high], axis=1))
        found = lax.dot_general(
            table_ref[...],
            jnp.concatenate(rows, axis=0),
            (((1,), (1,)), ((), ())),
            preferred_element_type=jnp.float32,
        )
        spectra_ref[first] = found[:, :lanes]
        spectra_ref[first + 1] = found[:, lanes:]


def synthesise(spectra_ref, table_ref):
    blocks, double, lanes = spectra_ref.shape
    found = []
    for first in range(0, blocks, 2):
        columns = []
        for block in (first, first + 1):
            high, low = in_parts(spectra_ref[block])
            columns.append(jnp.concatenate([high, low, high], axis=0))
        pair = jnp.dot(
            table_ref[...], jnp.concatenate(columns, axis=1), preferred_element_type=jnp.float32
        )
        found.append(pair[:, :lanes])
        found.append(pair[:, lanes:])
    return found


def multiply(left_ref, right_ref, out_ref, reverse):
    blocks, double, lanes = out_ref.shape
    width = double // 2

    def step(index, carry):
        real_rows = pl.ds(pl.multiple_of(index * 8, 8), 8)
        imag_rows = pl.ds(pl.multiple_of(width + index * 8, 8), 8)
        left_real = [left_ref[block, real_rows] for block in range(blocks)]
        left_imag = [left_ref[block, imag_rows] for block in range(blocks)]
        right_real = [right_ref[block, real_rows] for block in range(blocks)]
        right_imag = [right_ref[block, imag_rows] for block in range(blocks)]
        left_sum = [
            real - imag if reverse else real + imag for real, imag in zip(left_real, left_imag)
        ]
        right_sum = [real + imag for real, imag in zip(right_real, right_imag)]
        right_gap = [imag - real for real, imag in zip(right_real, right_imag)]
        for m in range(blocks):
            one = two = three = 0.0
            for l in range(blocks - m if reverse else m + 1):
                r = m + l if reverse else m - l
                one = one + right_real[r] * left_sum[l]
                two = two + left_real[l] * right_gap[r]
                three = three + left_imag[l] * right_sum[r]
            out_ref[m, real_rows] = one + three if reverse else one - three
            out_ref[m, imag_rows] = one + two
        return carry

    lax.fori_loop(0, width // 8, step, 0, unroll=2)


def gates(start_ref, mixed_refs, taps_ref, padded_ref):
    outer, inner, values = [
        short_filtered(padded_ref.at[group], ref, taps_ref[group])
        for group, ref in enumerate(mixed_refs)
    ]
    rows = lax.broadcasted_iota(jnp.int32, outer.shape, 0)
    live = (rows >= start_ref[0]).astype(jnp.float32)
    return outer, inner, values, live


def forward_kernel(
    start_ref,
    outer_ref,
    inner_ref,
    value_ref,
    kernel_ref,
    taps_ref,
    skip_ref,
    analysis_ref,
    synthesis_ref,
    convolved_ref,
    branch_ref,
    signal_spectra,
    kernel_spectra,
    spectra,
    padded,
):
    width = kernel_ref.shape[2]
    outer, inner, values, live = gates(start_ref, (outer_ref, inner_ref, value_ref), taps_ref, padded)
    gated = values * inner * live
    analyse(gated, analysis_ref, signal_spectra)
    analyse_kernel(kernel_ref, analysis_ref, kernel_spectra)
    multiply(kernel_spectra, signal_spectra, spectra, False)
    found = synthesise(spectra, synthesis_ref)
    pieces = [found[0][:width]]
    for block in range(1, len(found)):
        pieces.append(found[block][:width] + found[block - 1][width:])
    convolved = jnp.concatenate(pieces, axis=0) + gated * skip_ref[...]
    convolved_ref[...] = convolved
    branch_ref[...] = (convolved * outer).astype(jnp.bfloat16)


def lag_blocks(found, width):
    pieces = []
    for block in range(len(found)):
        piece = found[block][:width]
        if block + 1 < len(found):
            piece = piece - found[block + 1][width:]
        pieces.append(piece)
    return pieces


def backward_kernel(
    start_ref,
    grad_ref,
    convolved_ref,
    outer_ref,
    inner_ref,
    value_ref,
    kernel_ref,
    taps_ref,
    skip_ref,
    analysis_ref,
    synthesis_ref,
    mixed_grad_ref,
    kernel_kept_ref,
    kernel_given_ref,
    sums_ref,
    signal_spectra,
    kernel_spectra,
    grad_spectra,
    spectra,
    padded,
):
    width = kernel_ref.shape[2]
    mixed_refs = (outer_ref, inner_ref, value_ref)
    outer, inner, values, live = gates(start_ref, mixed_refs, taps_ref, padded)
    gated = values * inner * live
    branch_grad = grad_ref[...]
    conv_grad = branch_grad * outer
    outer_grad = branch_grad * convolved_ref[...]
    analyse(gated, analysis_ref, signal_spectra)
    analyse_kernel(kernel_ref, analysis_ref, kernel_spectra)
    analyse(conv_grad, analysis_ref, grad_spectra)
    multiply(signal_spectra, grad_spectra, spectra, True)
    lags = lag_blocks(synthesise(spectra, synthesis_ref), width)
    half = len(lags) // 2
    first = start_ref[1] == 0
    for block in range(half):
        columns = slice(block * width, (block + 1) * width)
        one, two = lags[block].T, lags[half + block].T
        kernel_kept_ref[:, columns] = jnp.where(first, one, two)
        kernel_given_ref[:, columns] = jnp.where(first, two, one)
    multiply(kernel_spectra, grad_spectra, spectra, True)
    back = jnp.concatenate(lag_blocks(synthesise(spectra, synthesis_ref), width), axis=0)
    gated_grad = (back + conv_grad * skip_ref[...]) * live

    def total(array):
        return jnp.sum(array, axis=0, keepdims=True)

    count = outer.shape[0]
    filter_rows, bias_rows, low_rows = [], [], []
    grads = (outer_grad, gated_grad * values, gated_grad * inner)
    for group in range(3):
        grad, mixed, taps = grads[group], mixed_refs[group][...], taps_ref[group]
        padded[group, :count] = grad
        padded[group, count : count + 8] = jnp.zeros((8, grad.shape[1]), jnp.float32)
        next_one, next_two = padded[group, 1 : 1 + count], padded[group, 2 : 2 + count]
        mixed_grad = taps[2:3] * grad + taps[1:2] * next_one + taps[0:1] * next_two
        low = mixed_grad.astype(jnp.bfloat16)
        mixed_grad_ref[group] = low
        filter_rows.append([total(next_two * mixed), total(next_one * mixed), total(grad * mixed)])
        bias_rows.append(total(grad))
        low_rows.append(total(low.astype(jnp.float32)))
    rows = [filter_rows[group][tap] for tap in range(3) for group in range(3)]
    rows = rows + bias_rows + low_rows + [total(conv_grad * gated)]
    sums_ref[...] = jnp.concatenate(rows, axis=0)


def kernel_parameters(mebibytes=56):
    return pltpu.CompilerParams(vmem_limit_bytes=mebibytes * 1024 * 1024)


def kernel_specs(tokens, parts, width, lanes, features):
    groups = features // lanes

    def mixed(group):
        return pl.BlockSpec((tokens, lanes), lambda tile, *_: (0, group * groups + tile))

    return (
        [pl.BlockSpec(memory_space=pltpu.SMEM)],
        [mixed(0), mixed(1), mixed(2)],
        [
            pl.BlockSpec((parts, lanes, width), lambda tile, *_: (0, tile, 0)),
            pl.BlockSpec((3, 4, lanes), lambda tile, *_: (0, 0, tile)),
            pl.BlockSpec((1, lanes), lambda tile, *_: (0, tile)),
            pl.BlockSpec((2 * width, 3 * width), lambda *_: (0, 0)),
            pl.BlockSpec((2 * width, 6 * width), lambda *_: (0, 0)),
        ],
        pl.BlockSpec((tokens, lanes), lambda tile, *_: (0, tile)),
        pltpu.VMEM((parts, 2 * width, lanes), jnp.float32),
    )


def forward_convolution(start, mixed, kernel, taps, skip, tables, lanes=128):
    parts, features, width = kernel.shape
    tokens = mixed.shape[0]
    start_spec, mixed_specs, rest, plain, spectra = kernel_specs(tokens, parts, width, lanes, features)
    return pl.pallas_call(
        forward_kernel,
        grid=(features // lanes,),
        in_specs=start_spec + mixed_specs + rest,
        out_specs=(plain, plain),
        out_shape=(
            jax.ShapeDtypeStruct((tokens, features), jnp.float32),
            jax.ShapeDtypeStruct((tokens, features), jnp.bfloat16),
        ),
        scratch_shapes=[spectra] * 3 + [pltpu.VMEM((3, tokens + 8, lanes), jnp.float32)],
        compiler_params=kernel_parameters(),
        cost_estimate=NO_COST,
        name="forward_convolution",
    )(start, mixed, mixed, mixed, kernel, taps, skip, *tables)


def backward_convolution(start, grad, convolved, mixed, kernel, taps, skip, tables, lanes=128):
    parts, features, width = kernel.shape
    tokens = mixed.shape[0]
    start_spec, mixed_specs, rest, plain, spectra = kernel_specs(tokens, parts, width, lanes, features)
    return pl.pallas_call(
        backward_kernel,
        grid=(features // lanes,),
        in_specs=start_spec + [plain, plain] + mixed_specs + rest,
        out_specs=(
            pl.BlockSpec((3, tokens, lanes), lambda tile: (0, 0, tile)),
            pl.BlockSpec((lanes, tokens // 2), lambda tile: (tile, 0)),
            pl.BlockSpec((lanes, tokens // 2), lambda tile: (tile, 0)),
            pl.BlockSpec((16, lanes), lambda tile: (0, tile)),
        ),
        out_shape=(
            jax.ShapeDtypeStruct((3, tokens, features), jnp.bfloat16),
            jax.ShapeDtypeStruct((features, tokens // 2), jnp.float32),
            jax.ShapeDtypeStruct((features, tokens // 2), jnp.float32),
            jax.ShapeDtypeStruct((16, features), jnp.float32),
        ),
        scratch_shapes=[spectra] * 4 + [pltpu.VMEM((3, tokens + 8, lanes), jnp.float32)],
        compiler_params=kernel_parameters(),
        cost_estimate=NO_COST,
        name="backward_convolution",
    )(start, grad, convolved, mixed, mixed, mixed, kernel, taps, skip, *tables)


def unit_rows(values):
    centered = values - jnp.mean(values, axis=-1, keepdims=True)
    spread = lax.rsqrt(jnp.mean(centered * centered, axis=-1, keepdims=True) + EPSILON)
    return centered * spread, spread


def unit_rows_back(grad, unit, spread, gain):
    scaled = grad * gain
    inner = scaled - jnp.mean(scaled, axis=-1, keepdims=True)
    return (inner - unit * jnp.mean(scaled * unit, axis=-1, keepdims=True)) * spread


def matmul(left, right):
    return jnp.dot(left, right, preferred_element_type=jnp.float32)


def matmul_back(left, right):
    return lax.dot_general(left, right, (((1,), (1,)), ((), ())), preferred_element_type=jnp.float32)


def columns_of(array, refs):
    first = 0
    for ref in refs:
        ref[...] = array[:, first : first + ref.shape[1]]
        first += ref.shape[1]


def column_sums(array):
    return jnp.sum(array, axis=0, keepdims=True)


def project_kernel(x_ref, gain_ref, bias_ref, weight_ref, offset_ref, normed_ref, mixed_ref):
    unit, _ = unit_rows(x_ref[...])
    normed = (unit * gain_ref[...] + bias_ref[...]).astype(jnp.bfloat16)
    normed_ref[...] = normed
    mixed_ref[...] = matmul(normed, weight_ref[...]) + offset_ref[...]


def feed_kernel(
    x_ref,
    branch_ref,
    out_weight_ref,
    out_bias_ref,
    gain_ref,
    bias_ref,
    up_weight_ref,
    up_bias_ref,
    down_weight_ref,
    down_bias_ref,
    residual_ref,
    normed_ref,
    activated_ref,
    slope_ref,
    *output_refs,
):
    residual = x_ref[...] + matmul(branch_ref[...], out_weight_ref[...]) + out_bias_ref[...]
    residual_ref[...] = residual
    unit, _ = unit_rows(residual)
    normed = (unit * gain_ref[...] + bias_ref[...]).astype(jnp.bfloat16)
    normed_ref[...] = normed
    total = residual + down_bias_ref[...]
    factor = math.sqrt(2.0 / math.pi)
    chunk = residual.shape[1]
    for first in range(0, up_weight_ref.shape[1], chunk):
        columns = slice(first, first + chunk)
        expanded = matmul(normed, up_weight_ref[:, columns]) + up_bias_ref[:, columns]
        square = expanded * expanded
        turned = jnp.tanh(factor * (expanded + 0.044715 * (square * expanded)))
        half = 0.5 + 0.5 * turned
        activated = (expanded * half).astype(jnp.bfloat16)
        activated_ref[:, columns] = activated
        slope_ref[:, columns] = half + (0.5 * factor) * expanded * (1.0 - turned * turned) * (
            1.0 + (3 * 0.044715) * square
        )
        total = total + matmul(activated, down_weight_ref[columns, :])
    columns_of(total, output_refs)


def feed_back_kernel(
    grad_ref,
    residual_ref,
    slope_ref,
    gain_ref,
    out_weight_ref,
    up_weight_ref,
    down_weight_ref,
    expanded_ref,
    residual_grad_ref,
    residual_low_ref,
    branch_grad_ref,
    sums_ref,
    wide_sums_ref,
):
    grad = grad_ref[...]
    grad_low = grad.astype(jnp.bfloat16)
    chunk = grad.shape[1]
    normed_grad = None
    wide = []
    for first in range(0, up_weight_ref.shape[1], chunk):
        columns = slice(first, first + chunk)
        expanded = matmul_back(grad_low, down_weight_ref[columns, :]) * slope_ref[:, columns]
        low = expanded.astype(jnp.bfloat16)
        expanded_ref[:, columns] = low
        wide.append(column_sums(low.astype(jnp.float32)))
        part = matmul_back(low, up_weight_ref[:, columns])
        normed_grad = part if normed_grad is None else normed_grad + part
    unit, spread = unit_rows(residual_ref[...])
    residual_grad = grad + unit_rows_back(normed_grad, unit, spread, gain_ref[...])
    residual_grad_ref[...] = residual_grad
    low = residual_grad.astype(jnp.bfloat16)
    residual_low_ref[...] = low
    branch_grad_ref[...] = matmul_back(low, out_weight_ref[...])
    sums = [
        column_sums(normed_grad * unit),
        column_sums(normed_grad),
        column_sums(low.astype(jnp.float32)),
        column_sums(grad),
    ]

    @pl.when(pl.program_id(0) == 0)
    def _():
        sums_ref[...] = jnp.zeros_like(sums_ref)
        wide_sums_ref[...] = jnp.zeros_like(wide_sums_ref)

    sums_ref[...] += jnp.concatenate(sums, axis=0)
    wide_sums_ref[...] += jnp.concatenate(wide, axis=1)


def input_grad_kernel(
    mixed_ref, weight_ref, x_ref, gain_ref, residual_grad_ref, first_ref, second_ref, sums_ref
):
    features = x_ref.shape[1]
    normed_grad = None
    for group in range(3):
        columns = slice(group * features, (group + 1) * features)
        part = matmul_back(mixed_ref[group], weight_ref[:, columns])
        normed_grad = part if normed_grad is None else normed_grad + part
    unit, spread = unit_rows(x_ref[...])
    total = residual_grad_ref[...] + unit_rows_back(normed_grad, unit, spread, gain_ref[...])
    columns_of(total, (first_ref, second_ref))
    sums = jnp.concatenate([column_sums(normed_grad * unit), column_sums(normed_grad)], axis=0)

    @pl.when(pl.program_id(0) == 0)
    def _():
        sums_ref[...] = jnp.zeros_like(sums_ref)

    sums_ref[...] += sums


def by_rows(kernel, name, rows, inputs, outputs, height=256):
    def spec(shape, held):
        if len(shape) == 3:
            return pl.BlockSpec((shape[0], height, shape[2]), lambda step: (0, step, 0))
        if shape[0] == rows and not held:
            return pl.BlockSpec((height, shape[1]), lambda step: (step, 0))
        return pl.BlockSpec(shape, lambda step: (0, 0))

    return pl.pallas_call(
        kernel,
        grid=(rows // height,),
        in_specs=[spec(array.shape, held) for array, held in inputs],
        out_specs=tuple(spec(shape, False) for shape, _ in outputs),
        out_shape=tuple(jax.ShapeDtypeStruct(shape, kind) for shape, kind in outputs),
        compiler_params=kernel_parameters(),
        cost_estimate=NO_COST,
        name=name,
    )(*[array for array, _ in inputs])


def product_kernel(half_ref, left_ref, right_ref, out_ref):
    out_ref[...] = product_tile(left_ref, right_ref)


def product_tile(left_ref, right_ref):
    if len(right_ref.shape) == 2:
        return product(left_ref[...], right_ref[...].astype(jnp.bfloat16))
    return jnp.concatenate(
        [product(left_ref[...], right_ref[group]) for group in range(right_ref.shape[0])], axis=1
    )


def product_specs(left, right, tile):
    tokens = left.shape[0]
    half = right.shape[-1] // 2
    left_spec = pl.BlockSpec((tokens, tile), lambda step, half_ref: (0, step))
    if right.ndim == 2:
        right_spec = pl.BlockSpec((tokens, half), lambda step, half_ref: (0, half_ref[0]))
        return half, left_spec, right_spec
    right_spec = pl.BlockSpec((right.shape[0], tokens, half), lambda step, half_ref: (0, 0, half_ref[0]))
    return half * right.shape[0], left_spec, right_spec


def half_product(left, right, half, tile=384):
    rows = left.shape[1]
    columns, left_spec, right_spec = product_specs(left, right, tile)
    return pl.pallas_call(
        product_kernel,
        grid_spec=pltpu.PrefetchScalarGridSpec(
            num_scalar_prefetch=1,
            grid=(rows // tile,),
            in_specs=[left_spec, right_spec],
            out_specs=pl.BlockSpec((tile, columns), lambda step, half_ref: (step, 0)),
        ),
        out_shape=jax.ShapeDtypeStruct((rows, columns), jnp.float32),
        compiler_params=kernel_parameters(24),
        cost_estimate=NO_COST,
        name="half_product",
    )(half, left, right)


def whole_product_kernel(left_ref, right_ref, out_ref):
    out_ref[...] = product(left_ref[...], right_ref[...])


def whole_product(left, right):
    tokens, rows = left.shape
    return pl.pallas_call(
        whole_product_kernel,
        grid=(right.shape[1] // rows,),
        in_specs=[
            pl.BlockSpec((tokens, rows), lambda step: (0, 0)),
            pl.BlockSpec((tokens, rows), lambda step: (0, step)),
        ],
        out_specs=pl.BlockSpec((rows, rows), lambda step: (0, step)),
        out_shape=jax.ShapeDtypeStruct((rows, right.shape[1]), jnp.float32),
        compiler_params=kernel_parameters(),
        cost_estimate=NO_COST,
        name="whole_product",
    )(left, right)


def parted_product_kernel(bits_ref, left_ref, right_ref, taken_ref, *out_refs):
    total = product_tile(left_ref, right_ref) + taken_ref[...]
    left = 0
    for part in range(len(out_refs) // 2):
        kept_ref, given_ref = out_refs[2 * part : 2 * part + 2]
        pieces, rows, columns = kept_ref.shape
        first = bits_ref[1 + part] == 0
        for piece in range(pieces):
            one = total[2 * piece * rows : (2 * piece + 1) * rows, left : left + columns]
            two = total[(2 * piece + 1) * rows : (2 * piece + 2) * rows, left : left + columns]
            kept_ref[piece] = jnp.where(first, one, two)
            given_ref[piece] = jnp.where(first, two, one)
        left += columns


def parted_product(left, right, half, taken, plan, tile=384):
    rows = left.shape[1]
    columns, left_spec, right_spec = product_specs(left, right, tile)
    steps = rows // tile
    specs, shapes = [], []
    for _, pieces in plan:
        shape = (pieces, rows // (2 * pieces), columns // len(plan))
        block = (pieces // steps,) + shape[1:]
        specs += [pl.BlockSpec(block, lambda step, bits_ref: (step, 0, 0))] * 2
        shapes += [jax.ShapeDtypeStruct(shape, jnp.float32)] * 2
    return pl.pallas_call(
        parted_product_kernel,
        grid_spec=pltpu.PrefetchScalarGridSpec(
            num_scalar_prefetch=1,
            grid=(steps,),
            in_specs=[
                left_spec,
                right_spec,
                pl.BlockSpec((tile, columns), lambda step, bits_ref: (step, 0)),
            ],
            out_specs=tuple(specs),
        ),
        out_shape=tuple(shapes),
        compiler_params=kernel_parameters(24),
        cost_estimate=NO_COST,
        name="parted_product",
    )(jnp.concatenate([half] + [which for which, _ in plan]), left, right, taken)


def fold_kernel(bit_ref, *refs):
    *sources, kept_ref, given_ref = refs
    first = bit_ref[0] == 0
    height, lane = kept_ref.shape[1], 0
    for kept, taken in zip(sources[::2], sources[1::2]):
        total = kept[...] + taken[...]
        for row in range(0, total.shape[1], height):
            columns = slice(lane, lane + total.shape[2])
            one, two = total[0, row : row + height], total[1, row : row + height]
            kept_ref[0, :, columns] = jnp.where(first, one, two)
            given_ref[0, :, columns] = jnp.where(first, two, one)
            lane += total.shape[2]


def fold(pairs, which, height):
    count = pairs[0][0].shape[0]
    operands, specs, columns = [], [], 0
    for kept, taken, *share in pairs:
        place, shares = share if share else (0, 1)
        block = (2, kept.shape[1], kept.shape[2] // shares)
        operands += [kept, taken]
        specs += [pl.BlockSpec(block, lambda step, place=place: (step, 0, place))] * 2
        columns += block[1] // height * block[2]
    one = pl.BlockSpec((1, height, columns), lambda step: (step, 0, 0))
    shape = jax.ShapeDtypeStruct((count // 2, height, columns), jnp.float32)
    return pl.pallas_call(
        fold_kernel,
        grid=(count // 2,),
        in_specs=[pl.BlockSpec(memory_space=pltpu.SMEM)] + specs,
        out_specs=(one, one),
        out_shape=(shape, shape),
        compiler_params=kernel_parameters(24),
        cost_estimate=NO_COST,
        name="fold",
    )(which, *operands)


def unpack_kernel(bits_ref, own_ref, y_ref, core_ref, both_ref, *out_refs):
    core_first, y_first = bits_ref[0] == 0, bits_ref[1] == 0
    own, beside = own_ref[...], y_ref[...]
    mine = [jnp.where(y_first, own, beside), jnp.where(y_first, beside, own)]
    own, beside = core_ref[...], both_ref[...]
    theirs = [jnp.where(y_first, own, beside), jnp.where(y_first, beside, own)]
    height = own.shape[0]
    for y in range(2):
        for core in range(2):
            block = jnp.where(core_first, mine[y], theirs[y])
            if core == 1:
                block = jnp.where(core_first, theirs[y], mine[y])
            lane = 0
            for ref in out_refs:
                rows, columns = ref.shape
                if columns == 128:
                    ref[(2 * core + y) * height : (2 * core + y + 1) * height] = block[:, lane:]
                    continue
                groups = 3 if columns == 3 * height * 16 and rows == 2 * height else 1
                half = columns // (2 * groups)
                for place in range(rows // (2 * height)):
                    for group in range(groups):
                        top = y * (rows // 2) + place * height
                        left = group * 2 * half + core * half
                        ref[top : top + height, left : left + half] = block[:, lane : lane + half]
                        lane += half


def gathered(share):
    y_other, core_other = swapped(share, "dp", 2), swapped(share, "dp", 1)
    return share, y_other, core_other, swapped(y_other, "dp", 1)


def unpacked(shares, shapes):
    return pl.pallas_call(
        unpack_kernel,
        in_specs=[pl.BlockSpec(memory_space=pltpu.SMEM)] + [pl.BlockSpec(memory_space=pltpu.VMEM)] * 4,
        out_specs=[pl.BlockSpec(memory_space=pltpu.VMEM)] * len(shapes),
        out_shape=[jax.ShapeDtypeStruct(shape, jnp.float32) for shape in shapes],
        compiler_params=kernel_parameters(24),
        cost_estimate=NO_COST,
        name="unpack",
    )(jnp.concatenate([flag("dp", 1), flag("dp", 2)]), *shares)


def swapped(array, axis, by):
    count = lax.axis_size(axis)
    return lax.ppermute(array, axis, [(i, i ^ by) for i in range(count)])


def bit(axis, by):
    return (lax.axis_index(axis) // by) % 2


def doubled(array, dim, axis, by):
    other = swapped(array, axis, by)
    first = bit(axis, by) == 0
    return jnp.concatenate(
        [jnp.where(first, array, other), jnp.where(first, other, array)], axis=dim
    )


def product(left, columns):
    return lax.dot_general(left, columns, (((0,), (0,)), ((), ())), preferred_element_type=jnp.float32)


def flag(axis, by):
    return bit(axis, by).astype(jnp.int32).reshape(1)


def reduced(kept, given, steps):
    for (axis, by), following in zip(steps, steps[1:] + [None]):
        taken = swapped(given, axis, by)
        if following is None:
            return (kept + taken)[0]
        kept, given = fold([(kept, taken)], flag(*following), kept.shape[1])


def by_sequences(
    tokens,
    offsets,
    norm_gain,
    norm_bias,
    proj_weight,
    proj_bias,
    short_filter,
    short_bias,
    long_kernel,
    skip_bias,
    out_weight,
    out_bias,
    second_gain,
    second_bias,
    up_weight,
    up_bias,
    down_weight,
    down_bias,
    cotangent,
):
    parts, width, features = tokens.shape
    length = parts * width
    hidden_units = up_weight.shape[1]
    hold = lax.optimization_barrier
    tables = tuple(jnp.asarray(table) for table in block_tables(width))
    start = lax.dynamic_slice_in_dim(offsets, lax.axis_index("seq"), 1, 0)
    core, other_core = flag("dp", 1), 1 - flag("dp", 1)
    scalars = jnp.concatenate([start, core])
    low, single = jnp.bfloat16, jnp.float32
    y_step, x_step = ("dp", 2), ("seq", 1)
    z_steps = [("seq", 1 << place) for place in range(1, parts.bit_length() - 1)]

    share = features // 4
    chunk = bit("dp", 1) * 2 + bit("dp", 2)
    piece = lax.dynamic_slice_in_dim(long_kernel, chunk * share, share, 0)
    pieces = jnp.stack([piece] + [swapped(piece, "seq", by) for by in range(2, parts, 2)])
    z = lax.axis_index("seq") // 2
    pieces = jnp.concatenate(
        [lax.dynamic_index_in_dim(pieces, z ^ other, 0) for other in range(parts // 2)]
    )
    hidden, pieces = hold((tokens.astype(single), pieces))
    hidden = lax.all_to_all(hidden, "seq", 0, 0, tiled=True)
    pieces = doubled(pieces[:, None], 1, *x_step).reshape(parts, share, width)
    kernel = doubled(doubled(pieces, 1, "dp", 2), 1, "dp", 1)
    upstream = cotangent.astype(single)
    taps = jnp.concatenate([short_filter.T, short_bias[None]], axis=0)
    taps = jnp.swapaxes(taps.reshape(4, 3, features), 0, 1)
    skip = skip_bias[None]
    hidden, kernel, upstream, taps, scalars = hold((hidden, kernel, upstream, taps, scalars))

    upstream = lax.all_to_all(upstream, "seq", 0, 0, tiled=True)
    hidden = hidden.reshape(length, features)
    normed_low, mixed = by_rows(
        project_kernel,
        "project",
        length,
        [
            (hidden, False),
            (norm_gain[None], True),
            (norm_bias[None], True),
            (proj_weight, True),
            (proj_bias[None], True),
        ],
        [((length, features), low), ((length, 3 * features), single)],
    )
    convolved, branch_low = forward_convolution(scalars, mixed, kernel, taps, skip, tables)
    residual, normed_two_low, activated_low, slope, *output = by_rows(
        feed_kernel,
        "feed",
        length,
        [
            (hidden, False),
            (branch_low, False),
            (out_weight, True),
            (out_bias[None], True),
            (second_gain[None], True),
            (second_bias[None], True),
            (up_weight, True),
            (up_bias[None], True),
            (down_weight, True),
            (down_bias[None], True),
        ],
        [
            ((length, features), single),
            ((length, features), low),
            ((length, hidden_units), low),
            ((length, hidden_units), single),
            ((length, features // 3), single),
            ((length, features * 2 // 3), single),
        ],
    )
    upstream, output = hold((upstream, output))

    def sent(columns):
        columns = columns.reshape(parts, width, -1)
        return lax.all_to_all(columns, "seq", 0, 0, tiled=True)

    output[0] = sent(output[0])
    upstream = upstream.reshape(length, features)
    down_given = half_product(activated_low, upstream, other_core, 768)
    upstream, down_given = hold((upstream, down_given))
    down_taken = swapped(down_given, "dp", 1)
    expanded_low, residual_grad, residual_low, branch_grad, sums_two, wide_sums = by_rows(
        feed_back_kernel,
        "feed_back",
        length,
        [
            (upstream, False),
            (residual, False),
            (slope, False),
            (second_gain[None], True),
            (out_weight, True),
            (up_weight, True),
            (down_weight, True),
        ],
        [
            ((length, hidden_units), low),
            ((length, features), single),
            ((length, features), low),
            ((length, features), single),
            ((4, features), single),
            ((1, hidden_units), single),
        ],
    )
    expanded_low, residual_low, branch_grad = hold((expanded_low, residual_low, branch_grad))
    side = whole_product(normed_two_low, expanded_low)
    side, down_taken, output = hold((side, down_taken, output))
    side = lax.psum_scatter(side, ("seq", "dp"), scatter_dimension=0, tiled=True)
    down_kept, down_given = parted_product(
        activated_low, upstream, core, down_taken, [(flag(*y_step), parts)], 768
    )
    branch_grad, down_given = hold((branch_grad, down_given))

    output[1] = sent(output[1])
    down_taken = swapped(down_given, *y_step)
    mixed_low, kernel_kept, kernel_given, sums = backward_convolution(
        scalars, branch_grad, convolved, mixed, kernel, taps, skip, tables
    )
    proj_given = half_product(normed_low, mixed_low, other_core)
    *input_grad, sums_one = by_rows(
        input_grad_kernel,
        "input_grad",
        length,
        [
            (mixed_low, False),
            (proj_weight, True),
            (hidden, False),
            (norm_gain[None], True),
            (residual_grad, False),
        ],
        [
            ((length, features * 2 // 3), single),
            ((length, features // 3), single),
            ((2, features), single),
        ],
    )
    input_grad, mixed_low, proj_given, kernel_given, down_taken, sums_one, sums, output = hold(
        (input_grad, mixed_low, proj_given, kernel_given, down_taken, sums_one, sums, output)
    )

    rows = features // (2 * parts)
    input_grad[0] = sent(input_grad[0])
    down_kept, down_given = fold([(down_kept, down_taken)], flag(*x_step), down_kept.shape[1])
    down_taken = swapped(down_given, *x_step)
    kernel_taken = swapped(kernel_given, "dp", 1)
    proj_taken = swapped(proj_given, "dp", 1)
    proj_kept, proj_given = parted_product(
        normed_low, mixed_low, core, proj_taken, [(flag(*y_step), parts)]
    )
    proj_given, residual_low = hold((proj_given, residual_low))
    proj_taken = swapped(proj_given, *y_step)
    out_given = half_product(branch_low, residual_low, other_core, 768)
    out_taken = swapped(out_given, "dp", 1)
    out_kept, out_given = parted_product(
        branch_low, residual_low, core, out_taken, [(flag(*y_step), parts)], 768
    )
    output = jnp.concatenate(output, axis=2)
    vectors = [sums_one[0], sums_one[1]]
    vectors += [sums[first : first + 3].reshape(-1) for first in range(0, 15, 3)]
    vectors += [sums[15], sums_two[2], sums_two[0], sums_two[1], wide_sums[0], sums_two[3]]
    sizes = [vector.shape[0] // parts for vector in vectors]
    packed = jnp.concatenate([vector.reshape(parts, -1) for vector in vectors], axis=1)
    packed = jnp.pad(packed, ((0, 0), (0, 4 * rows * 128 - packed.shape[1])))
    packed = packed.reshape(parts, 2, 2 * rows, 128)
    packed_kept = lax.dynamic_index_in_dim(packed, core[0], 1, keepdims=False)
    packed_given = lax.dynamic_index_in_dim(packed, other_core[0], 1, keepdims=False)
    packed_taken = swapped(packed_given, "dp", 1)
    kernel_kept, kernel_taken = [
        array.reshape(parts, 2 * rows, -1) for array in (kernel_kept, kernel_taken)
    ]
    kernel_kept, kernel_taken, packed_kept, packed_taken = [
        array.reshape(2 * parts, rows, -1)
        for array in (kernel_kept, kernel_taken, packed_kept, packed_taken)
    ]
    rest_kept, rest_given = fold(
        [(kernel_kept, kernel_taken), (packed_kept, packed_taken)], flag(*y_step), rows
    )
    input_grad, down_taken, proj_taken, rest_given, out_given, output = hold(
        (input_grad, down_taken, proj_taken, rest_given, out_given, output)
    )

    input_grad[1] = sent(input_grad[1])
    rest_taken = swapped(rest_given, *y_step)
    out_taken = swapped(out_given, *y_step)
    proj_kept, proj_given = fold([(proj_kept, proj_taken)], flag(*x_step), rows)
    proj_taken = swapped(proj_given, *x_step)
    feed_kept, feed_given = fold([(down_kept, down_taken)], flag(*z_steps[0]), rows)
    feed_taken = swapped(feed_given, *z_steps[0])
    input_grad, proj_taken, rest_taken, out_taken, feed_taken = hold(
        (input_grad, proj_taken, rest_taken, out_taken, feed_taken)
    )

    rest_kept, rest_given = fold(
        [(out_kept, out_taken), (rest_kept, rest_taken)], flag(*x_step), rows
    )
    rest_given, feed_taken = hold((rest_given, feed_taken))
    rest_taken = swapped(rest_given, *x_step)
    feed_kept, feed_given = fold([(feed_kept, feed_taken)], flag(*z_steps[1]), rows)
    feed_taken = swapped(feed_given, *z_steps[1])
    input_grad = jnp.concatenate(input_grad, axis=2)
    mixer_kept, mixer_given = fold(
        [(proj_kept, proj_taken), (rest_kept, rest_taken)], flag(*z_steps[0]), rows
    )
    feed_kept, mixer_given = hold((feed_kept, mixer_given))
    mixer_taken = swapped(mixer_given, *z_steps[0])
    feed_share = (feed_kept + feed_taken)[0]
    feed_shares = gathered(feed_share)
    mixer_taken, input_grad, *feed_shares = hold((mixer_taken, input_grad, *feed_shares))
    mixer_kept, mixer_given = fold([(mixer_kept, mixer_taken)], flag(*z_steps[1]), rows)
    mixer_taken = swapped(mixer_given, *z_steps[1])
    (down_share,) = unpacked(feed_shares, [(hidden_units // parts, features)])
    side = lax.all_gather(side, "dp", axis=0, tiled=True)
    mixer_taken, down_share, up_share = hold((mixer_taken, down_share, side))
    mixer_share = (mixer_kept + mixer_taken)[0]
    proj_share, out_share, kernel_share, packed = unpacked(
        gathered(mixer_share),
        [
            (features // parts, 3 * features),
            (features // parts, features),
            (features // parts, length),
            (4 * rows, 128),
        ],
    )
    packed = packed.reshape(-1)
    ends = np.cumsum(sizes)
    vectors = [packed[end - size : end] for size, end in zip(sizes, ends)]
    return (
        output,
        input_grad,
        vectors[0],
        vectors[1],
        proj_share,
        vectors[6],
        jnp.stack(vectors[2:5], axis=1),
        vectors[5],
        kernel_share,
        vectors[7],
        out_share,
        vectors[8],
        vectors[9],
        vectors[10],
        up_share,
        vectors[11],
        down_share,
        vectors[12],
    )


def per_device(tokens, offsets, *rest):
    fits = (
        tokens.shape[0] == lax.axis_size("seq")
        and lax.axis_size("dp") == 4
        and tokens.shape[0] % 2 == 0
        and tokens.shape[1] % 128 == 0
        and lax.axis_size("seq") & (lax.axis_size("seq") - 1) == 0
    )
    plan = by_sequences if fits else by_channels
    return plan(tokens, offsets, *rest)


def solution(mesh):
    return jax.shard_map(
        per_device,
        mesh=mesh,
        in_specs=(
            P("dp", "seq", None),
            P("dp"),
            P(),
            P(),
            P(),
            P(),
            P(),
            P(),
            P(None, "seq"),
            P(),
            P(),
            P(),
            P(),
            P(),
            P(),
            P(),
            P(),
            P(),
            P("dp", "seq", None),
        ),
        out_specs=(
            P("dp", "seq", None),
            P("dp", "seq", None),
            P("seq"),
            P("seq"),
            P("seq", None),
            P("seq"),
            P("seq", None),
            P("seq"),
            P("seq", None),
            P("seq"),
            P("seq", None),
            P("seq"),
            P("seq"),
            P("seq"),
            P("seq", None),
            P("seq"),
            P("seq", None),
            P("seq"),
        ),
        check_vma=False,
    )
```
